128 devices in a mesh: reg: 16 (over y_lo, x, core), ch: 8 (over z, y_hi).
Axes of the slice: x: 4, y: 4 (y_hi: 2, y_lo: 2; y = y_hi * 2 + y_lo), z: 4, core: 2. Of those that a mesh axis runs over, the one named last changes fastest.
Arguments:
- inner_state: float32 [2, 122880], P(None, 'reg'), may hold values from -6 to 6
- energy: float32 [122880], P('reg'), may hold values from -20 to 20
- blocks: float32 [1024, 512, 512], P(('reg', 'ch')), may hold values from -1.25 to 1.25
- pattern: int32 [1024, 2], P(('reg', 'ch')), may hold values from 0 to 239, as said below
- surface: float32 [416, 122880], P('ch', 'reg'), may hold values from -3 to 3
- channel_symmetry: int32 [416], P('ch'), may hold values from 0 to 59
- outer_state: float32 [2, 416, 8192], P(None, 'ch', 'reg'), may hold values from -6 to 6
- channel_energy: float32 [416], P('ch'), may hold values from -10 to 10
- couple_source: int32 [416, 4], replicated, may hold values from 0 to 415
- couple_order: int32 [416, 4], replicated, may hold values from 0 to 2
- couple_weight: float32 [416, 4], replicated, may hold values from -24 to 24
Outputs:
- new_inner: float32 [2, 122880], P(None, 'reg')
- new_outer: float32 [2, 416, 8192], P(None, 'ch', 'reg')
The draws below stay inside these ranges and needn't reach their ends.
Inputs may be any that keep to these rules, and one draw needn't show every extreme that they name: `pattern`: column 0 is a block row within the tile of the reg index that holds the row, below 15; column 1 is a global block column whose symmetry (block // 4) is one above or one below that of the block row.
All inputs are finite; a program needn't handle non-finite values.
Results may differ from the reference program's by a relative error of at most 0.0012.
Values may be sent and summed in bfloat16 or wider, within the bound.
No kernel may reach another device: no remote copies, remote signals or barrier semaphores. Data moves between devices by JAX's collectives and lax.ppermute only.
A program may use at most 64 MiB of HBM per device.

```python
import jax
import jax.numpy as jnp
from jax import lax

NSYM = 60
BLOCKS_PER_SYMM = 4
BLOCK_ROWS = 512
CHAN = 416
NLAM = 3
KCPL = 4
SYM_ROWS = 2048
ORDER = 122880
REGION_BLOCK_ROWS = 15
REGION_BLOCKS = 64
STORED_BLOCKS = 1024
RAD = 8192


def draw_pattern(key, part):
    key = jax.random.fold_in(key, 11)
    random_subkeys = jax.random.split(key, 3)
    stored_block_index = jnp.arange(STORED_BLOCKS, dtype=jnp.int32)
    region_index = stored_block_index // REGION_BLOCKS
    row_within_block = jax.random.randint(random_subkeys[0], (STORED_BLOCKS,), 0, REGION_BLOCK_ROWS, dtype=jnp.int32)
    symmetry = (region_index * REGION_BLOCK_ROWS + row_within_block) // BLOCKS_PER_SYMM
    upward_coupling = jax.random.randint(random_subkeys[1], (STORED_BLOCKS,), 0, 2, dtype=jnp.int32)
    target_block = symmetry + 2 * upward_coupling - 1
    target_block = jnp.where(target_block < 0, 1, jnp.where(target_block >= NSYM, NSYM - 2, target_block))
    column_index = target_block * BLOCKS_PER_SYMM + jax.random.randint(random_subkeys[2], (STORED_BLOCKS,), 0, BLOCKS_PER_SYMM, dtype=jnp.int32)
    return jnp.stack([row_within_block, column_index], axis=1)


def with_ends(result, own_key, smallest, high):
    longest = result.shape.index(max(result.shape))
    spots = []
    for shift in (0, 1):
        where = [jax.random.randint(jax.random.fold_in(own_key, axis), (), 0, length) for axis, length in enumerate(result.shape)]
        where[longest] = (where[longest] + shift) % result.shape[longest]
        spots.append(tuple(where))
    return result.at[spots[0]].set(smallest).at[spots[1]].set(high)


def block_levels(own_key, extent, cuts, low, high):
    factor_of = 1.0
    for dim, shards_of in cuts:
        steps = jax.random.uniform(jax.random.fold_in(jax.random.fold_in(own_key, 6), dim), (shards_of,), jnp.float32, low / len(cuts), high / len(cuts))
        factor_of = factor_of * jnp.repeat(jnp.exp(steps), extent[dim] // shards_of).reshape((-1,) + (1,) * (len(extent) - 1 - dim))
    return factor_of


def scatter_about(stream_key, shape, spread, reach, cuts=(), kind=jnp.bfloat16):
    values = spread * jax.random.normal(stream_key, shape, jnp.float32)
    if cuts:
        values = values * block_levels(stream_key, shape, cuts, -0.22, 0.18)
    return jnp.clip(values, -reach, reach).astype(kind)


def setup_inputs(seed: int = 0) -> dict:
    streams_of = jax.random.split(jax.random.key(seed), 12)
    return {
        "inner_state": scatter_about(streams_of[0], (2, ORDER), 1.0, 6.0, ((1, 16),), jnp.float32),
        "energy": jnp.clip(jax.random.uniform(streams_of[1], (ORDER,), jnp.float32, -20.0, 20.0) * block_levels(streams_of[1], (ORDER,), ((0, 16),), -0.4, 0.0), -20.0, 20.0),
        "blocks": scatter_about(streams_of[2], (STORED_BLOCKS, BLOCK_ROWS, BLOCK_ROWS), 0.2, 1.25, ((0, 128),), jnp.float32),
        "pattern": draw_pattern(jax.random.fold_in(streams_of[11], 71), 0),
        "surface": scatter_about(streams_of[4], (CHAN, ORDER), 0.5, 3.0, ((0, 8), (1, 16)), jnp.float32),
        "channel_symmetry": with_ends(jax.random.randint(streams_of[5], (CHAN,), 0, NSYM), jax.random.fold_in(streams_of[5], 1), 0, NSYM - 1).astype(jnp.int32),
        "outer_state": scatter_about(streams_of[6], (2, CHAN, RAD), 1.0, 6.0, ((1, 8), (2, 16)), jnp.float32),
        "channel_energy": jnp.clip(jax.random.uniform(streams_of[7], (CHAN,), jnp.float32, -10.0, 10.0) * block_levels(streams_of[7], (CHAN,), ((0, 8),), -0.4, 0.0), -10.0, 10.0),
        "couple_source": with_ends(jax.random.randint(streams_of[8], (CHAN, KCPL), 0, CHAN), jax.random.fold_in(streams_of[8], 1), 0, CHAN - 1).astype(jnp.int32),
        "couple_order": with_ends(jax.random.randint(streams_of[9], (CHAN, KCPL), 0, NLAM), jax.random.fold_in(streams_of[9], 1), 0, NLAM - 1).astype(jnp.int32),
        "couple_weight": scatter_about(streams_of[10], (CHAN, KCPL), 4.0, 24.0, (), jnp.float32),
    }


PRECISE = lax.Precision.HIGHEST
TIME_STEP = 0.05
GRID_STEP = 0.5
BOUNDARY_RADIUS = 20.0


def radial_grid(first, count):
    return BOUNDARY_RADIUS + (first + jnp.arange(count, dtype=jnp.int32) + 1).astype(jnp.float32) * GRID_STEP


def build_mats(source, order_list, weight, chan_total):
    onehot = source[:, :, None] == jnp.arange(chan_total, dtype=jnp.int32)[None, None, :]
    matrices = []
    for order in range(NLAM):
        picked = jnp.where(order_list == order, weight, jnp.float32(0.0))
        matrices.append(jnp.sum(jnp.where(onehot, picked[:, :, None], jnp.float32(0.0)), axis=1).astype(jnp.bfloat16))
    return jnp.stack(matrices)


def radial_sum(totals, radius):
    combined = jnp.zeros(totals.shape[1:], jnp.float32)
    for order in range(totals.shape[0]):
        combined = combined + (BOUNDARY_RADIUS / radius) ** order * totals[order]
    return combined


def reference(inner_state, energy, blocks, pattern, surface, channel_symmetry, outer_state, channel_energy, couple_source, couple_order, couple_weight):
    block_count = NSYM * BLOCKS_PER_SYMM
    rows = jnp.arange(ORDER, dtype=jnp.int32)
    masked = jnp.where(channel_symmetry[:, None] == (rows // SYM_ROWS)[None, :], surface, jnp.float32(0.0))
    coupling_mats = build_mats(couple_source, couple_order, couple_weight, CHAN).astype(jnp.float32)
    radius = radial_grid(0, RAD)
    angular = channel_symmetry.astype(jnp.float32)
    potential = angular[:, None] * (angular[:, None] + 1.0) / (2.0 * radius[None, :] ** 2) + channel_energy[:, None]
    stored_block_rows = (jnp.arange(STORED_BLOCKS, dtype=jnp.int32) // REGION_BLOCKS) * REGION_BLOCK_ROWS + pattern[:, 0]

    def hamiltonian(inner_vec, outer_vec):
        pieces = inner_vec.reshape(2, block_count, BLOCK_ROWS)[:, pattern[:, 1]]
        products = jnp.einsum("sij,psj->psi", blocks, pieces, precision=PRECISE)
        dipole = jnp.zeros((2, block_count, BLOCK_ROWS), jnp.float32).at[:, stored_block_rows].add(products).reshape(2, ORDER)
        boundary = jnp.dot(inner_vec, masked.T, precision=PRECISE)
        slope = (outer_vec[:, :, 0] - boundary) / GRID_STEP
        inner_out = energy * inner_vec + (dipole + 0.5 * jnp.dot(slope, masked, precision=PRECISE))
        padded = jnp.concatenate([boundary[:, :, None], outer_vec, jnp.zeros((2, CHAN, 1), jnp.float32)], axis=2)
        kinetic = -0.5 * (padded[:, :, 2:] - 2.0 * outer_vec + padded[:, :, :-2]) / (GRID_STEP * GRID_STEP)
        halves = outer_vec.astype(jnp.bfloat16).astype(jnp.float32)
        totals = jnp.einsum("lts,psr->lptr", coupling_mats, halves, precision=PRECISE)
        rounded = radial_sum(totals, radius).astype(jnp.bfloat16)
        mixed = lax.optimization_barrier(rounded).astype(jnp.float32)
        outer_out = kinetic + potential * outer_vec + mixed
        return inner_out, outer_out

    inner_vec, outer_vec = inner_state, outer_state
    total_inner, total_outer = inner_state, outer_state
    for term in (1, 2):
        inner_image, outer_image = hamiltonian(inner_vec, outer_vec)
        factor = TIME_STEP / term
        inner_vec = factor * jnp.stack([inner_image[1], -inner_image[0]])
        outer_vec = factor * jnp.stack([outer_image[1], -outer_image[0]])
        total_inner = total_inner + inner_vec
        total_outer = total_outer + outer_vec
    return total_inner, total_outer
```

```python
import functools

import jax
import jax.numpy as jnp
from jax import lax
from jax.experimental import pallas as pl
from jax.experimental.pallas import tpu as pltpu
from jax.sharding import PartitionSpec as P

BLOCKS_PER_SYMM = 4
NLAM = 3
TIME_STEP = 0.05
GRID_STEP = 0.5
BOUNDARY_RADIUS = 20.0
FIRST = TIME_STEP
SECOND = TIME_STEP / 2
LANES = 128
HALO_BLOCKS = 7
HALO_ROWS = 8 * HALO_BLOCKS
WINDOW = 64
F32 = jnp.float32
NT = (((1,), (1,)), ((), ()))


def params(megabytes):
    return pltpu.CompilerParams(vmem_limit_bytes=megabytes * 2**20)


def lane_index(shape):
    return lax.broadcasted_iota(jnp.int32, shape, len(shape) - 1)


def row_index(shape):
    return lax.broadcasted_iota(jnp.int32, shape, len(shape) - 2)


def square(rows):
    count = rows.shape[0]
    if count < LANES:
        rows = jnp.concatenate([rows, jnp.zeros((LANES - count, LANES), F32)], axis=0)
    return rows.T


def wide(column):
    return jnp.broadcast_to(column, (column.shape[0], LANES))


def boundary_sum(vec_rows, surf_ref, sym, first_tile, tiles):
    chan = surf_ref.shape[0]
    sums = [jnp.zeros((chan, LANES), F32) for _ in range(2)]
    for tile in range(tiles):
        here = ((first_tile + tile) // 16).astype(F32)
        values = jnp.where(sym == here, surf_ref[:, LANES * tile : LANES * (tile + 1)], 0.0)
        for part in range(2):
            sums[part] = sums[part] + values * vec_rows(tile, part)
    return [jnp.sum(total, axis=1, keepdims=True) for total in sums]


def surface_rows(slope, surf_ref, sym, first_tile, tiles, out_ref):
    columns = [wide(column) for column in slope]
    for tile in range(tiles):
        here = ((first_tile + tile) // 16).astype(F32)
        values = jnp.where(sym == here, surf_ref[:, LANES * tile : LANES * (tile + 1)], 0.0)
        rows = [jnp.sum(values * columns[part], axis=0, keepdims=True) for part in range(2)]
        at = slice(2 * tile, 2 * tile + 2)
        out_ref[at, :] = out_ref[at, :] + jnp.concatenate(rows, axis=0)


def turn_rows(rows):
    count = rows.shape[0]
    even = row_index(rows.shape) % 2 == 0
    return jnp.where(even, pltpu.roll(rows, count - 1, 0), -pltpu.roll(rows, 1, 0))


def turn_lanes(cells):
    other = pltpu.roll(cells, WINDOW, 1)
    return jnp.where(lane_index(cells.shape) < WINDOW, other, -other)


def start_kernel(idx_ref, u_ref, surf_ref, sym_ref, energy_ref, w_ref, first_ref, left_ref, right_ref, rows_ref, cols_ref, edge_ref, wt_ref):
    reg = idx_ref[0]
    tiles = u_ref.shape[1] // LANES
    chan = surf_ref.shape[0]
    head = jnp.zeros((1, LANES - chan), F32)
    sym_row = jnp.concatenate([sym_ref[...].astype(F32), head], axis=1)
    energy_row = jnp.concatenate([energy_ref[...], head], axis=1)
    base = square(jnp.concatenate([sym_row, energy_row], axis=0))
    sym = wide(base[:chan, 0:1])
    for tile in range(tiles):
        rows_ref[2 * tile : 2 * tile + 2, :] = u_ref[:, LANES * tile : LANES * (tile + 1)]
    partial = boundary_sum(
        lambda tile, part: u_ref[part : part + 1, LANES * tile : LANES * (tile + 1)],
        surf_ref, sym, reg * tiles, tiles,
    )
    for part in range(2):
        for piece in range(w_ref.shape[2] // LANES):
            cells = w_ref[part, :, LANES * piece : LANES * (piece + 1)]
            cells = jnp.concatenate([cells, jnp.zeros((LANES - chan, LANES), F32)], axis=0)
            wt_ref[part, LANES * piece : LANES * (piece + 1), :] = cells.T
    lane = lane_index((chan, LANES))
    cols = jnp.where(lane == 0, sym, 0.0)
    cols = jnp.where(lane == 1, wide(base[:chan, 1:2]), cols)
    for part in range(2):
        cols = jnp.where(lane == 2 + part, wide(partial[part]), cols)
    cols = jnp.concatenate([cols, jnp.zeros((cols_ref.shape[0] - chan, LANES), F32)], axis=0)
    cols_ref[...] = cols
    back = jnp.concatenate([cols, jnp.zeros((LANES - cols.shape[0], LANES), F32)], axis=0).T
    partial_rows = back[2:4, :]
    count = w_ref.shape[2]
    spot = lambda part, point: wt_ref[part, point : point + 1, :]
    zeros = jnp.zeros((2, LANES), F32)
    left_ref[:HALO_ROWS, :] = rows_ref[:HALO_ROWS, :]
    left_ref[HALO_ROWS:, :] = jnp.concatenate([partial_rows, spot(0, 0), spot(0, 1), spot(1, 0), spot(1, 1), zeros], axis=0)
    right_ref[:HALO_ROWS, :] = rows_ref[2 * tiles - HALO_ROWS :, :]
    right_ref[HALO_ROWS:, :] = jnp.concatenate(
        [partial_rows, spot(0, count - 2), spot(0, count - 1), spot(1, count - 2), spot(1, count - 1), zeros], axis=0
    )
    cell0 = jnp.concatenate([spot(0, 0), spot(1, 0)], axis=0)
    cell1 = jnp.concatenate([spot(0, 1), spot(1, 1)], axis=0)
    shifted = pltpu.roll(jnp.concatenate([cell0] * 4, axis=0), WINDOW, 1)[0:2]
    group = 8
    first_ref[0:group] = jnp.broadcast_to((partial_rows + shifted)[None], (group, 2, LANES))
    others = first_ref.shape[0] - group
    first_ref[group:] = jnp.broadcast_to((cell1 + shifted)[None], (others, 2, LANES))
    windows = count // WINDOW
    zero = jnp.zeros((1, LANES), F32)
    for window in range(windows):
        low, high = WINDOW * window - 1, WINDOW * (window + 1)
        edge_ref[4 * window : 4 * window + 4, :] = jnp.concatenate(
            [
                spot(0, low) if window else zero,
                spot(1, low) if window else zero,
                spot(0, high) if window < windows - 1 else zero,
                spot(1, high) if window < windows - 1 else zero,
            ],
            axis=0,
        )
    edge_ref[4 * windows : 4 * windows + 8, :] = jnp.concatenate([cell1, cell0, sym_row, energy_row, zeros], axis=0)


def expand_states(left_ref, mine_ref, right_ref, states_ref):
    shape = (8, 4 * LANES)
    keep = row_index(shape) // 2 == lane_index(shape) // LANES
    blocks = mine_ref.shape[0] // 8
    for column in range(2 * HALO_BLOCKS + blocks):
        if column < HALO_BLOCKS:
            rows = left_ref[8 * column : 8 * column + 8, :]
        elif column < HALO_BLOCKS + blocks:
            at = 8 * (column - HALO_BLOCKS)
            rows = mine_ref[at : at + 8, :]
        else:
            at = 8 * (column - HALO_BLOCKS - blocks)
            rows = right_ref[at : at + 8, :]
        whole = jnp.where(keep, jnp.concatenate([rows] * 4, axis=1), 0.0)
        lead = whole.astype(jnp.bfloat16).astype(F32)
        states_ref[column] = jnp.concatenate([lead, whole - lead], axis=0).astype(jnp.bfloat16)


def add_block(pattern_ref, idx_ref, block_ref, states_ref, sums_ref):
    step = pl.program_id(0)
    rows = sums_ref.shape[0]
    column = jnp.clip(pattern_ref[step, 1] - idx_ref[0] * rows + HALO_BLOCKS, 0, states_ref.shape[0] - 1)
    row = jnp.clip(pattern_ref[step, 0], 0, rows - 1)
    state = states_ref[column]
    block = block_ref[0]
    lead = block.astype(jnp.bfloat16)
    rest = (block - lead.astype(F32)).astype(jnp.bfloat16)
    product = lax.dot_general(state, lead, NT, preferred_element_type=F32)
    product = product + lax.dot_general(state, rest, NT, preferred_element_type=F32)
    sums_ref[row] = sums_ref[row] + (product[:8] + product[8:])


def fold_sums(sums_ref, out_ref):
    shape = (8, LANES)
    for row in range(sums_ref.shape[0]):
        total = sums_ref[row]
        total = total + pltpu.roll(total, 4, 0)
        total = total + pltpu.roll(total, 2, 0)
        picked = jnp.zeros(shape, F32)
        for piece in range(4):
            picked = jnp.where(row_index(shape) // 2 == piece, total[:, LANES * piece : LANES * (piece + 1)], picked)
        out_ref[8 * row : 8 * row + 8, :] = picked


def dipole_kernel(pattern_ref, idx_ref, block_ref, mine_ref, left_ref, right_ref, out_ref, states_ref, sums_ref):
    step = pl.program_id(0)

    @pl.when(step == 0)
    def _():
        expand_states(left_ref, mine_ref, right_ref, states_ref)
        sums_ref[...] = jnp.zeros(sums_ref.shape, F32)

    add_block(pattern_ref, idx_ref, block_ref, states_ref, sums_ref)

    @pl.when(step == pl.num_programs(0) - 1)
    def _():
        fold_sums(sums_ref, out_ref)


def pack_kernel(idx_ref, dipole_ref, surf_ref, cols_ref, edge_ref, w_ref, first_ref, left_ref, right_ref, message_ref, side_ref, total_ref):
    reg, ch = idx_ref[0], idx_ref[1]
    chan = surf_ref.shape[0]
    padded = cols_ref.shape[0]
    tiles = surf_ref.shape[1] // LANES
    windows = message_ref.shape[0]
    regs = first_ref.shape[0] // windows
    sym = wide(cols_ref[:chan, 0:1])
    received = first_ref[ch]
    lane2 = lane_index((2, LANES))
    low = jnp.where(lane2 < WINDOW, received, 0.0)
    cell0 = jnp.where(lane2 < WINDOW, pltpu.roll(jnp.concatenate([received] * 4, axis=0), WINDOW, 1)[0:2], 0.0)
    cell1 = jnp.where(reg == 0, edge_ref[4 * windows : 4 * windows + 2, :], low)
    whole = jnp.zeros((2, LANES), F32)
    for source in range(regs):
        whole = whole + first_ref[source * windows + ch]
    whole = jnp.where((lane2 < WINDOW) & (reg == 0), whole, 0.0)
    beside = left_ref[HALO_ROWS : HALO_ROWS + 2, :] + right_ref[HALO_ROWS : HALO_ROWS + 2, :]
    side = square(
        jnp.concatenate(
            [
                cell0, cell1, beside, whole,
                left_ref[HALO_ROWS + 2 : HALO_ROWS + 4, :], right_ref[HALO_ROWS + 2 : HALO_ROWS + 4, :],
                left_ref[HALO_ROWS + 4 : HALO_ROWS + 6, :], right_ref[HALO_ROWS + 4 : HALO_ROWS + 6, :],
            ],
            axis=0,
        )
    )[:chan]
    symmetry, energy = cols_ref[:chan, 0:1], cols_ref[:chan, 1:2]
    radius = BOUNDARY_RADIUS + GRID_STEP
    potential = symmetry * (symmetry + 1.0) / (2.0 * radius * radius) + energy
    slope, start = [], []
    for part in range(2):
        here, beyond = side[:, part : part + 1], side[:, 2 + part : 3 + part]
        boundary = cols_ref[:chan, 2 + part : 3 + part] + side[:, 4 + part : 5 + part]
        slope.append(here - boundary)
        start.append(-2.0 * (beyond - 2.0 * here + boundary) + potential * here)
    lane = lane_index((chan, LANES))
    out = jnp.where((lane >= 6) & (lane < 16), side, 0.0)
    for part in range(2):
        out = jnp.where(lane == part, wide(start[part]), out)
    out = jnp.where(lane == 2, sym, out)
    out = jnp.where(lane == 3, wide(energy), out)
    side_ref[...] = jnp.concatenate([out, jnp.zeros((padded - chan, LANES), F32)], axis=0)
    total_ref[...] = dipole_ref[...]
    surface_rows(slope, surf_ref, sym, reg * tiles, tiles, total_ref)
    lines = total_ref.shape[0]
    total = total_ref[...]
    tail = jnp.concatenate([edge_ref[4 * windows + 4 : 4 * windows + 6, :], whole, jnp.zeros((6, LANES), F32)], axis=0)
    half = lane < WINDOW
    for window in range(windows):
        message_ref[window, :lines, :] = total
        at = LANES * (window // 2)
        one, two = w_ref[0, :, at : at + LANES], w_ref[1, :, at : at + LANES]
        if window % 2 == 0:
            cells = jnp.where(half, one, pltpu.roll(two, WINDOW, 1))
        else:
            cells = jnp.where(half, pltpu.roll(one, WINDOW, 1), two)
        message_ref[window, lines : lines + padded, :] = jnp.concatenate(
            [cells, jnp.zeros((padded - chan, LANES), F32)], axis=0
        )
        edges = edge_ref[4 * window : 4 * window + 4, :]
        if window == 0:
            edges = jnp.concatenate([left_ref[HALO_ROWS + 3 : HALO_ROWS + 4, :], left_ref[HALO_ROWS + 5 : HALO_ROWS + 6, :], edges[2:4]], axis=0)
        if window == windows - 1:
            edges = jnp.concatenate([edges[0:2], right_ref[HALO_ROWS + 2 : HALO_ROWS + 3, :], right_ref[HALO_ROWS + 4 : HALO_ROWS + 5, :]], axis=0)
        message_ref[window, lines + padded :, :] = jnp.concatenate([edges, cell0, tail], axis=0)


def doubled(energy_ref, rows_ref):
    for tile in range(energy_ref.shape[0]):
        rows_ref[2 * tile : 2 * tile + 2, :] = jnp.broadcast_to(energy_ref[tile : tile + 1, :], (2, LANES))


def update_kernel(idx_ref, received_ref, u_ref, energy_ref, surf_ref, cols_ref, out_ref, left_ref, right_ref, energy_rows_ref):
    reg = idx_ref[0]
    lines = u_ref.shape[0]
    tiles = lines // 2
    chan = surf_ref.shape[0]
    doubled(energy_ref, energy_rows_ref)
    image = energy_rows_ref[...] * u_ref[...]
    for source in range(received_ref.shape[0]):
        image = image + received_ref[source, :lines, :]
    out_ref[...] = FIRST * turn_rows(image)
    sym = wide(cols_ref[:chan, 0:1])
    partial = boundary_sum(
        lambda tile, part: out_ref[2 * tile + part : 2 * tile + part + 1, :], surf_ref, sym, reg * tiles, tiles
    )
    lane = lane_index((chan, LANES))
    cols = jnp.where(lane == 0, wide(partial[0]), 0.0)
    cols = jnp.where(lane == 1, wide(partial[1]), cols)
    rows = jnp.concatenate([cols, jnp.zeros((LANES - chan, LANES), F32)], axis=0).T[0:8, :]
    left_ref[:HALO_ROWS, :] = out_ref[:HALO_ROWS, :]
    left_ref[HALO_ROWS:, :] = rows
    right_ref[:HALO_ROWS, :] = out_ref[lines - HALO_ROWS :, :]
    right_ref[HALO_ROWS:, :] = rows


def stencil(cells, lows, highs, potential, seams):
    count = cells.shape[1]
    lane = lane_index(cells.shape)
    below, above = pltpu.roll(cells, 1, 1), pltpu.roll(cells, count - 1, 1)
    for (first, last), low, high in zip(seams, lows, highs):
        below = jnp.where(lane == first, low, below)
        above = jnp.where(lane == last, high, above)
    return -2.0 * (above - 2.0 * cells + below) + potential * cells


def outer_kernel(idx_ref, received_ref, mats_ref, w_ref, side_ref, cross_ref, start_ref, plain_ref, edge_ref):
    reg, ch = idx_ref[0], idx_ref[1]
    groups, padded = cross_ref.shape[0], cross_ref.shape[1]
    chan, count = w_ref.shape[1], w_ref.shape[2]
    rows = groups * padded
    lines = received_ref.shape[1] - padded - 16
    cells = received_ref[:, lines : lines + padded, :].reshape(rows, LANES)
    flipped = received_ref[:, lines + padded :, :].reshape(groups * 16, LANES).T
    extra = jnp.concatenate(
        [pltpu.roll(flipped[:padded], (LANES - 16 * group) % LANES, 1) for group in range(groups)], axis=0
    )
    first_point = reg * count + ch * WINDOW
    lane = lane_index((1, LANES))
    point = (first_point + lane % WINDOW + 1).astype(F32)
    radius = BOUNDARY_RADIUS + GRID_STEP * point
    extra_point = jnp.where(lane < 2, first_point, jnp.where(lane < 4, first_point + WINDOW + 1, 1)).astype(F32)
    extra_ratio = BOUNDARY_RADIUS / (BOUNDARY_RADIUS + GRID_STEP * extra_point)
    ratio = BOUNDARY_RADIUS / radius

    def mix(states, scale):
        totals = jnp.dot(mats_ref[...], states.astype(jnp.bfloat16), preferred_element_type=F32)
        mixed = totals[:rows] + scale * totals[rows : 2 * rows] + scale * scale * totals[2 * rows :]
        return mixed.astype(jnp.bfloat16).astype(F32)

    symmetry, energy = extra[:, 6:7], extra[:, 7:8]
    potential = symmetry * (symmetry + 1.0) / (2.0 * radius * radius) + energy
    mixed = mix(jnp.concatenate([cells, extra], axis=1), jnp.concatenate([ratio, extra_ratio], axis=1))
    main, beside = mixed[:, :LANES], mixed[:, LANES:]
    edge_ref[...] = beside
    start_ref[...] = edge_ref[pl.ds(pl.multiple_of(ch * padded, 8), padded), :]
    inner_end = (reg == 0) & (ch == 0)
    seams = ((0, WINDOW - 1), (WINDOW, 2 * WINDOW - 1))
    lows = [jnp.where(inner_end, extra[:, 8 + part : 9 + part], extra[:, part : part + 1]) for part in range(2)]
    highs = [extra[:, 2 + part : 3 + part] for part in range(2)]
    first = FIRST * turn_lanes(stencil(cells, lows, highs, potential, seams) + main)
    later = mix(first, ratio)
    cross = FIRST * turn_lanes(main)
    mixed_lows = [jnp.where(inner_end, 0.0, beside[:, part : part + 1]) for part in range(2)]
    mixed_highs = [beside[:, 2 + part : 3 + part] for part in range(2)]
    lows = [FIRST * mixed_lows[1], -FIRST * mixed_lows[0]]
    highs = [FIRST * mixed_highs[1], -FIRST * mixed_highs[0]]
    cross = cross + SECOND * turn_lanes(stencil(cross, lows, highs, potential, seams) + later)
    cross_ref[...] = cross.reshape(groups, padded, LANES)

    side = side_ref[...][:chan]
    symmetry, energy = side[:, 2:3], side[:, 3:4]
    lane = lane_index((1, count))
    radius = BOUNDARY_RADIUS + GRID_STEP * (reg * count + lane + 1).astype(F32)
    potential = symmetry * (symmetry + 1.0) / (2.0 * radius * radius) + energy

    def potential_at(index):
        there = BOUNDARY_RADIUS + GRID_STEP * (reg * count + index + 1).astype(F32)
        return symmetry * (symmetry + 1.0) / (2.0 * there * there) + energy

    last = (reg + 1) * count >= cross_end(count)
    images, lows, highs = [], [], []
    for part in range(2):
        values = w_ref[part]
        at = 8 + 4 * part
        low2, low1, high1, high2 = (side[:, at + i : at + i + 1] for i in range(4))
        low = jnp.where(reg == 0, side[:, 6 + part : 7 + part], low1)
        images.append(stencil(values, [low], [high1], potential, ((0, count - 1),)))
        under = -2.0 * (values[:, 0:1] - 2.0 * low1 + low2) + potential_at(jnp.int32(-1)) * low1
        over = -2.0 * (high2 - 2.0 * high1 + values[:, count - 1 : count]) + potential_at(jnp.int32(count)) * high1
        lows.append(jnp.where(reg == 0, 0.0, under))
        highs.append(jnp.where(last, 0.0, over))
    turned = [FIRST * images[1], -FIRST * images[0]]
    lows = [FIRST * lows[1], -FIRST * lows[0]]
    highs = [FIRST * highs[1], -FIRST * highs[0]]
    again = [stencil(turned[p], [lows[p]], [highs[p]], potential, ((0, count - 1),)) for p in range(2)]
    plain_ref[0] = w_ref[0] + turned[0] + SECOND * again[1]
    plain_ref[1] = w_ref[1] + turned[1] - SECOND * again[0]


def cross_end(count):
    return 16 * count


def second_kernel(
    pattern_ref, idx_ref, block_ref, mine_ref, left_ref, right_ref, own_ref, surf_ref, side_ref, start_ref, cross_ref,
    message_ref, states_ref, sums_ref, total_ref,
):
    step = pl.program_id(0)

    @pl.when(step == 0)
    def _():
        expand_states(left_ref, mine_ref, right_ref, states_ref)
        sums_ref[...] = jnp.zeros(sums_ref.shape, F32)

    add_block(pattern_ref, idx_ref, block_ref, states_ref, sums_ref)

    @pl.when(step == pl.num_programs(0) - 1)
    def _():
        reg = idx_ref[0]
        chan = surf_ref.shape[0]
        tiles = surf_ref.shape[1] // LANES
        fold_sums(sums_ref, total_ref)
        ends = own_ref[HALO_ROWS:, :] + left_ref[HALO_ROWS:, :] + right_ref[HALO_ROWS:, :]
        boundary = square(ends)[:chan]
        mixed = start_ref[:chan, :]
        side = side_ref[:chan, :]
        image = [side[:, part : part + 1] + mixed[:, 4 + part : 5 + part] for part in range(2)]
        slope = [FIRST * image[1] - boundary[:, 0:1], -FIRST * image[0] - boundary[:, 1:2]]
        surface_rows(slope, surf_ref, wide(side[:, 2:3]), reg * tiles, tiles, total_ref)
        lines = total_ref.shape[0]
        for group in range(message_ref.shape[0]):
            message_ref[group, :lines, :] = total_ref[...]
            message_ref[group, lines:, :] = cross_ref[group]


def finish_kernel(idx_ref, received_ref, u_ref, first_ref, energy_ref, plain_ref, ends_ref, inner_ref, outer_ref, energy_rows_ref):
    reg = idx_ref[0]
    lines = u_ref.shape[0]
    chan = plain_ref.shape[1]
    doubled(energy_ref, energy_rows_ref)
    image = energy_rows_ref[...] * first_ref[...]
    sources = received_ref.shape[0]
    for source in range(sources):
        image = image + received_ref[source, :lines, :]
    total = u_ref[...] + first_ref[...] + SECOND * turn_rows(image)
    energy_rows_ref[...] = total
    for tile in range(lines // 2):
        inner_ref[:, LANES * tile : LANES * (tile + 1)] = energy_rows_ref[2 * tile : 2 * tile + 2, :]
    columns = square(ends_ref[...])[:chan]
    lane = lane_index((chan, LANES))
    half = lane < WINDOW
    for piece in range(sources // 2):
        even = received_ref[2 * piece, lines : lines + chan, :]
        odd = received_ref[2 * piece + 1, lines : lines + chan, :]
        one = jnp.where(half, even, pltpu.roll(odd, WINDOW, 1))
        two = jnp.where(half, pltpu.roll(even, WINDOW, 1), odd)
        at = slice(LANES * piece, LANES * (piece + 1))
        one = plain_ref[0, :, at] + one
        two = plain_ref[1, :, at] + two
        if piece == 0:
            here = (lane == 0) & (reg == 0)
            one = one + jnp.where(here, -2.0 * SECOND * columns[:, 1:2], 0.0)
            two = two + jnp.where(here, 2.0 * SECOND * columns[:, 0:1], 0.0)
        outer_ref[0, :, at] = one
        outer_ref[1, :, at] = two


def build_mats(source, order_list, weight, groups, chan_local, padded):
    def lay(values, fill):
        values = values.reshape(groups, chan_local, values.shape[1])
        values = jnp.pad(values, ((0, 0), (0, padded - chan_local), (0, 0)), constant_values=fill)
        return values.reshape(groups * padded, -1)

    place = (source // chan_local) * padded + source % chan_local
    place, order_list, weight = lay(place, 0), lay(order_list, NLAM), lay(weight, 0)
    onehot = place[:, :, None] == jnp.arange(groups * padded, dtype=jnp.int32)[None, None, :]
    matrices = []
    for order in range(NLAM):
        picked = jnp.where(order_list == order, weight, 0.0)
        matrices.append(jnp.sum(jnp.where(onehot, picked[:, :, None], 0.0), axis=1).astype(jnp.bfloat16))
    return jnp.concatenate(matrices, axis=0)


def shape_of(*shape):
    return jax.ShapeDtypeStruct(shape, F32)


def local(
    inner_state, energy, blocks, pattern, surface, channel_symmetry, outer_state, channel_energy,
    couple_source, couple_order, couple_weight, *, regs, groups,
):
    tile_len = inner_state.shape[1]
    lines = 2 * tile_len // LANES
    block_len = blocks.shape[1]
    block_rows = tile_len // block_len
    chan = outer_state.shape[1]
    count = outer_state.shape[2]
    padded = -(-chan // 8) * 8
    devices = regs * groups
    idx = jnp.stack([lax.axis_index("reg"), lax.axis_index("ch")]).astype(jnp.int32)
    smem = pl.BlockSpec(memory_space=pltpu.SMEM)
    vmem = pl.BlockSpec(memory_space=pltpu.VMEM)
    halo = HALO_ROWS + 8
    energy_rows = energy.reshape(lines // 2, LANES)

    first_msg, left, right, rows, cols, edges = pl.pallas_call(
        start_kernel,
        out_shape=(
            shape_of(devices, 2, LANES), shape_of(halo, LANES), shape_of(halo, LANES), shape_of(lines, LANES),
            shape_of(padded, LANES), shape_of(4 * groups + 8, LANES),
        ),
        in_specs=[smem] + [vmem] * 5,
        out_specs=(vmem,) * 6,
        scratch_shapes=[pltpu.VMEM((2, count, LANES), F32)],
        compiler_params=params(32),
        name="start",
    )(idx, inner_state, surface, channel_symmetry.reshape(1, chan), channel_energy.reshape(1, chan), outer_state)

    firsts = lax.all_to_all(first_msg, ("reg", "ch"), 0, 0)
    up = [(i, i + 1) for i in range(regs - 1)]
    down = [(i + 1, i) for i in range(regs - 1)]
    from_left = lax.ppermute(right, "reg", up)
    from_right = lax.ppermute(left, "reg", down)
    mats = build_mats(couple_source, couple_order, couple_weight, groups, chan, padded)

    whole = lambda *shape: pl.BlockSpec(shape, lambda step, *_: (0,) * len(shape))
    block_spec = pl.BlockSpec((1, block_len, block_len), lambda step, *_: (step, 0, 0))
    states = pltpu.VMEM((2 * HALO_BLOCKS + block_rows, 16, block_len), jnp.bfloat16)
    sums = pltpu.VMEM((block_rows, 8, block_len), F32)
    dipole = pl.pallas_call(
        dipole_kernel,
        grid_spec=pltpu.PrefetchScalarGridSpec(
            num_scalar_prefetch=2,
            grid=(blocks.shape[0],),
            in_specs=[block_spec, whole(lines, LANES), whole(halo, LANES), whole(halo, LANES)],
            out_specs=whole(lines, LANES),
            scratch_shapes=[states, sums],
        ),
        out_shape=shape_of(lines, LANES),
        compiler_params=params(32),
        name="dipole",
    )(pattern, idx, blocks, rows, from_left, from_right)

    message, side = pl.pallas_call(
        pack_kernel,
        out_shape=(shape_of(groups, lines + padded + 16, LANES), shape_of(padded, LANES)),
        in_specs=[smem] + [vmem] * 8,
        out_specs=(vmem,) * 2,
        scratch_shapes=[pltpu.VMEM((lines, LANES), F32)],
        compiler_params=params(32),
        name="pack",
    )(idx, dipole, surface, cols, edges, outer_state, firsts, from_left, from_right)
    received = lax.all_to_all(message, "ch", 0, 0)

    first, left, right = pl.pallas_call(
        update_kernel,
        out_shape=(shape_of(lines, LANES), shape_of(halo, LANES), shape_of(halo, LANES)),
        in_specs=[smem] + [vmem] * 5,
        out_specs=(vmem,) * 3,
        scratch_shapes=[pltpu.VMEM((lines, LANES), F32)],
        compiler_params=params(32),
        name="update",
    )(idx, received, rows, energy_rows, surface, cols)
    from_left = lax.ppermute(right, "reg", up)
    from_right = lax.ppermute(left, "reg", down)

    cross, start, plain = pl.pallas_call(
        outer_kernel,
        out_shape=(shape_of(groups, padded, LANES), shape_of(padded, LANES), shape_of(2, chan, count)),
        in_specs=[smem] + [vmem] * 4,
        out_specs=(vmem,) * 3,
        scratch_shapes=[pltpu.VMEM((groups * padded, LANES), F32)],
        compiler_params=params(48),
        name="outer",
    )(idx, received, mats, outer_state, side)

    message = pl.pallas_call(
        second_kernel,
        grid_spec=pltpu.PrefetchScalarGridSpec(
            num_scalar_prefetch=2,
            grid=(blocks.shape[0],),
            in_specs=[
                block_spec, whole(lines, LANES), whole(halo, LANES), whole(halo, LANES), whole(halo, LANES),
                whole(chan, tile_len), whole(padded, LANES), whole(padded, LANES), whole(groups, padded, LANES),
            ],
            out_specs=whole(groups, lines + padded, LANES),
            scratch_shapes=[states, sums, pltpu.VMEM((lines, LANES), F32)],
        ),
        out_shape=shape_of(groups, lines + padded, LANES),
        compiler_params=params(32),
        name="second",
    )(pattern, idx, blocks, first, from_left, from_right, left, surface, side, start, cross)

    ends = left[HALO_ROWS:] + from_right[HALO_ROWS:]
    step = 2
    while step < regs:
        pairs = [(i + step, i) for i in range(0, regs, 2 * step)]
        ends = ends + lax.ppermute(ends, "reg", pairs)
        step *= 2
    received = lax.all_to_all(message, "ch", 0, 0)

    return pl.pallas_call(
        finish_kernel,
        out_shape=(shape_of(2, tile_len), shape_of(2, chan, count)),
        in_specs=[smem] + [vmem] * 6,
        out_specs=(vmem,) * 2,
        scratch_shapes=[pltpu.VMEM((lines, LANES), F32)],
        compiler_params=params(32),
        name="finish",
    )(idx, received, rows, first, energy_rows, plain, ends)


def solution(mesh):
    return jax.shard_map(
        functools.partial(local, regs=mesh.shape["reg"], groups=mesh.shape["ch"]),
        mesh=mesh,
        in_specs=(
            P(None, "reg"),
            P("reg"),
            P(("reg", "ch"), None, None),
            P(("reg", "ch"), None),
            P("ch", "reg"),
            P("ch"),
            P(None, "ch", "reg"),
            P("ch"),
            P(),
            P(),
            P(),
        ),
        out_specs=(P(None, "reg"), P(None, "ch", "reg")),
        check_vma=False,
    )
```

```python
import functools

import jax
import jax.numpy as jnp
from jax import lax
from jax.experimental import pallas as pl
from jax.experimental.pallas import tpu as pltpu
from jax.sharding import PartitionSpec as P

BLOCKS_PER_SYMM = 4
NLAM = 3
TIME_STEP = 0.05
GRID_STEP = 0.5
BOUNDARY_RADIUS = 20.0
FIRST = TIME_STEP
SECOND = TIME_STEP / 2
LANES = 128
HALO_BLOCKS = 7
HALO_ROWS = 8 * HALO_BLOCKS
WINDOW = 64
F32 = jnp.float32
NT = (((1,), (1,)), ((), ()))


def params(megabytes):
    return pltpu.CompilerParams(vmem_limit_bytes=megabytes * 2**20)


def lane_index(shape):
    return lax.broadcasted_iota(jnp.int32, shape, len(shape) - 1)


def row_index(shape):
    return lax.broadcasted_iota(jnp.int32, shape, len(shape) - 2)


def square(rows):
    count = rows.shape[0]
    if count < LANES:
        rows = jnp.concatenate([rows, jnp.zeros((LANES - count, LANES), F32)], axis=0)
    return rows.T


def wide(column):
    return jnp.broadcast_to(column, (column.shape[0], LANES))


def cells_of(w_ref, part, piece, chan):
    pieces = w_ref.shape[0] // (2 * chan)
    return w_ref[pl.ds(2 * piece + part, chan, stride=2 * pieces), :]


def boundary_sum(vec_rows, surf_ref, sym, first_tile, tiles):
    chan = surf_ref.shape[0]
    sums = [jnp.zeros((chan, LANES), F32) for _ in range(2)]
    for tile in range(tiles):
        here = ((first_tile + tile) // 16).astype(F32)
        values = jnp.where(sym == here, surf_ref[:, LANES * tile : LANES * (tile + 1)], 0.0)
        for part in range(2):
            sums[part] = sums[part] + values * vec_rows(tile, part)
    return [jnp.sum(total, axis=1, keepdims=True) for total in sums]


def surface_rows(slope, surf_ref, sym, first_tile, tiles, out_ref):
    columns = [wide(column) for column in slope]
    for tile in range(tiles):
        here = ((first_tile + tile) // 16).astype(F32)
        values = jnp.where(sym == here, surf_ref[:, LANES * tile : LANES * (tile + 1)], 0.0)
        rows = [jnp.sum(values * columns[part], axis=0, keepdims=True) for part in range(2)]
        at = slice(2 * tile, 2 * tile + 2)
        out_ref[at, :] = out_ref[at, :] + jnp.concatenate(rows, axis=0)


def turn_rows(rows):
    count = rows.shape[0]
    even = row_index(rows.shape) % 2 == 0
    return jnp.where(even, pltpu.roll(rows, count - 1, 0), -pltpu.roll(rows, 1, 0))


def turn_lanes(cells):
    other = pltpu.roll(cells, WINDOW, 1)
    return jnp.where(lane_index(cells.shape) < WINDOW, other, -other)


def start_kernel(
    idx_ref, u_hbm, surf_hbm, w_hbm, energy_hbm, sym_hbm, level_hbm,
    first_ref, left_ref, right_ref, rows_ref, cols_ref, edge_ref, doubled_ref,
    wt_ref, u_ref, surf_ref, w_ref, energy_ref, sym_ref, level_ref, sems,
):
    copies = [
        pltpu.make_async_copy(source, target, sems.at[i])
        for i, (source, target) in enumerate(
            [
                (sym_hbm, sym_ref), (level_hbm, level_ref), (w_hbm, w_ref), (energy_hbm, energy_ref), (u_hbm, u_ref),
                (surf_hbm, surf_ref),
            ]
        )
    ]
    for copy in copies:
        copy.start()
    reg = idx_ref[0]
    tiles = u_ref.shape[1] // LANES
    chan = surf_ref.shape[0]
    copies[0].wait()
    copies[1].wait()
    head = jnp.zeros((1, LANES - chan), F32)
    sym_row = jnp.concatenate([sym_ref[...].astype(F32), head], axis=1)
    energy_row = jnp.concatenate([level_ref[...], head], axis=1)
    base = square(jnp.concatenate([sym_row, energy_row], axis=0))
    sym = wide(base[:chan, 0:1])
    copies[2].wait()
    for part in range(2):
        for piece in range(wt_ref.shape[1] // LANES):
            cells = cells_of(w_ref, part, piece, chan)
            cells = jnp.concatenate([cells, jnp.zeros((LANES - chan, LANES), F32)], axis=0)
            wt_ref[part, LANES * piece : LANES * (piece + 1), :] = cells.T
    copies[3].wait()
    for tile in range(tiles):
        doubled_ref[2 * tile : 2 * tile + 2, :] = jnp.broadcast_to(energy_ref[tile : tile + 1, :], (2, LANES))
    copies[4].wait()
    for tile in range(tiles):
        rows_ref[2 * tile : 2 * tile + 2, :] = u_ref[:, LANES * tile : LANES * (tile + 1)]
    copies[5].wait()
    partial = boundary_sum(
        lambda tile, part: u_ref[part : part + 1, LANES * tile : LANES * (tile + 1)],
        surf_ref, sym, reg * tiles, tiles,
    )
    lane = lane_index((chan, LANES))
    cols = jnp.where(lane == 0, sym, 0.0)
    cols = jnp.where(lane == 1, wide(base[:chan, 1:2]), cols)
    for part in range(2):
        cols = jnp.where(lane == 2 + part, wide(partial[part]), cols)
    cols = jnp.concatenate([cols, jnp.zeros((cols_ref.shape[0] - chan, LANES), F32)], axis=0)
    cols_ref[...] = cols
    back = jnp.concatenate([cols, jnp.zeros((LANES - cols.shape[0], LANES), F32)], axis=0).T
    partial_rows = back[2:4, :]
    count = wt_ref.shape[1]
    spot = lambda part, point: wt_ref[part, point : point + 1, :]
    zeros = jnp.zeros((2, LANES), F32)
    left_ref[:HALO_ROWS, :] = rows_ref[:HALO_ROWS, :]
    left_ref[HALO_ROWS:, :] = jnp.concatenate([partial_rows, spot(0, 0), spot(0, 1), spot(1, 0), spot(1, 1), zeros], axis=0)
    right_ref[:HALO_ROWS, :] = rows_ref[2 * tiles - HALO_ROWS :, :]
    right_ref[HALO_ROWS:, :] = jnp.concatenate(
        [partial_rows, spot(0, count - 2), spot(0, count - 1), spot(1, count - 2), spot(1, count - 1), zeros], axis=0
    )
    cell0 = jnp.concatenate([spot(0, 0), spot(1, 0)], axis=0)
    cell1 = jnp.concatenate([spot(0, 1), spot(1, 1)], axis=0)
    shifted = pltpu.roll(jnp.concatenate([cell0] * 4, axis=0), WINDOW, 1)[0:2]
    first_ref[0] = partial_rows + shifted
    others = first_ref.shape[0] - 1
    first_ref[1:] = jnp.broadcast_to((cell1 + shifted)[None], (others, 2, LANES))
    windows = count // WINDOW
    zero = jnp.zeros((1, LANES), F32)
    for window in range(windows):
        low, high = WINDOW * window - 1, WINDOW * (window + 1)
        edge_ref[4 * window : 4 * window + 4, :] = jnp.concatenate(
            [
                spot(0, low) if window else zero,
                spot(1, low) if window else zero,
                spot(0, high) if window < windows - 1 else zero,
                spot(1, high) if window < windows - 1 else zero,
            ],
            axis=0,
        )
    edge_ref[4 * windows : 4 * windows + 8, :] = jnp.concatenate([cell1, cell0, sym_row, energy_row, zeros], axis=0)


def add_blocks(idx_ref, pattern_hbm, blocks, mine_ref, left_ref, right_ref, out_ref, pattern_ref, states_ref, sums_ref, sem):
    count, block_len = pattern_ref.shape[1], sums_ref.shape[2]
    rows = mine_ref.shape[0] // 8
    pieces = block_len // LANES
    copy = pltpu.make_async_copy(pattern_hbm, pattern_ref, sem)
    copy.start()
    for column in range(HALO_BLOCKS):
        states_ref[column] = left_ref[8 * column : 8 * column + 8, :]
        states_ref[HALO_BLOCKS + rows + column] = right_ref[8 * column : 8 * column + 8, :]
    for column in range(rows):
        states_ref[HALO_BLOCKS + column] = mine_ref[8 * column : 8 * column + 8, :]
    sums_ref[...] = jnp.zeros(sums_ref.shape, F32)
    copy.wait()
    for i in range(count):
        row = jnp.clip(pattern_ref[0, i], 0, rows - 1)
        column = jnp.clip(pattern_ref[1, i] - idx_ref[0] * rows + HALO_BLOCKS, 0, states_ref.shape[0] - 1)
        tile = states_ref[column]
        state = jnp.concatenate([tile[2 * piece : 2 * piece + 2, :] for piece in range(pieces)], axis=1)
        lead = state.astype(jnp.bfloat16).astype(F32)
        state = jnp.concatenate([lead, state - lead, jnp.zeros((12, block_len), F32)], axis=0).astype(jnp.bfloat16)
        block = blocks(i)
        lead = block.astype(jnp.bfloat16)
        rest = (block - lead.astype(F32)).astype(jnp.bfloat16)
        product = lax.dot_general(state, lead, NT, preferred_element_type=F32)
        product = product + lax.dot_general(state, rest, NT, preferred_element_type=F32)
        sums_ref[row] = sums_ref[row] + product[:8]
    shape = (8, LANES)
    for row in range(rows):
        total = sums_ref[row]
        total = total + pltpu.roll(total, 6, 0)
        picked = jnp.zeros(shape, F32)
        for piece in range(pieces):
            values = total[:, LANES * piece : LANES * (piece + 1)]
            values = pltpu.roll(values, 2 * piece, 0) if piece else values
            picked = jnp.where(row_index(shape) // 2 == piece, values, picked)
        out_ref[8 * row : 8 * row + 8, :] = picked


def fetched(blocks_hbm, first, held_ref, sems):
    copies = [pltpu.make_async_copy(blocks_hbm.at[first + i], held_ref.at[i], sems.at[i]) for i in range(held_ref.shape[0])]
    for copy in copies:
        copy.start()

    def block(i):
        copies[i - first].wait()
        return held_ref[i - first]

    return block


def dipole_kernel(
    idx_ref, pattern_hbm, blocks_hbm, mine_ref, left_ref, right_ref, out_ref,
    pattern_ref, states_ref, sums_ref, sem, held_ref, sems,
):
    block = fetched(blocks_hbm, 0, held_ref, sems)
    add_blocks(idx_ref, pattern_hbm, block, mine_ref, left_ref, right_ref, out_ref, pattern_ref, states_ref, sums_ref, sem)


def pack_kernel(idx_ref, dipole_ref, surf_ref, cols_ref, edge_ref, w_ref, first_ref, left_ref, right_ref, message_ref, side_ref, total_ref):
    reg = idx_ref[0]
    chan = surf_ref.shape[0]
    padded = cols_ref.shape[0]
    tiles = surf_ref.shape[1] // LANES
    windows = message_ref.shape[0]
    regs = first_ref.shape[0]
    sym = wide(cols_ref[:chan, 0:1])
    received = first_ref[0]
    lane2 = lane_index((2, LANES))
    low = jnp.where(lane2 < WINDOW, received, 0.0)
    cell0 = jnp.where(lane2 < WINDOW, pltpu.roll(jnp.concatenate([received] * 4, axis=0), WINDOW, 1)[0:2], 0.0)
    cell1 = jnp.where(reg == 0, edge_ref[4 * windows : 4 * windows + 2, :], low)
    whole = jnp.zeros((2, LANES), F32)
    for source in range(regs):
        whole = whole + first_ref[source]
    whole = jnp.where((lane2 < WINDOW) & (reg == 0), whole, 0.0)
    beside = left_ref[HALO_ROWS : HALO_ROWS + 2, :] + right_ref[HALO_ROWS : HALO_ROWS + 2, :]
    side = square(
        jnp.concatenate(
            [
                cell0, cell1, beside, whole,
                left_ref[HALO_ROWS + 2 : HALO_ROWS + 4, :], right_ref[HALO_ROWS + 2 : HALO_ROWS + 4, :],
                left_ref[HALO_ROWS + 4 : HALO_ROWS + 6, :], right_ref[HALO_ROWS + 4 : HALO_ROWS + 6, :],
            ],
            axis=0,
        )
    )[:chan]
    symmetry, energy = cols_ref[:chan, 0:1], cols_ref[:chan, 1:2]
    radius = BOUNDARY_RADIUS + GRID_STEP
    potential = symmetry * (symmetry + 1.0) / (2.0 * radius * radius) + energy
    slope, start = [], []
    for part in range(2):
        here, beyond = side[:, part : part + 1], side[:, 2 + part : 3 + part]
        boundary = cols_ref[:chan, 2 + part : 3 + part] + side[:, 4 + part : 5 + part]
        slope.append(here - boundary)
        start.append(-2.0 * (beyond - 2.0 * here + boundary) + potential * here)
    lane = lane_index((chan, LANES))
    out = jnp.where((lane >= 6) & (lane < 16), side, 0.0)
    for part in range(2):
        out = jnp.where(lane == part, wide(start[part]), out)
    out = jnp.where(lane == 2, sym, out)
    out = jnp.where(lane == 3, wide(energy), out)
    side_ref[...] = jnp.concatenate([out, jnp.zeros((padded - chan, LANES), F32)], axis=0)
    total_ref[...] = dipole_ref[...]
    surface_rows(slope, surf_ref, sym, reg * tiles, tiles, total_ref)
    lines = total_ref.shape[0]
    total = total_ref[...]
    tail = jnp.concatenate([edge_ref[4 * windows + 4 : 4 * windows + 6, :], whole, jnp.zeros((6, LANES), F32)], axis=0)
    half = lane < WINDOW
    for window in range(windows):
        message_ref[window, :lines, :] = total
        one, two = (cells_of(w_ref, part, window // 2, chan) for part in range(2))
        if window % 2 == 0:
            cells = jnp.where(half, one, pltpu.roll(two, WINDOW, 1))
        else:
            cells = jnp.where(half, pltpu.roll(one, WINDOW, 1), two)
        message_ref[window, lines : lines + padded, :] = jnp.concatenate(
            [cells, jnp.zeros((padded - chan, LANES), F32)], axis=0
        )
        edges = edge_ref[4 * window : 4 * window + 4, :]
        if window == 0:
            edges = jnp.concatenate([left_ref[HALO_ROWS + 3 : HALO_ROWS + 4, :], left_ref[HALO_ROWS + 5 : HALO_ROWS + 6, :], edges[2:4]], axis=0)
        if window == windows - 1:
            edges = jnp.concatenate([edges[0:2], right_ref[HALO_ROWS + 2 : HALO_ROWS + 3, :], right_ref[HALO_ROWS + 4 : HALO_ROWS + 5, :]], axis=0)
        message_ref[window, lines + padded :, :] = jnp.concatenate([edges, cell0, tail], axis=0)


def update_kernel(idx_ref, received_ref, u_ref, energy_ref, surf_ref, cols_ref, out_ref, left_ref, right_ref):
    reg = idx_ref[0]
    lines = u_ref.shape[0]
    tiles = lines // 2
    chan = surf_ref.shape[0]
    image = energy_ref[...] * u_ref[...]
    for source in range(received_ref.shape[0]):
        image = image + received_ref[source, :lines, :]
    out_ref[...] = FIRST * turn_rows(image)
    sym = wide(cols_ref[:chan, 0:1])
    partial = boundary_sum(
        lambda tile, part: out_ref[2 * tile + part : 2 * tile + part + 1, :], surf_ref, sym, reg * tiles, tiles
    )
    lane = lane_index((chan, LANES))
    cols = jnp.where(lane == 0, wide(partial[0]), 0.0)
    cols = jnp.where(lane == 1, wide(partial[1]), cols)
    rows = jnp.concatenate([cols, jnp.zeros((LANES - chan, LANES), F32)], axis=0).T[0:8, :]
    left_ref[:HALO_ROWS, :] = out_ref[:HALO_ROWS, :]
    left_ref[HALO_ROWS:, :] = rows
    right_ref[:HALO_ROWS, :] = out_ref[lines - HALO_ROWS :, :]
    right_ref[HALO_ROWS:, :] = rows


def stencil(cells, lows, highs, potential, seams):
    count = cells.shape[1]
    lane = lane_index(cells.shape)
    below, above = pltpu.roll(cells, 1, 1), pltpu.roll(cells, count - 1, 1)
    for (first, last), low, high in zip(seams, lows, highs):
        below = jnp.where(lane == first, low, below)
        above = jnp.where(lane == last, high, above)
    return -2.0 * (above - 2.0 * cells + below) + potential * cells


def outer_kernel(count, idx_ref, received_ref, mats_ref, blocks_hbm, cross_ref, start_ref, near_ref, edge_ref, sem):
    copy = pltpu.make_async_copy(blocks_hbm.at[: near_ref.shape[0]], near_ref, sem)
    copy.start()
    reg, ch = idx_ref[0], idx_ref[1]
    groups, padded = cross_ref.shape[0], cross_ref.shape[1]
    rows = groups * padded
    lines = received_ref.shape[1] - padded - 16
    cells = received_ref[:, lines : lines + padded, :].reshape(rows, LANES)
    flipped = received_ref[:, lines + padded :, :].reshape(groups * 16, LANES).T
    extra = jnp.concatenate(
        [pltpu.roll(flipped[:padded], (LANES - 16 * group) % LANES, 1) for group in range(groups)], axis=0
    )
    first_point = reg * count + ch * WINDOW
    lane = lane_index((1, LANES))
    point = (first_point + lane % WINDOW + 1).astype(F32)
    radius = BOUNDARY_RADIUS + GRID_STEP * point
    extra_point = jnp.where(lane < 2, first_point, jnp.where(lane < 4, first_point + WINDOW + 1, 1)).astype(F32)
    extra_ratio = BOUNDARY_RADIUS / (BOUNDARY_RADIUS + GRID_STEP * extra_point)
    ratio = BOUNDARY_RADIUS / radius

    def mix(states, scale):
        totals = jnp.dot(mats_ref[...], states.astype(jnp.bfloat16), preferred_element_type=F32)
        mixed = totals[:rows] + scale * totals[rows : 2 * rows] + scale * scale * totals[2 * rows :]
        return mixed.astype(jnp.bfloat16).astype(F32)

    symmetry, energy = extra[:, 6:7], extra[:, 7:8]
    potential = symmetry * (symmetry + 1.0) / (2.0 * radius * radius) + energy
    mixed = mix(jnp.concatenate([cells, extra], axis=1), jnp.concatenate([ratio, extra_ratio], axis=1))
    main, beside = mixed[:, :LANES], mixed[:, LANES:]
    edge_ref[...] = beside
    start_ref[...] = edge_ref[pl.ds(pl.multiple_of(ch * padded, 8), padded), :]
    inner_end = (reg == 0) & (ch == 0)
    seams = ((0, WINDOW - 1), (WINDOW, 2 * WINDOW - 1))
    lows = [jnp.where(inner_end, extra[:, 8 + part : 9 + part], extra[:, part : part + 1]) for part in range(2)]
    highs = [extra[:, 2 + part : 3 + part] for part in range(2)]
    first = FIRST * turn_lanes(stencil(cells, lows, highs, potential, seams) + main)
    later = mix(first, ratio)
    cross = FIRST * turn_lanes(main)
    mixed_lows = [jnp.where(inner_end, 0.0, beside[:, part : part + 1]) for part in range(2)]
    mixed_highs = [beside[:, 2 + part : 3 + part] for part in range(2)]
    lows = [FIRST * mixed_lows[1], -FIRST * mixed_lows[0]]
    highs = [FIRST * mixed_highs[1], -FIRST * mixed_highs[0]]
    cross = cross + SECOND * turn_lanes(stencil(cross, lows, highs, potential, seams) + later)
    cross_ref[...] = cross.reshape(groups, padded, LANES)
    copy.wait()


def plain_part(regs, reg, w_ref, side_ref, plain_ref):
    chan, count = plain_ref.shape[1], plain_ref.shape[2]
    side = side_ref[...][:chan]
    symmetry, energy = side[:, 2:3], side[:, 3:4]
    lane = lane_index((1, count))
    radius = BOUNDARY_RADIUS + GRID_STEP * (reg * count + lane + 1).astype(F32)
    potential = symmetry * (symmetry + 1.0) / (2.0 * radius * radius) + energy

    def potential_at(index):
        there = BOUNDARY_RADIUS + GRID_STEP * (reg * count + index + 1).astype(F32)
        return symmetry * (symmetry + 1.0) / (2.0 * there * there) + energy

    last = reg == regs - 1
    images, lows, highs = [], [], []
    values_of = [
        jnp.concatenate([cells_of(w_ref, part, piece, chan) for piece in range(count // LANES)], axis=1) for part in range(2)
    ]
    for part in range(2):
        values = values_of[part]
        at = 8 + 4 * part
        low2, low1, high1, high2 = (side[:, at + i : at + i + 1] for i in range(4))
        low = jnp.where(reg == 0, side[:, 6 + part : 7 + part], low1)
        images.append(stencil(values, [low], [high1], potential, ((0, count - 1),)))
        under = -2.0 * (values[:, 0:1] - 2.0 * low1 + low2) + potential_at(jnp.int32(-1)) * low1
        over = -2.0 * (high2 - 2.0 * high1 + values[:, count - 1 : count]) + potential_at(jnp.int32(count)) * high1
        lows.append(jnp.where(reg == 0, 0.0, under))
        highs.append(jnp.where(last, 0.0, over))
    turned = [FIRST * images[1], -FIRST * images[0]]
    lows = [FIRST * lows[1], -FIRST * lows[0]]
    highs = [FIRST * highs[1], -FIRST * highs[0]]
    again = [stencil(turned[p], [lows[p]], [highs[p]], potential, ((0, count - 1),)) for p in range(2)]
    plain_ref[0] = values_of[0] + turned[0] + SECOND * again[1]
    plain_ref[1] = values_of[1] + turned[1] - SECOND * again[0]


def second_kernel(
    idx_ref, pattern_hbm, near_ref, blocks_hbm, mine_ref, left_ref, right_ref, own_ref, surf_ref, side_ref, start_ref, cross_ref,
    message_ref, pattern_ref, states_ref, sums_ref, sem, held_ref, sems, total_ref,
):
    near = near_ref.shape[0]
    rest = fetched(blocks_hbm, near, held_ref, sems)
    block = lambda i: near_ref[i] if i < near else rest(i)
    add_blocks(idx_ref, pattern_hbm, block, mine_ref, left_ref, right_ref, total_ref, pattern_ref, states_ref, sums_ref, sem)
    reg = idx_ref[0]
    chan = surf_ref.shape[0]
    tiles = surf_ref.shape[1] // LANES
    ends = own_ref[HALO_ROWS:, :] + left_ref[HALO_ROWS:, :] + right_ref[HALO_ROWS:, :]
    boundary = square(ends)[:chan]
    mixed = start_ref[:chan, :]
    side = side_ref[:chan, :]
    image = [side[:, part : part + 1] + mixed[:, 4 + part : 5 + part] for part in range(2)]
    slope = [FIRST * image[1] - boundary[:, 0:1], -FIRST * image[0] - boundary[:, 1:2]]
    surface_rows(slope, surf_ref, wide(side[:, 2:3]), reg * tiles, tiles, total_ref)
    lines = total_ref.shape[0]
    for group in range(message_ref.shape[0]):
        message_ref[group, :lines, :] = total_ref[...]
        message_ref[group, lines:, :] = cross_ref[group]


def finish_kernel(idx_ref, received_ref, u_ref, first_ref, energy_ref, plain_ref, ends_ref, inner_ref, outer_ref, total_ref):
    reg = idx_ref[0]
    lines = u_ref.shape[0]
    chan = plain_ref.shape[1]
    image = energy_ref[...] * first_ref[...]
    sources = received_ref.shape[0]
    for source in range(sources):
        image = image + received_ref[source, :lines, :]
    total = u_ref[...] + first_ref[...] + SECOND * turn_rows(image)
    total_ref[...] = total
    for tile in range(lines // 2):
        inner_ref[:, LANES * tile : LANES * (tile + 1)] = total_ref[2 * tile : 2 * tile + 2, :]
    columns = square(ends_ref[...])[:chan]
    lane = lane_index((chan, LANES))
    half = lane < WINDOW
    for piece in range(sources // 2):
        even = received_ref[2 * piece, lines : lines + chan, :]
        odd = received_ref[2 * piece + 1, lines : lines + chan, :]
        one = jnp.where(half, even, pltpu.roll(odd, WINDOW, 1))
        two = jnp.where(half, pltpu.roll(even, WINDOW, 1), odd)
        at = slice(LANES * piece, LANES * (piece + 1))
        one = plain_ref[0, :, at] + one
        two = plain_ref[1, :, at] + two
        if piece == 0:
            here = (lane == 0) & (reg == 0)
            one = one + jnp.where(here, -2.0 * SECOND * columns[:, 1:2], 0.0)
            two = two + jnp.where(here, 2.0 * SECOND * columns[:, 0:1], 0.0)
        for part, cells in enumerate((one, two)):
            outer_ref[pl.ds(2 * piece + part, chan, stride=sources), :] = cells


def aside_kernel(regs, idx_ref, table_ref, w_ref, side_ref, mats_ref, plain_ref):
    plain_part(regs, idx_ref[0], w_ref, side_ref, plain_ref)
    build_mats(table_ref, mats_ref)


def build_mats(table_ref, mats_ref):
    rows = mats_ref.shape[0] // NLAM
    span = table_ref.shape[1]
    entries = table_ref.shape[0] // 4
    for first in range(0, rows, LANES):
        count = min(LANES, rows - first)
        columns = square(table_ref[:, first : first + LANES])[:count]
        here = lane_index((count, span)).astype(F32)
        sums = [jnp.zeros((count, span), F32) for _ in range(NLAM)]
        for entry in range(entries):
            hit = columns[:, entry : entry + 1] == here
            order = columns[:, entries + entry : entries + entry + 1]
            weight = columns[:, 2 * entries + entry : 2 * entries + entry + 1]
            for level in range(NLAM):
                picked = jnp.where(order == level, weight, 0.0)
                sums[level] = sums[level] + jnp.where(hit, picked, 0.0)
        for level in range(NLAM):
            at = level * rows + first
            mats_ref[at : at + count, :] = sums[level][:, :rows].astype(jnp.bfloat16)


def coupling_table(source, order_list, weight, groups, chan, padded):
    place = (source // chan) * padded + source % chan
    rows = jnp.concatenate([place.T.astype(F32), order_list.T.astype(F32), weight.T, jnp.zeros_like(weight.T)], axis=0)
    rows = rows.reshape(rows.shape[0], groups, chan)
    rows = jnp.pad(rows, ((0, 0), (0, 0), (0, padded - chan))).reshape(rows.shape[0], groups * padded)
    return jnp.pad(rows, ((0, 0), (0, -rows.shape[1] % LANES)))


def shape_of(*shape):
    return jax.ShapeDtypeStruct(shape, F32)


def local(
    inner_state, energy, blocks, pattern, surface, channel_symmetry, outer_state, channel_energy,
    couple_source, couple_order, couple_weight, *, regs, groups,
):
    tile_len = inner_state.shape[1]
    lines = 2 * tile_len // LANES
    block_len = blocks.shape[1]
    block_rows = tile_len // block_len
    chan = outer_state.shape[1]
    count = outer_state.shape[2]
    padded = -(-chan // 8) * 8
    idx = jnp.stack([lax.axis_index("reg"), lax.axis_index("ch")]).astype(jnp.int32)
    smem = pl.BlockSpec(memory_space=pltpu.SMEM)
    vmem = pl.BlockSpec(memory_space=pltpu.VMEM)
    hbm = pl.BlockSpec(memory_space=pltpu.HBM)
    far = lambda array: pltpu.with_memory_space_constraint(array, pltpu.HBM)
    halo = HALO_ROWS + 8
    pieces = count // LANES
    cells = outer_state.reshape(2, chan, pieces, LANES).transpose(1, 2, 0, 3).reshape(2 * chan * pieces, LANES)
    near = blocks.shape[0] * 5 // 8
    places = far(pattern.T)

    first_msg, left, right, rows, cols, edges, energy_rows = pl.pallas_call(
        start_kernel,
        out_shape=(
            shape_of(regs, 2, LANES), shape_of(halo, LANES), shape_of(halo, LANES), shape_of(lines, LANES),
            shape_of(padded, LANES), shape_of(4 * groups + 8, LANES), shape_of(lines, LANES),
        ),
        in_specs=[smem] + [hbm] * 6,
        out_specs=(vmem,) * 7,
        scratch_shapes=[
            pltpu.VMEM((2, count, LANES), F32), pltpu.VMEM((2, tile_len), F32), pltpu.VMEM((chan, tile_len), F32),
            pltpu.VMEM(cells.shape, F32), pltpu.VMEM((lines // 2, LANES), F32),
            pltpu.VMEM((1, chan), jnp.int32), pltpu.VMEM((1, chan), F32), pltpu.SemaphoreType.DMA((6,)),
        ],
        compiler_params=params(8),
        name="start",
    )(idx, far(inner_state), far(surface), far(cells), far(energy.reshape(lines // 2, LANES)),
      far(channel_symmetry.reshape(1, chan)), far(channel_energy.reshape(1, chan)))

    firsts = lax.all_to_all(first_msg, "reg", 0, 0)
    up = [(i, i + 1) for i in range(regs - 1)]
    down = [(i + 1, i) for i in range(regs - 1)]
    from_left = lax.ppermute(right, "reg", up)
    from_right = lax.ppermute(left, "reg", down)
    block_scratch = [
        pltpu.SMEM(places.shape, jnp.int32),
        pltpu.VMEM((2 * HALO_BLOCKS + block_rows, 8, LANES), F32),
        pltpu.VMEM((block_rows, 8, block_len), F32),
        pltpu.SemaphoreType.DMA,
    ]
    held = lambda blocks: [pltpu.VMEM((blocks, block_len, block_len), F32), pltpu.SemaphoreType.DMA((blocks,))]
    dipole = pl.pallas_call(
        dipole_kernel,
        out_shape=shape_of(lines, LANES),
        in_specs=[smem, hbm, hbm] + [vmem] * 3,
        out_specs=vmem,
        scratch_shapes=block_scratch + held(blocks.shape[0]),
        compiler_params=params(16),
        name="dipole",
    )(idx, places, far(blocks), rows, from_left, from_right)

    message, side = pl.pallas_call(
        pack_kernel,
        out_shape=(shape_of(groups, lines + padded + 16, LANES), shape_of(padded, LANES)),
        in_specs=[smem] + [vmem] * 8,
        out_specs=(vmem,) * 2,
        scratch_shapes=[pltpu.VMEM((lines, LANES), F32)],
        compiler_params=params(8),
        name="pack",
    )(idx, dipole, surface, cols, edges, cells, firsts, from_left, from_right)
    received = lax.all_to_all(message, "ch", 0, 0)

    table = coupling_table(couple_source, couple_order, couple_weight, groups, chan, padded)
    mats, plain = pl.pallas_call(
        functools.partial(aside_kernel, regs),
        out_shape=(
            jax.ShapeDtypeStruct((NLAM * groups * padded, groups * padded), jnp.bfloat16), shape_of(2, chan, count),
        ),
        in_specs=[smem] + [vmem] * 3,
        out_specs=(vmem,) * 2,
        compiler_params=params(8),
        name="aside",
    )(idx, table, cells, side)
    received, mats = lax.optimization_barrier((received, mats))

    first, left, right = pl.pallas_call(
        update_kernel,
        out_shape=(shape_of(lines, LANES), shape_of(halo, LANES), shape_of(halo, LANES)),
        in_specs=[smem] + [vmem] * 5,
        out_specs=(vmem,) * 3,
        compiler_params=params(8),
        name="update",
    )(idx, received, rows, energy_rows, surface, cols)
    from_left = lax.ppermute(right, "reg", up)
    from_right = lax.ppermute(left, "reg", down)

    cross, start, near_blocks = pl.pallas_call(
        functools.partial(outer_kernel, count),
        out_shape=(shape_of(groups, padded, LANES), shape_of(padded, LANES), shape_of(near, block_len, block_len)),
        in_specs=[smem] + [vmem] * 2 + [hbm],
        out_specs=(vmem,) * 3,
        scratch_shapes=[pltpu.VMEM((groups * padded, LANES), F32), pltpu.SemaphoreType.DMA],
        compiler_params=params(12),
        name="outer",
    )(idx, received, mats, far(blocks))

    ends = left[HALO_ROWS:] + from_right[HALO_ROWS:]
    steps = [1 << i for i in range(1, regs.bit_length() - 1)]

    def gather_ends(ends, step):
        pairs = [(i + step, i) for i in range(0, regs, 2 * step)]
        return ends + lax.ppermute(ends, "reg", pairs)

    ends = gather_ends(ends, steps[0])
    cross, ends = lax.optimization_barrier((cross, ends))
    ends = gather_ends(ends, steps[1])
    message = pl.pallas_call(
        second_kernel,
        out_shape=shape_of(groups, lines + padded, LANES),
        in_specs=[smem, hbm, vmem, hbm] + [vmem] * 8,
        out_specs=vmem,
        scratch_shapes=block_scratch + held(blocks.shape[0] - near) + [pltpu.VMEM((lines, LANES), F32)],
        compiler_params=params(16),
        name="second",
    )(idx, places, near_blocks, far(blocks), first, from_left, from_right, left, surface, side, start, cross)
    message, ends = lax.optimization_barrier((message, ends))
    received = lax.all_to_all(message, "ch", 0, 0)
    for step in steps[2:]:
        ends = gather_ends(ends, step)

    inner, outer = pl.pallas_call(
        finish_kernel,
        out_shape=(shape_of(2, tile_len), shape_of(*cells.shape)),
        in_specs=[smem] + [vmem] * 6,
        out_specs=(vmem,) * 2,
        scratch_shapes=[pltpu.VMEM((lines, LANES), F32)],
        compiler_params=params(8),
        name="finish",
    )(idx, received, rows, first, energy_rows, plain, ends)
    return inner, outer.reshape(chan, pieces, 2, LANES).transpose(2, 0, 1, 3).reshape(2, chan, count)


def solution(mesh):
    return jax.shard_map(
        functools.partial(local, regs=mesh.shape["reg"], groups=mesh.shape["ch"]),
        mesh=mesh,
        in_specs=(
            P(None, "reg"),
            P("reg"),
            P(("reg", "ch"), None, None),
            P(("reg", "ch"), None),
            P("ch", "reg"),
            P("ch"),
            P(None, "ch", "reg"),
            P("ch"),
            P(),
            P(),
            P(),
        ),
        out_specs=(P(None, "reg"), P(None, "ch", "reg")),
        check_vma=False,
    )
```

```python
import functools

import jax
import jax.numpy as jnp
from jax import lax
from jax.experimental import pallas as pl
from jax.experimental.pallas import tpu as pltpu
from jax.sharding import PartitionSpec as P

BLOCKS_PER_SYMM = 4
NLAM = 3
TIME_STEP = 0.05
GRID_STEP = 0.5
BOUNDARY_RADIUS = 20.0
FIRST = TIME_STEP
SECOND = TIME_STEP / 2
LANES = 128
HALO_BLOCKS = 7
HALO_ROWS = 8 * HALO_BLOCKS
WINDOW = 64
F32 = jnp.float32
NT = (((1,), (1,)), ((), ()))


def params(megabytes):
    return pltpu.CompilerParams(vmem_limit_bytes=megabytes * 2**20)


def lane_index(shape):
    return lax.broadcasted_iota(jnp.int32, shape, len(shape) - 1)


def row_index(shape):
    return lax.broadcasted_iota(jnp.int32, shape, len(shape) - 2)


def square(rows):
    count = rows.shape[0]
    if count < LANES:
        rows = jnp.concatenate([rows, jnp.zeros((LANES - count, LANES), F32)], axis=0)
    return rows.T


def wide(column):
    return jnp.broadcast_to(column, (column.shape[0], LANES))


def cells_of(w_ref, part, piece, chan):
    pieces = w_ref.shape[0] // (2 * chan)
    return w_ref[pl.ds(2 * piece + part, chan, stride=2 * pieces), :]


def boundary_sum(vec_rows, surf_ref, sym, first_tile, tiles):
    chan = surf_ref.shape[0]
    sums = [jnp.zeros((chan, LANES), F32) for _ in range(2)]
    for tile in range(tiles):
        here = ((first_tile + tile) // 16).astype(F32)
        values = jnp.where(sym == here, surf_ref[:, LANES * tile : LANES * (tile + 1)], 0.0)
        for part in range(2):
            sums[part] = sums[part] + values * vec_rows(tile, part)
    return [jnp.sum(total, axis=1, keepdims=True) for total in sums]


def surface_rows(slope, surf_ref, sym, first_tile, tiles, out_ref):
    columns = [wide(column) for column in slope]
    for tile in range(tiles):
        here = ((first_tile + tile) // 16).astype(F32)
        values = jnp.where(sym == here, surf_ref[:, LANES * tile : LANES * (tile + 1)], 0.0)
        rows = [jnp.sum(values * columns[part], axis=0, keepdims=True) for part in range(2)]
        at = slice(2 * tile, 2 * tile + 2)
        out_ref[at, :] = out_ref[at, :] + jnp.concatenate(rows, axis=0)


def turn_rows(rows):
    count = rows.shape[0]
    even = row_index(rows.shape) % 2 == 0
    return jnp.where(even, pltpu.roll(rows, count - 1, 0), -pltpu.roll(rows, 1, 0))


def turn_lanes(cells):
    other = pltpu.roll(cells, WINDOW, 1)
    return jnp.where(lane_index(cells.shape) < WINDOW, other, -other)


def sort_sides(reg, pair_ref, next_ref, left_ref, right_ref):
    odd = reg % 2 == 1
    left_ref[...] = jnp.where(odd, pair_ref[...], next_ref[...])
    right_ref[...] = jnp.where(odd, next_ref[...], pair_ref[...])


def start_kernel(
    idx_ref, pattern_hbm, u_hbm, surf_hbm, w_hbm, energy_hbm, sym_hbm, level_hbm,
    first_ref, pair_ref, next_ref, rows_ref, cols_ref, edge_ref, doubled_ref, ints_ref,
    left_ref, right_ref, wt_ref, u_ref, surf_ref, w_ref, energy_ref, sym_ref, level_ref, pattern_ref, sems,
):
    copies = [
        pltpu.make_async_copy(source, target, sems.at[i])
        for i, (source, target) in enumerate(
            [
                (sym_hbm, sym_ref), (level_hbm, level_ref), (w_hbm, w_ref), (energy_hbm, energy_ref), (u_hbm, u_ref),
                (surf_hbm, surf_ref), (pattern_hbm, pattern_ref),
            ]
        )
    ]
    for copy in copies:
        copy.start()
    reg = idx_ref[0]
    tiles = u_ref.shape[1] // LANES
    chan = surf_ref.shape[0]
    copies[0].wait()
    copies[1].wait()
    head = jnp.zeros((1, LANES - chan), F32)
    sym_row = jnp.concatenate([sym_ref[...].astype(F32), head], axis=1)
    energy_row = jnp.concatenate([level_ref[...], head], axis=1)
    base = square(jnp.concatenate([sym_row, energy_row], axis=0))
    sym = wide(base[:chan, 0:1])
    copies[2].wait()
    for part in range(2):
        for piece in range(wt_ref.shape[1] // LANES):
            cells = cells_of(w_ref, part, piece, chan)
            cells = jnp.concatenate([cells, jnp.zeros((LANES - chan, LANES), F32)], axis=0)
            wt_ref[part, LANES * piece : LANES * (piece + 1), :] = cells.T
    copies[3].wait()
    for tile in range(tiles):
        doubled_ref[2 * tile : 2 * tile + 2, :] = jnp.broadcast_to(energy_ref[tile : tile + 1, :], (2, LANES))
    copies[4].wait()
    for tile in range(tiles):
        rows_ref[2 * tile : 2 * tile + 2, :] = u_ref[:, LANES * tile : LANES * (tile + 1)]
    copies[5].wait()
    partial = boundary_sum(
        lambda tile, part: u_ref[part : part + 1, LANES * tile : LANES * (tile + 1)],
        surf_ref, sym, reg * tiles, tiles,
    )
    lane = lane_index((chan, LANES))
    cols = jnp.where(lane == 0, sym, 0.0)
    cols = jnp.where(lane == 1, wide(base[:chan, 1:2]), cols)
    for part in range(2):
        cols = jnp.where(lane == 2 + part, wide(partial[part]), cols)
    cols = jnp.concatenate([cols, jnp.zeros((cols_ref.shape[0] - chan, LANES), F32)], axis=0)
    cols_ref[...] = cols
    back = jnp.concatenate([cols, jnp.zeros((LANES - cols.shape[0], LANES), F32)], axis=0).T
    partial_rows = back[2:4, :]
    count = wt_ref.shape[1]
    spot = lambda part, point: wt_ref[part, point : point + 1, :]
    zeros = jnp.zeros((2, LANES), F32)
    left_ref[:HALO_ROWS, :] = rows_ref[:HALO_ROWS, :]
    left_ref[HALO_ROWS:, :] = jnp.concatenate([partial_rows, spot(0, 0), spot(0, 1), spot(1, 0), spot(1, 1), zeros], axis=0)
    right_ref[:HALO_ROWS, :] = rows_ref[2 * tiles - HALO_ROWS :, :]
    right_ref[HALO_ROWS:, :] = jnp.concatenate(
        [partial_rows, spot(0, count - 2), spot(0, count - 1), spot(1, count - 2), spot(1, count - 1), zeros], axis=0
    )
    sort_sides(reg, left_ref, right_ref, pair_ref, next_ref)
    cell0 = jnp.concatenate([spot(0, 0), spot(1, 0)], axis=0)
    cell1 = jnp.concatenate([spot(0, 1), spot(1, 1)], axis=0)
    shifted = pltpu.roll(jnp.concatenate([cell0] * 4, axis=0), WINDOW, 1)[0:2]
    first_ref[0] = partial_rows + shifted
    others = first_ref.shape[0] - 1
    first_ref[1:] = jnp.broadcast_to((cell1 + shifted)[None], (others, 2, LANES))
    windows = count // WINDOW
    zero = jnp.zeros((1, LANES), F32)
    for window in range(windows):
        low, high = WINDOW * window - 1, WINDOW * (window + 1)
        edge_ref[4 * window : 4 * window + 4, :] = jnp.concatenate(
            [
                spot(0, low) if window else zero,
                spot(1, low) if window else zero,
                spot(0, high) if window < windows - 1 else zero,
                spot(1, high) if window < windows - 1 else zero,
            ],
            axis=0,
        )
    edge_ref[4 * windows : 4 * windows + 8, :] = jnp.concatenate([cell1, cell0, sym_row, energy_row, zeros], axis=0)
    copies[6].wait()
    ints_ref[0], ints_ref[1] = idx_ref[0], idx_ref[1]
    held = pattern_ref.shape[1]
    for i in range(held):
        ints_ref[2 + i] = pattern_ref[0, i]
        ints_ref[2 + held + i] = pattern_ref[1, i]


def add_blocks(ints_ref, count, blocks, mine_ref, left_ref, right_ref, out_ref, states_ref, sums_ref):
    block_len = sums_ref.shape[2]
    rows = mine_ref.shape[0] // 8
    pieces = block_len // LANES
    for column in range(HALO_BLOCKS):
        states_ref[column] = left_ref[8 * column : 8 * column + 8, :]
        states_ref[HALO_BLOCKS + rows + column] = right_ref[8 * column : 8 * column + 8, :]
    for column in range(rows):
        states_ref[HALO_BLOCKS + column] = mine_ref[8 * column : 8 * column + 8, :]
    sums_ref[...] = jnp.zeros(sums_ref.shape, F32)
    for i in range(count):
        row = jnp.clip(ints_ref[2 + i], 0, rows - 1)
        column = jnp.clip(ints_ref[2 + count + i] - ints_ref[0] * rows + HALO_BLOCKS, 0, states_ref.shape[0] - 1)
        tile = states_ref[column]
        state = jnp.concatenate([tile[2 * piece : 2 * piece + 2, :] for piece in range(pieces)], axis=1)
        lead = state.astype(jnp.bfloat16).astype(F32)
        state = jnp.concatenate([lead, state - lead, jnp.zeros((12, block_len), F32)], axis=0).astype(jnp.bfloat16)
        block = blocks(i)
        lead = block.astype(jnp.bfloat16)
        rest = (block - lead.astype(F32)).astype(jnp.bfloat16)
        product = lax.dot_general(state, lead, NT, preferred_element_type=F32)
        product = product + lax.dot_general(state, rest, NT, preferred_element_type=F32)
        sums_ref[row] = sums_ref[row] + product[:8]
    shape = (8, LANES)
    for row in range(rows):
        total = sums_ref[row]
        total = total + pltpu.roll(total, 6, 0)
        picked = jnp.zeros(shape, F32)
        for piece in range(pieces):
            values = total[:, LANES * piece : LANES * (piece + 1)]
            values = pltpu.roll(values, 2 * piece, 0) if piece else values
            picked = jnp.where(row_index(shape) // 2 == piece, values, picked)
        out_ref[8 * row : 8 * row + 8, :] = picked


def fetched(blocks_hbm, first, held_ref, sems):
    copies = [pltpu.make_async_copy(blocks_hbm.at[first + i], held_ref.at[i], sems.at[i]) for i in range(held_ref.shape[0])]
    for copy in copies:
        copy.start()

    def block(i):
        copies[i - first].wait()
        return held_ref[i - first]

    return block


def dipole_kernel(
    ints_ref, blocks_hbm, mine_ref, pair_ref, next_ref, out_ref, left_ref, right_ref, states_ref, sums_ref, held_ref, sems
):
    sort_sides(ints_ref[0], pair_ref, next_ref, left_ref, right_ref)
    block = fetched(blocks_hbm, 0, held_ref, sems)
    add_blocks(ints_ref, held_ref.shape[0], block, mine_ref, left_ref, right_ref, out_ref, states_ref, sums_ref)


def pack_kernel(
    idx_ref, dipole_ref, surf_ref, cols_ref, edge_ref, w_ref, first_ref, pair_ref, next_ref,
    message_hbm, side_ref, left_ref, right_ref, total_ref, message_ref, sems,
):
    sort_sides(idx_ref[0], pair_ref, next_ref, left_ref, right_ref)
    reg = idx_ref[0]
    chan = surf_ref.shape[0]
    padded = cols_ref.shape[0]
    tiles = surf_ref.shape[1] // LANES
    windows = message_hbm.shape[0]
    regs = first_ref.shape[0]
    sym = wide(cols_ref[:chan, 0:1])
    received = first_ref[0]
    lane2 = lane_index((2, LANES))
    low = jnp.where(lane2 < WINDOW, received, 0.0)
    cell0 = jnp.where(lane2 < WINDOW, pltpu.roll(jnp.concatenate([received] * 4, axis=0), WINDOW, 1)[0:2], 0.0)
    cell1 = jnp.where(reg == 0, edge_ref[4 * windows : 4 * windows + 2, :], low)
    whole = jnp.zeros((2, LANES), F32)
    for source in range(regs):
        whole = whole + first_ref[source]
    whole = jnp.where((lane2 < WINDOW) & (reg == 0), whole, 0.0)
    beside = left_ref[HALO_ROWS : HALO_ROWS + 2, :] + right_ref[HALO_ROWS : HALO_ROWS + 2, :]
    side = square(
        jnp.concatenate(
            [
                cell0, cell1, beside, whole,
                left_ref[HALO_ROWS + 2 : HALO_ROWS + 4, :], right_ref[HALO_ROWS + 2 : HALO_ROWS + 4, :],
                left_ref[HALO_ROWS + 4 : HALO_ROWS + 6, :], right_ref[HALO_ROWS + 4 : HALO_ROWS + 6, :],
            ],
            axis=0,
        )
    )[:chan]
    symmetry, energy = cols_ref[:chan, 0:1], cols_ref[:chan, 1:2]
    radius = BOUNDARY_RADIUS + GRID_STEP
    potential = symmetry * (symmetry + 1.0) / (2.0 * radius * radius) + energy
    slope, start = [], []
    for part in range(2):
        here, beyond = side[:, part : part + 1], side[:, 2 + part : 3 + part]
        boundary = cols_ref[:chan, 2 + part : 3 + part] + side[:, 4 + part : 5 + part]
        slope.append(here - boundary)
        start.append(-2.0 * (beyond - 2.0 * here + boundary) + potential * here)
    lane = lane_index((chan, LANES))
    out = jnp.where((lane >= 6) & (lane < 16), side, 0.0)
    for part in range(2):
        out = jnp.where(lane == part, wide(start[part]), out)
    out = jnp.where(lane == 2, sym, out)
    out = jnp.where(lane == 3, wide(energy), out)
    side_ref[...] = jnp.concatenate([out, jnp.zeros((padded - chan, LANES), F32)], axis=0)
    tail = jnp.concatenate([edge_ref[4 * windows + 4 : 4 * windows + 6, :], whole, jnp.zeros((6, LANES), F32)], axis=0)
    half = lane < WINDOW
    for window in range(windows):
        one, two = (cells_of(w_ref, part, window // 2, chan) for part in range(2))
        if window % 2 == 0:
            cells = jnp.where(half, one, pltpu.roll(two, WINDOW, 1))
        else:
            cells = jnp.where(half, pltpu.roll(one, WINDOW, 1), two)
        message_ref[window, :padded, :] = jnp.concatenate(
            [cells, jnp.zeros((padded - chan, LANES), F32)], axis=0
        )
        edges = edge_ref[4 * window : 4 * window + 4, :]
        if window == 0:
            edges = jnp.concatenate([left_ref[HALO_ROWS + 3 : HALO_ROWS + 4, :], left_ref[HALO_ROWS + 5 : HALO_ROWS + 6, :], edges[2:4]], axis=0)
        if window == windows - 1:
            edges = jnp.concatenate([edges[0:2], right_ref[HALO_ROWS + 2 : HALO_ROWS + 3, :], right_ref[HALO_ROWS + 4 : HALO_ROWS + 5, :]], axis=0)
        message_ref[window, padded:, :] = jnp.concatenate([edges, cell0, tail], axis=0)
    lines = total_ref.shape[0]
    outer_copy = pltpu.make_async_copy(message_ref, message_hbm.at[:, lines:], sems.at[windows])
    outer_copy.start()
    total_ref[...] = dipole_ref[...]
    surface_rows(slope, surf_ref, sym, reg * tiles, tiles, total_ref)
    copies = [pltpu.make_async_copy(total_ref, message_hbm.at[window, :lines], sems.at[window]) for window in range(windows)]
    for copy in copies:
        copy.start()
    for copy in copies + [outer_copy]:
        copy.wait()


def update_kernel(
    idx_ref, received_ref, u_ref, energy_ref, surf_ref, cols_ref, out_ref, pair_ref, next_ref, left_ref, right_ref
):
    reg = idx_ref[0]
    lines = u_ref.shape[0]
    tiles = lines // 2
    chan = surf_ref.shape[0]
    image = energy_ref[...] * u_ref[...]
    for source in range(received_ref.shape[0]):
        image = image + received_ref[source, :lines, :]
    out_ref[...] = FIRST * turn_rows(image)
    sym = wide(cols_ref[:chan, 0:1])
    partial = boundary_sum(
        lambda tile, part: out_ref[2 * tile + part : 2 * tile + part + 1, :], surf_ref, sym, reg * tiles, tiles
    )
    lane = lane_index((chan, LANES))
    cols = jnp.where(lane == 0, wide(partial[0]), 0.0)
    cols = jnp.where(lane == 1, wide(partial[1]), cols)
    rows = jnp.concatenate([cols, jnp.zeros((LANES - chan, LANES), F32)], axis=0).T[0:8, :]
    left_ref[:HALO_ROWS, :] = out_ref[:HALO_ROWS, :]
    left_ref[HALO_ROWS:, :] = rows
    right_ref[:HALO_ROWS, :] = out_ref[lines - HALO_ROWS :, :]
    right_ref[HALO_ROWS:, :] = rows
    sort_sides(reg, left_ref, right_ref, pair_ref, next_ref)


def stencil(cells, lows, highs, potential, seams):
    count = cells.shape[1]
    lane = lane_index(cells.shape)
    below, above = pltpu.roll(cells, 1, 1), pltpu.roll(cells, count - 1, 1)
    for (first, last), low, high in zip(seams, lows, highs):
        below = jnp.where(lane == first, low, below)
        above = jnp.where(lane == last, high, above)
    return -2.0 * (above - 2.0 * cells + below) + potential * cells


def mats_of(mats_hbm, mats_ref, sems):
    rows = mats_ref.shape[0] // NLAM
    spans = [pl.ds(level * rows, rows) for level in range(NLAM)]
    copies = [pltpu.make_async_copy(mats_hbm.at[span], mats_ref.at[span], sems.at[i]) for i, span in enumerate(spans)]
    for copy in copies:
        copy.start()
    waiting = set(range(NLAM))

    def mats(level):
        if level in waiting:
            waiting.discard(level)
            copies[level].wait()
        return mats_ref[spans[level], :]

    return mats


def outer_kernel(count, idx_ref, received_ref, mats_hbm, blocks_hbm, cross_ref, start_ref, near_ref, edge_ref, mats_ref, sems, sem):
    mats = mats_of(mats_hbm, mats_ref, sems)
    copy = pltpu.make_async_copy(blocks_hbm.at[: near_ref.shape[0]], near_ref, sem)
    copy.start()
    reg, ch = idx_ref[0], idx_ref[1]
    groups, padded = cross_ref.shape[0], cross_ref.shape[1]
    rows = groups * padded
    lines = received_ref.shape[1] - padded - 16
    cells = received_ref[:, lines : lines + padded, :].reshape(rows, LANES)
    flipped = received_ref[:, lines + padded :, :].reshape(groups * 16, LANES).T
    extra = jnp.concatenate(
        [pltpu.roll(flipped[:padded], (LANES - 16 * group) % LANES, 1) for group in range(groups)], axis=0
    )
    first_point = reg * count + ch * WINDOW
    lane = lane_index((1, LANES))
    point = (first_point + lane % WINDOW + 1).astype(F32)
    radius = BOUNDARY_RADIUS + GRID_STEP * point
    extra_point = jnp.where(lane < 2, first_point, jnp.where(lane < 4, first_point + WINDOW + 1, 1)).astype(F32)
    extra_ratio = BOUNDARY_RADIUS / (BOUNDARY_RADIUS + GRID_STEP * extra_point)
    ratio = BOUNDARY_RADIUS / radius

    def mix(states, scale):
        states = states.astype(jnp.bfloat16)
        mixed, power = 0.0, 1.0
        for level in range(NLAM):
            mixed = mixed + power * jnp.dot(mats(level), states, preferred_element_type=F32)
            power = power * scale
        return mixed.astype(jnp.bfloat16).astype(F32)

    symmetry, energy = extra[:, 6:7], extra[:, 7:8]
    potential = symmetry * (symmetry + 1.0) / (2.0 * radius * radius) + energy
    mixed = mix(jnp.concatenate([cells, extra], axis=1), jnp.concatenate([ratio, extra_ratio], axis=1))
    main, beside = mixed[:, :LANES], mixed[:, LANES:]
    edge_ref[...] = beside
    start_ref[...] = edge_ref[pl.ds(pl.multiple_of(ch * padded, 8), padded), :]
    inner_end = (reg == 0) & (ch == 0)
    seams = ((0, WINDOW - 1), (WINDOW, 2 * WINDOW - 1))
    lows = [jnp.where(inner_end, extra[:, 8 + part : 9 + part], extra[:, part : part + 1]) for part in range(2)]
    highs = [extra[:, 2 + part : 3 + part] for part in range(2)]
    first = FIRST * turn_lanes(stencil(cells, lows, highs, potential, seams) + main)
    later = mix(first, ratio)
    cross = FIRST * turn_lanes(main)
    mixed_lows = [jnp.where(inner_end, 0.0, beside[:, part : part + 1]) for part in range(2)]
    mixed_highs = [beside[:, 2 + part : 3 + part] for part in range(2)]
    lows = [FIRST * mixed_lows[1], -FIRST * mixed_lows[0]]
    highs = [FIRST * mixed_highs[1], -FIRST * mixed_highs[0]]
    cross = cross + SECOND * turn_lanes(stencil(cross, lows, highs, potential, seams) + later)
    cross_ref[...] = cross.reshape(groups, padded, LANES)
    copy.wait()


def plain_part(regs, reg, w_ref, side_ref, plain_ref):
    chan, count = plain_ref.shape[1], plain_ref.shape[2]
    side = side_ref[...][:chan]
    symmetry, energy = side[:, 2:3], side[:, 3:4]
    lane = lane_index((1, count))
    radius = BOUNDARY_RADIUS + GRID_STEP * (reg * count + lane + 1).astype(F32)
    potential = symmetry * (symmetry + 1.0) / (2.0 * radius * radius) + energy

    def potential_at(index):
        there = BOUNDARY_RADIUS + GRID_STEP * (reg * count + index + 1).astype(F32)
        return symmetry * (symmetry + 1.0) / (2.0 * there * there) + energy

    last = reg == regs - 1
    images, lows, highs = [], [], []
    values_of = [
        jnp.concatenate([cells_of(w_ref, part, piece, chan) for piece in range(count // LANES)], axis=1) for part in range(2)
    ]
    for part in range(2):
        values = values_of[part]
        at = 8 + 4 * part
        low2, low1, high1, high2 = (side[:, at + i : at + i + 1] for i in range(4))
        low = jnp.where(reg == 0, side[:, 6 + part : 7 + part], low1)
        images.append(stencil(values, [low], [high1], potential, ((0, count - 1),)))
        under = -2.0 * (values[:, 0:1] - 2.0 * low1 + low2) + potential_at(jnp.int32(-1)) * low1
        over = -2.0 * (high2 - 2.0 * high1 + values[:, count - 1 : count]) + potential_at(jnp.int32(count)) * high1
        lows.append(jnp.where(reg == 0, 0.0, under))
        highs.append(jnp.where(last, 0.0, over))
    turned = [FIRST * images[1], -FIRST * images[0]]
    lows = [FIRST * lows[1], -FIRST * lows[0]]
    highs = [FIRST * highs[1], -FIRST * highs[0]]
    again = [stencil(turned[p], [lows[p]], [highs[p]], potential, ((0, count - 1),)) for p in range(2)]
    plain_ref[0] = values_of[0] + turned[0] + SECOND * again[1]
    plain_ref[1] = values_of[1] + turned[1] - SECOND * again[0]


def second_kernel(
    ints_ref, near_ref, blocks_hbm, mine_ref, pair_ref, next_ref, own_ref, surf_ref, side_ref, start_ref, cross_ref,
    message_hbm, left_ref, right_ref, states_ref, sums_ref, held_ref, sems, total_ref, out_sems,
):
    sort_sides(ints_ref[0], pair_ref, next_ref, left_ref, right_ref)
    near = near_ref.shape[0]
    rest = fetched(blocks_hbm, near, held_ref, sems)
    outer_copy = pltpu.make_async_copy(cross_ref, message_hbm.at[:, total_ref.shape[0] :], out_sems.at[message_hbm.shape[0]])
    outer_copy.start()
    block = lambda i: near_ref[i] if i < near else rest(i)
    add_blocks(ints_ref, near + held_ref.shape[0], block, mine_ref, left_ref, right_ref, total_ref, states_ref, sums_ref)
    reg = ints_ref[0]
    chan = surf_ref.shape[0]
    tiles = surf_ref.shape[1] // LANES
    ends = own_ref[HALO_ROWS:, :] + left_ref[HALO_ROWS:, :] + right_ref[HALO_ROWS:, :]
    boundary = square(ends)[:chan]
    mixed = start_ref[:chan, :]
    side = side_ref[:chan, :]
    image = [side[:, part : part + 1] + mixed[:, 4 + part : 5 + part] for part in range(2)]
    slope = [FIRST * image[1] - boundary[:, 0:1], -FIRST * image[0] - boundary[:, 1:2]]
    surface_rows(slope, surf_ref, wide(side[:, 2:3]), reg * tiles, tiles, total_ref)
    lines = total_ref.shape[0]
    groups = message_hbm.shape[0]
    copies = [pltpu.make_async_copy(total_ref, message_hbm.at[group, :lines], out_sems.at[group]) for group in range(groups)]
    for copy in copies:
        copy.start()
    for copy in copies + [outer_copy]:
        copy.wait()


def finish_kernel(idx_ref, received_ref, u_ref, first_ref, energy_ref, plain_ref, ends_ref, inner_ref, outer_ref, total_ref):
    reg = idx_ref[0]
    lines = u_ref.shape[0]
    chan = plain_ref.shape[1]
    image = energy_ref[...] * first_ref[...]
    sources = received_ref.shape[0]
    for source in range(sources):
        image = image + received_ref[source, :lines, :]
    total = u_ref[...] + first_ref[...] + SECOND * turn_rows(image)
    total_ref[...] = total
    for tile in range(lines // 2):
        inner_ref[:, LANES * tile : LANES * (tile + 1)] = total_ref[2 * tile : 2 * tile + 2, :]
    columns = square(ends_ref[...])[:chan]
    lane = lane_index((chan, LANES))
    half = lane < WINDOW
    for piece in range(sources // 2):
        even = received_ref[2 * piece, lines : lines + chan, :]
        odd = received_ref[2 * piece + 1, lines : lines + chan, :]
        one = jnp.where(half, even, pltpu.roll(odd, WINDOW, 1))
        two = jnp.where(half, pltpu.roll(even, WINDOW, 1), odd)
        at = slice(LANES * piece, LANES * (piece + 1))
        one = plain_ref[0, :, at] + one
        two = plain_ref[1, :, at] + two
        if piece == 0:
            here = (lane == 0) & (reg == 0)
            one = one + jnp.where(here, -2.0 * SECOND * columns[:, 1:2], 0.0)
            two = two + jnp.where(here, 2.0 * SECOND * columns[:, 0:1], 0.0)
        for part, cells in enumerate((one, two)):
            outer_ref[pl.ds(2 * piece + part, chan, stride=sources), :] = cells


def aside_kernel(regs, idx_ref, table_ref, w_ref, side_ref, mats_ref, plain_ref):
    plain_part(regs, idx_ref[0], w_ref, side_ref, plain_ref)
    build_mats(table_ref, mats_ref)


def build_mats(table_ref, mats_ref):
    rows = mats_ref.shape[0] // NLAM
    span = table_ref.shape[1]
    entries = table_ref.shape[0] // 4
    for first in range(0, rows, LANES):
        count = min(LANES, rows - first)
        columns = square(table_ref[:, first : first + LANES])[:count]
        here = lane_index((count, span)).astype(F32)
        sums = [jnp.zeros((count, span), F32) for _ in range(NLAM)]
        for entry in range(entries):
            hit = columns[:, entry : entry + 1] == here
            order = columns[:, entries + entry : entries + entry + 1]
            weight = columns[:, 2 * entries + entry : 2 * entries + entry + 1]
            for level in range(NLAM):
                picked = jnp.where(order == level, weight, 0.0)
                sums[level] = sums[level] + jnp.where(hit, picked, 0.0)
        for level in range(NLAM):
            at = level * rows + first
            mats_ref[at : at + count, :] = sums[level][:, :rows].astype(jnp.bfloat16)


def coupling_table(source, order_list, weight, groups, chan, padded):
    place = (source // chan) * padded + source % chan
    rows = jnp.concatenate([place.T.astype(F32), order_list.T.astype(F32), weight.T, jnp.zeros_like(weight.T)], axis=0)
    rows = rows.reshape(rows.shape[0], groups, chan)
    rows = jnp.pad(rows, ((0, 0), (0, 0), (0, padded - chan))).reshape(rows.shape[0], groups * padded)
    return jnp.pad(rows, ((0, 0), (0, -rows.shape[1] % LANES)))


def shape_of(*shape):
    return jax.ShapeDtypeStruct(shape, F32)


def local(
    inner_state, energy, blocks, pattern, surface, channel_symmetry, outer_state, channel_energy,
    couple_source, couple_order, couple_weight, *, regs, groups,
):
    tile_len = inner_state.shape[1]
    lines = 2 * tile_len // LANES
    block_len = blocks.shape[1]
    block_rows = tile_len // block_len
    chan = outer_state.shape[1]
    count = outer_state.shape[2]
    padded = -(-chan // 8) * 8
    idx = jnp.stack([lax.axis_index("reg"), lax.axis_index("ch")]).astype(jnp.int32)
    smem = pl.BlockSpec(memory_space=pltpu.SMEM)
    vmem = pl.BlockSpec(memory_space=pltpu.VMEM)
    hbm = pl.BlockSpec(memory_space=pltpu.HBM)
    far = lambda array: pltpu.with_memory_space_constraint(array, pltpu.HBM)
    halo = HALO_ROWS + 8
    pieces = count // LANES
    cells = outer_state.reshape(2, chan, pieces, LANES).transpose(1, 2, 0, 3).reshape(2 * chan * pieces, LANES)
    near = blocks.shape[0] * 5 // 8

    both = [pltpu.VMEM((halo, LANES), F32)] * 2
    first_msg, pair, other, rows, cols, edges, energy_rows, ints = pl.pallas_call(
        start_kernel,
        out_shape=(
            shape_of(regs, 2, LANES), shape_of(halo, LANES), shape_of(halo, LANES), shape_of(lines, LANES),
            shape_of(padded, LANES), shape_of(4 * groups + 8, LANES), shape_of(lines, LANES),
            jax.ShapeDtypeStruct((2 + pattern.size,), jnp.int32),
        ),
        in_specs=[smem] + [hbm] * 7,
        out_specs=(vmem,) * 7 + (smem,),
        scratch_shapes=both
        + [
            pltpu.VMEM((2, count, LANES), F32), pltpu.VMEM((2, tile_len), F32), pltpu.VMEM((chan, tile_len), F32),
            pltpu.VMEM(cells.shape, F32), pltpu.VMEM((lines // 2, LANES), F32),
            pltpu.VMEM((1, chan), jnp.int32), pltpu.VMEM((1, chan), F32), pltpu.SMEM((2, blocks.shape[0]), jnp.int32),
            pltpu.SemaphoreType.DMA((7,)),
        ],
        compiler_params=params(8),
        name="start",
    )(idx, far(pattern.T), far(inner_state), far(surface), far(cells), far(energy.reshape(lines // 2, LANES)),
      far(channel_symmetry.reshape(1, chan)), far(channel_energy.reshape(1, chan)))

    firsts = lax.all_to_all(first_msg, "reg", 0, 0)
    on_chip = [(i, i ^ 1) for i in range(regs)]
    off_chip = [move for i in range(1, regs - 1, 2) for move in ((i, i + 1), (i + 1, i))]
    from_pair = lax.ppermute(pair, "reg", on_chip)
    from_other = lax.ppermute(other, "reg", off_chip)
    block_scratch = [
        pltpu.VMEM((2 * HALO_BLOCKS + block_rows, 8, LANES), F32),
        pltpu.VMEM((block_rows, 8, block_len), F32),
    ]
    held = lambda blocks: [pltpu.VMEM((blocks, block_len, block_len), F32), pltpu.SemaphoreType.DMA((blocks,))]
    dipole = pl.pallas_call(
        dipole_kernel,
        out_shape=shape_of(lines, LANES),
        in_specs=[smem, hbm] + [vmem] * 3,
        out_specs=vmem,
        scratch_shapes=both + block_scratch + held(blocks.shape[0]),
        compiler_params=params(16),
        name="dipole",
    )(ints, far(blocks), rows, from_pair, from_other)

    message, side = pl.pallas_call(
        pack_kernel,
        out_shape=(shape_of(groups, lines + padded + 16, LANES), shape_of(padded, LANES)),
        in_specs=[smem] + [vmem] * 8,
        out_specs=(hbm, vmem),
        scratch_shapes=both
        + [
            pltpu.VMEM((lines, LANES), F32), pltpu.VMEM((groups, padded + 16, LANES), F32),
            pltpu.SemaphoreType.DMA((groups + 1,)),
        ],
        compiler_params=params(8),
        name="pack",
    )(ints, dipole, surface, cols, edges, cells, firsts, from_pair, from_other)
    received = lax.all_to_all(message, "ch", 0, 0)

    table = coupling_table(couple_source, couple_order, couple_weight, groups, chan, padded)
    mats_shape = (NLAM * groups * padded, groups * padded)
    mats, plain = pl.pallas_call(
        functools.partial(aside_kernel, regs),
        out_shape=(jax.ShapeDtypeStruct(mats_shape, jnp.bfloat16), shape_of(2, chan, count)),
        in_specs=[smem] + [vmem] * 3,
        out_specs=(vmem,) * 2,
        compiler_params=params(8),
        name="aside",
    )(ints, table, cells, side)
    received, mats = lax.optimization_barrier((received, mats))

    first, pair, other = pl.pallas_call(
        update_kernel,
        out_shape=(shape_of(lines, LANES), shape_of(halo, LANES), shape_of(halo, LANES)),
        in_specs=[smem] + [vmem] * 5,
        out_specs=(vmem,) * 3,
        scratch_shapes=both,
        compiler_params=params(8),
        name="update",
    )(ints, received, rows, energy_rows, surface, cols)
    from_pair = lax.ppermute(pair, "reg", on_chip)
    from_other = lax.ppermute(other, "reg", off_chip)

    moves = [[(2, 0), (4, 6), (10, 8), (12, 14)], [(6, 0), (14, 8)], [(8, 0)]]
    ends = pair[HALO_ROWS:] + from_pair[HALO_ROWS:]
    ends = ends + lax.ppermute(ends, "reg", moves[0])
    cross, start, near_blocks = pl.pallas_call(
        functools.partial(outer_kernel, count),
        out_shape=(shape_of(groups, padded, LANES), shape_of(padded, LANES), shape_of(near, block_len, block_len)),
        in_specs=[smem, vmem, hbm, hbm],
        out_specs=(vmem,) * 3,
        scratch_shapes=[
            pltpu.VMEM((groups * padded, LANES), F32), pltpu.VMEM(mats_shape, jnp.bfloat16),
            pltpu.SemaphoreType.DMA((NLAM,)), pltpu.SemaphoreType.DMA,
        ],
        compiler_params=params(16),
        name="outer",
    )(ints, received, far(mats), far(blocks))
    cross, ends = lax.optimization_barrier((cross, ends))
    ends = ends + lax.ppermute(ends, "reg", moves[1])
    message = pl.pallas_call(
        second_kernel,
        out_shape=shape_of(groups, lines + padded, LANES),
        in_specs=[smem, vmem, hbm] + [vmem] * 8,
        out_specs=hbm,
        scratch_shapes=both
        + block_scratch
        + held(blocks.shape[0] - near)
        + [pltpu.VMEM((lines, LANES), F32), pltpu.SemaphoreType.DMA((groups + 1,))],
        compiler_params=params(16),
        name="second",
    )(ints, near_blocks, far(blocks), first, from_pair, from_other, pair, surface, side, start, cross)
    message, ends = lax.optimization_barrier((message, ends))
    received = lax.all_to_all(message, "ch", 0, 0)
    ends = ends + lax.ppermute(ends, "reg", moves[2])

    inner, outer = pl.pallas_call(
        finish_kernel,
        out_shape=(shape_of(2, tile_len), shape_of(*cells.shape)),
        in_specs=[smem] + [vmem] * 6,
        out_specs=(vmem,) * 2,
        scratch_shapes=[pltpu.VMEM((lines, LANES), F32)],
        compiler_params=params(8),
        name="finish",
    )(ints, received, rows, first, energy_rows, plain, ends)
    return inner, outer.reshape(chan, pieces, 2, LANES).transpose(2, 0, 1, 3).reshape(2, chan, count)


def solution(mesh):
    return jax.shard_map(
        functools.partial(local, regs=mesh.shape["reg"], groups=mesh.shape["ch"]),
        mesh=mesh,
        in_specs=(
            P(None, "reg"),
            P("reg"),
            P(("reg", "ch"), None, None),
            P(("reg", "ch"), None),
            P("ch", "reg"),
            P("ch"),
            P(None, "ch", "reg"),
            P("ch"),
            P(),
            P(),
            P(),
        ),
        out_specs=(P(None, "reg"), P(None, "ch", "reg")),
        check_vma=False,
    )
```

```python
import functools

import jax
import jax.numpy as jnp
from jax import lax
from jax.experimental import pallas as pl
from jax.experimental.pallas import tpu as pltpu
from jax.sharding import PartitionSpec as P

BLOCKS_PER_SYMM = 4
NLAM = 3
TIME_STEP = 0.05
GRID_STEP = 0.5
BOUNDARY_RADIUS = 20.0
FIRST = TIME_STEP
SECOND = TIME_STEP / 2
LANES = 128
HALO_BLOCKS = 7
HALO_ROWS = 8 * HALO_BLOCKS
WINDOW = 64
F32 = jnp.float32
NT = (((1,), (1,)), ((), ()))


def params(megabytes):
    return pltpu.CompilerParams(vmem_limit_bytes=megabytes * 2**20)


def lane_index(shape):
    return lax.broadcasted_iota(jnp.int32, shape, len(shape) - 1)


def row_index(shape):
    return lax.broadcasted_iota(jnp.int32, shape, len(shape) - 2)


def square(rows):
    count = rows.shape[0]
    if count < LANES:
        rows = jnp.concatenate([rows, jnp.zeros((LANES - count, LANES), F32)], axis=0)
    return rows.T


def wide(column):
    return jnp.broadcast_to(column, (column.shape[0], LANES))


def cells_of(w_ref, part, piece, chan):
    pieces = w_ref.shape[0] // (2 * chan)
    return w_ref[pl.ds(2 * piece + part, chan, stride=2 * pieces), :]


def boundary_sum(vec_rows, surf_ref, sym, first_tile, tiles):
    chan = surf_ref.shape[0]
    sums = [jnp.zeros((chan, LANES), F32) for _ in range(2)]
    for tile in range(tiles):
        here = ((first_tile + tile) // 16).astype(F32)
        values = jnp.where(sym == here, surf_ref[:, LANES * tile : LANES * (tile + 1)], 0.0)
        for part in range(2):
            sums[part] = sums[part] + values * vec_rows(tile, part)
    return [jnp.sum(total, axis=1, keepdims=True) for total in sums]


def surface_rows(slope, surf_ref, sym, first_tile, tiles, out_ref):
    columns = [wide(column) for column in slope]
    for tile in range(tiles):
        here = ((first_tile + tile) // 16).astype(F32)
        values = jnp.where(sym == here, surf_ref[:, LANES * tile : LANES * (tile + 1)], 0.0)
        rows = [jnp.sum(values * columns[part], axis=0, keepdims=True) for part in range(2)]
        at = slice(2 * tile, 2 * tile + 2)
        out_ref[at, :] = out_ref[at, :] + jnp.concatenate(rows, axis=0)


def turn_rows(rows):
    count = rows.shape[0]
    even = row_index(rows.shape) % 2 == 0
    return jnp.where(even, pltpu.roll(rows, count - 1, 0), -pltpu.roll(rows, 1, 0))


def turn_lanes(cells):
    other = pltpu.roll(cells, WINDOW, 1)
    return jnp.where(lane_index(cells.shape) < WINDOW, other, -other)


def halved(values):
    lead = values.astype(jnp.bfloat16).astype(F32)
    return lead, values - lead


def sort_sides(reg, pair_ref, next_ref, left_ref, right_ref):
    odd = reg % 2 == 1
    left_ref[...] = jnp.where(odd, pair_ref[...], next_ref[...])
    right_ref[...] = jnp.where(odd, next_ref[...], pair_ref[...])


def start_kernel(
    idx_ref, pattern_hbm, u_hbm, surf_hbm, w_hbm, energy_hbm, sym_hbm, level_hbm,
    first_ref, pair_ref, next_ref, rows_ref, cols_ref, edge_ref, doubled_ref, ints_ref,
    left_ref, right_ref, wt_ref, u_ref, surf_ref, w_ref, energy_ref, sym_ref, level_ref, pattern_ref, sems,
):
    copies = [
        pltpu.make_async_copy(source, target, sems.at[i])
        for i, (source, target) in enumerate(
            [
                (sym_hbm, sym_ref), (level_hbm, level_ref), (w_hbm, w_ref), (energy_hbm, energy_ref), (u_hbm, u_ref),
                (surf_hbm, surf_ref), (pattern_hbm, pattern_ref),
            ]
        )
    ]
    for copy in copies:
        copy.start()
    reg = idx_ref[0]
    tiles = u_ref.shape[1] // LANES
    chan = surf_ref.shape[0]
    copies[0].wait()
    copies[1].wait()
    head = jnp.zeros((1, LANES - chan), F32)
    sym_row = jnp.concatenate([sym_ref[...].astype(F32), head], axis=1)
    energy_row = jnp.concatenate([level_ref[...], head], axis=1)
    base = square(jnp.concatenate([sym_row, energy_row], axis=0))
    sym = wide(base[:chan, 0:1])
    copies[2].wait()
    for part in range(2):
        for piece in range(wt_ref.shape[1] // LANES):
            cells = cells_of(w_ref, part, piece, chan)
            cells = jnp.concatenate([cells, jnp.zeros((LANES - chan, LANES), F32)], axis=0)
            wt_ref[part, LANES * piece : LANES * (piece + 1), :] = cells.T
    copies[3].wait()
    for tile in range(tiles):
        doubled_ref[2 * tile : 2 * tile + 2, :] = jnp.broadcast_to(energy_ref[tile : tile + 1, :], (2, LANES))
    copies[4].wait()
    for tile in range(tiles):
        rows_ref[2 * tile : 2 * tile + 2, :] = u_ref[:, LANES * tile : LANES * (tile + 1)]
    copies[5].wait()
    partial = boundary_sum(
        lambda tile, part: u_ref[part : part + 1, LANES * tile : LANES * (tile + 1)],
        surf_ref, sym, reg * tiles, tiles,
    )
    lane = lane_index((chan, LANES))
    cols = jnp.where(lane == 0, sym, 0.0)
    cols = jnp.where(lane == 1, wide(base[:chan, 1:2]), cols)
    for part in range(2):
        cols = jnp.where(lane == 2 + part, wide(partial[part]), cols)
    cols = jnp.concatenate([cols, jnp.zeros((cols_ref.shape[0] - chan, LANES), F32)], axis=0)
    cols_ref[...] = cols
    back = jnp.concatenate([cols, jnp.zeros((LANES - cols.shape[0], LANES), F32)], axis=0).T
    partial_rows = back[2:4, :]
    count = wt_ref.shape[1]
    spot = lambda part, point: wt_ref[part, point : point + 1, :]
    zeros = jnp.zeros((2, LANES), F32)
    left_ref[:HALO_ROWS, :] = rows_ref[:HALO_ROWS, :]
    left_ref[HALO_ROWS:, :] = jnp.concatenate([partial_rows, spot(0, 0), spot(0, 1), spot(1, 0), spot(1, 1), zeros], axis=0)
    right_ref[:HALO_ROWS, :] = rows_ref[2 * tiles - HALO_ROWS :, :]
    right_ref[HALO_ROWS:, :] = jnp.concatenate(
        [partial_rows, spot(0, count - 2), spot(0, count - 1), spot(1, count - 2), spot(1, count - 1), zeros], axis=0
    )
    sort_sides(reg, left_ref, right_ref, pair_ref, next_ref)
    cell0 = jnp.concatenate([spot(0, 0), spot(1, 0)], axis=0)
    cell1 = jnp.concatenate([spot(0, 1), spot(1, 1)], axis=0)
    shifted = pltpu.roll(jnp.concatenate([cell0] * 4, axis=0), WINDOW, 1)[0:2]
    first_ref[0] = partial_rows + shifted
    others = first_ref.shape[0] - 1
    first_ref[1:] = jnp.broadcast_to((cell1 + shifted)[None], (others, 2, LANES))
    windows = count // WINDOW
    zero = jnp.zeros((1, LANES), F32)
    for window in range(windows):
        low, high = WINDOW * window - 1, WINDOW * (window + 1)
        edge_ref[4 * window : 4 * window + 4, :] = jnp.concatenate(
            [
                spot(0, low) if window else zero,
                spot(1, low) if window else zero,
                spot(0, high) if window < windows - 1 else zero,
                spot(1, high) if window < windows - 1 else zero,
            ],
            axis=0,
        )
    edge_ref[4 * windows : 4 * windows + 8, :] = jnp.concatenate([cell1, cell0, sym_row, energy_row, zeros], axis=0)
    copies[6].wait()
    ints_ref[0], ints_ref[1] = idx_ref[0], idx_ref[1]
    held = pattern_ref.shape[1]
    for i in range(held):
        ints_ref[2 + i] = pattern_ref[0, i]
        ints_ref[2 + held + i] = pattern_ref[1, i]


def sum_blocks(ints_ref, count, blocks, mine_ref, left_ref, right_ref, states_ref, sums_ref):
    block_len = sums_ref.shape[2]
    rows = mine_ref.shape[0] // 8
    pieces = block_len // LANES
    for column in range(HALO_BLOCKS):
        states_ref[column] = left_ref[8 * column : 8 * column + 8, :]
        states_ref[HALO_BLOCKS + rows + column] = right_ref[8 * column : 8 * column + 8, :]
    for column in range(rows):
        states_ref[HALO_BLOCKS + column] = mine_ref[8 * column : 8 * column + 8, :]
    sums_ref[...] = jnp.zeros(sums_ref.shape, F32)
    for i in range(count):
        row = jnp.clip(ints_ref[2 + i], 0, rows - 1)
        column = jnp.clip(ints_ref[2 + count + i] - ints_ref[0] * rows + HALO_BLOCKS, 0, states_ref.shape[0] - 1)
        tile = states_ref[column]
        state = jnp.concatenate([tile[2 * piece : 2 * piece + 2, :] for piece in range(pieces)], axis=1)
        lead = state.astype(jnp.bfloat16).astype(F32)
        state = jnp.concatenate([lead, state - lead, jnp.zeros((12, block_len), F32)], axis=0).astype(jnp.bfloat16)
        block = blocks(i)
        lead = block.astype(jnp.bfloat16)
        rest = (block - lead.astype(F32)).astype(jnp.bfloat16)
        product = lax.dot_general(state, lead, NT, preferred_element_type=F32)
        product = product + lax.dot_general(state, rest, NT, preferred_element_type=F32)
        sums_ref[row] = sums_ref[row] + product[:8]


def fold_sums(sums_ref, out_ref):
    rows, pieces = sums_ref.shape[0], sums_ref.shape[2] // LANES
    shape = (8, LANES)
    for row in range(rows):
        total = sums_ref[row]
        total = total + pltpu.roll(total, 6, 0)
        picked = jnp.zeros(shape, F32)
        for piece in range(pieces):
            values = total[:, LANES * piece : LANES * (piece + 1)]
            values = pltpu.roll(values, 2 * piece, 0) if piece else values
            picked = jnp.where(row_index(shape) // 2 == piece, values, picked)
        out_ref[8 * row : 8 * row + 8, :] = out_ref[8 * row : 8 * row + 8, :] + picked


def fetched(blocks_hbm, first, held_ref, sems):
    copies = [pltpu.make_async_copy(blocks_hbm.at[first + i], held_ref.at[i], sems.at[i]) for i in range(held_ref.shape[0])]
    for copy in copies:
        copy.start()

    def block(i):
        copies[i - first].wait()
        return held_ref[i - first]

    return block


def dipole_kernel(
    ints_ref, blocks_hbm, mine_ref, pair_ref, next_ref, out_ref, left_ref, right_ref, states_ref, sums_ref, held_ref, sems
):
    sort_sides(ints_ref[0], pair_ref, next_ref, left_ref, right_ref)
    block = fetched(blocks_hbm, 0, held_ref, sems)
    sum_blocks(ints_ref, held_ref.shape[0], block, mine_ref, left_ref, right_ref, states_ref, sums_ref)
    out_ref[...] = jnp.zeros(out_ref.shape, F32)
    fold_sums(sums_ref, out_ref)


def pack_kernel(
    idx_ref, dipole_ref, surf_ref, cols_ref, edge_ref, w_ref, first_ref, pair_ref, next_ref,
    message_hbm, side_ref, left_ref, right_ref, total_ref, packed_ref, message_ref, sems,
):
    sort_sides(idx_ref[0], pair_ref, next_ref, left_ref, right_ref)
    reg = idx_ref[0]
    chan = surf_ref.shape[0]
    padded = cols_ref.shape[0]
    tiles = surf_ref.shape[1] // LANES
    windows = message_hbm.shape[0]
    regs = first_ref.shape[0]
    sym = wide(cols_ref[:chan, 0:1])
    received = first_ref[0]
    lane2 = lane_index((2, LANES))
    low = jnp.where(lane2 < WINDOW, received, 0.0)
    cell0 = jnp.where(lane2 < WINDOW, pltpu.roll(jnp.concatenate([received] * 4, axis=0), WINDOW, 1)[0:2], 0.0)
    cell1 = jnp.where(reg == 0, edge_ref[4 * windows : 4 * windows + 2, :], low)
    whole = jnp.zeros((2, LANES), F32)
    for source in range(regs):
        whole = whole + first_ref[source]
    whole = jnp.where((lane2 < WINDOW) & (reg == 0), whole, 0.0)
    beside = left_ref[HALO_ROWS : HALO_ROWS + 2, :] + right_ref[HALO_ROWS : HALO_ROWS + 2, :]
    side = square(
        jnp.concatenate(
            [
                cell0, cell1, beside, whole,
                left_ref[HALO_ROWS + 2 : HALO_ROWS + 4, :], right_ref[HALO_ROWS + 2 : HALO_ROWS + 4, :],
                left_ref[HALO_ROWS + 4 : HALO_ROWS + 6, :], right_ref[HALO_ROWS + 4 : HALO_ROWS + 6, :],
            ],
            axis=0,
        )
    )[:chan]
    symmetry, energy = cols_ref[:chan, 0:1], cols_ref[:chan, 1:2]
    radius = BOUNDARY_RADIUS + GRID_STEP
    potential = symmetry * (symmetry + 1.0) / (2.0 * radius * radius) + energy
    slope, start = [], []
    for part in range(2):
        here, beyond = side[:, part : part + 1], side[:, 2 + part : 3 + part]
        boundary = cols_ref[:chan, 2 + part : 3 + part] + side[:, 4 + part : 5 + part]
        slope.append(here - boundary)
        start.append(-2.0 * (beyond - 2.0 * here + boundary) + potential * here)
    lane = lane_index((chan, LANES))
    out = jnp.where((lane >= 6) & (lane < 16), side, 0.0)
    for part in range(2):
        out = jnp.where(lane == part, wide(start[part]), out)
    out = jnp.where(lane == 2, sym, out)
    out = jnp.where(lane == 3, wide(energy), out)
    side_ref[...] = jnp.concatenate([out, jnp.zeros((padded - chan, LANES), F32)], axis=0)
    level = halved(edge_ref[4 * windows + 5 : 4 * windows + 6, :])
    ends = halved(whole)
    tail = [cell0, edge_ref[4 * windows + 4 : 4 * windows + 5, :], level[0], ends[0], level[1], ends[1], jnp.zeros((3, LANES), F32)]
    gap = jnp.zeros((WINDOW - chan, LANES), F32)
    half = lane < WINDOW
    for window in range(windows):
        one, two = (cells_of(w_ref, part, window // 2, chan) for part in range(2))
        if window % 2 == 0:
            cells = jnp.where(half, one, pltpu.roll(two, WINDOW, 1))
        else:
            cells = jnp.where(half, pltpu.roll(one, WINDOW, 1), two)
        edges = edge_ref[4 * window : 4 * window + 4, :]
        if window == 0:
            edges = jnp.concatenate([left_ref[HALO_ROWS + 3 : HALO_ROWS + 4, :], left_ref[HALO_ROWS + 5 : HALO_ROWS + 6, :], edges[2:4]], axis=0)
        if window == windows - 1:
            edges = jnp.concatenate([edges[0:2], right_ref[HALO_ROWS + 2 : HALO_ROWS + 3, :], right_ref[HALO_ROWS + 4 : HALO_ROWS + 5, :]], axis=0)
        message_ref[window] = jnp.concatenate([cells, gap, edges] + tail, axis=0).astype(jnp.bfloat16)
    lines = packed_ref.shape[0]
    outer_copy = pltpu.make_async_copy(message_ref, message_hbm.at[:, lines:], sems.at[windows])
    outer_copy.start()
    total_ref[...] = dipole_ref[...]
    surface_rows(slope, surf_ref, sym, reg * tiles, tiles, total_ref)
    packed_ref[...] = jnp.concatenate(halved(total_ref[...]), axis=0).astype(jnp.bfloat16)
    copies = [pltpu.make_async_copy(packed_ref, message_hbm.at[window, :lines], sems.at[window]) for window in range(windows)]
    for copy in copies:
        copy.start()
    for copy in copies + [outer_copy]:
        copy.wait()


def update_kernel(
    idx_ref, received_ref, u_ref, energy_ref, surf_ref, cols_ref, out_ref, pair_ref, next_ref, left_ref, right_ref
):
    reg = idx_ref[0]
    lines = u_ref.shape[0]
    tiles = lines // 2
    chan = surf_ref.shape[0]
    image = energy_ref[...] * u_ref[...]
    for source in range(received_ref.shape[0]):
        values = received_ref[source, : 2 * lines, :].astype(F32)
        image = image + (values[:lines] + values[lines:])
    out_ref[...] = FIRST * turn_rows(image)
    sym = wide(cols_ref[:chan, 0:1])
    partial = boundary_sum(
        lambda tile, part: out_ref[2 * tile + part : 2 * tile + part + 1, :], surf_ref, sym, reg * tiles, tiles
    )
    lane = lane_index((chan, LANES))
    cols = jnp.where(lane == 0, wide(partial[0]), 0.0)
    cols = jnp.where(lane == 1, wide(partial[1]), cols)
    rows = jnp.concatenate([cols, jnp.zeros((LANES - chan, LANES), F32)], axis=0).T[0:8, :]
    left_ref[:HALO_ROWS, :] = out_ref[:HALO_ROWS, :]
    left_ref[HALO_ROWS:, :] = rows
    right_ref[:HALO_ROWS, :] = out_ref[lines - HALO_ROWS :, :]
    right_ref[HALO_ROWS:, :] = rows
    sort_sides(reg, left_ref, right_ref, pair_ref, next_ref)


def stencil(cells, lows, highs, potential, seams):
    count = cells.shape[1]
    lane = lane_index(cells.shape)
    below, above = pltpu.roll(cells, 1, 1), pltpu.roll(cells, count - 1, 1)
    for (first, last), low, high in zip(seams, lows, highs):
        below = jnp.where(lane == first, low, below)
        above = jnp.where(lane == last, high, above)
    return -2.0 * (above - 2.0 * cells + below) + potential * cells


def mats_of(mats_hbm, mats_ref, sems):
    rows = mats_ref.shape[0] // NLAM
    spans = [pl.ds(level * rows, rows) for level in range(NLAM)]
    copies = [pltpu.make_async_copy(mats_hbm.at[span], mats_ref.at[span], sems.at[i]) for i, span in enumerate(spans)]
    for copy in copies:
        copy.start()
    waiting = set(range(NLAM))

    def mats(level):
        if level in waiting:
            waiting.discard(level)
            copies[level].wait()
        return mats_ref[spans[level], :]

    return mats


def outer_kernel(count, idx_ref, received_ref, mats_hbm, blocks_hbm, cross_ref, start_ref, near_ref, edge_ref, mats_ref, sems, sem):
    copy = pltpu.make_async_copy(blocks_hbm.at[: near_ref.shape[0]], near_ref, sem)
    copy.start()
    mats = mats_of(mats_hbm, mats_ref, sems)
    reg, ch = idx_ref[0], idx_ref[1]
    groups, padded = cross_ref.shape[0], cross_ref.shape[1]
    lines = received_ref.shape[1] - WINDOW - 16
    rows = groups * padded
    cells = received_ref[:, lines : lines + WINDOW, :].astype(F32)[:, :padded].reshape(rows, LANES)
    flipped = received_ref[:, lines + WINDOW :, :].astype(F32).reshape(groups * 16, LANES).T
    extra = jnp.concatenate(
        [pltpu.roll(flipped[:padded], (LANES - 16 * group) % LANES, 1) for group in range(groups)], axis=0
    )
    first_point = reg * count + ch * WINDOW
    lane = lane_index((1, LANES))
    point = (first_point + lane % WINDOW + 1).astype(F32)
    radius = BOUNDARY_RADIUS + GRID_STEP * point
    extra_point = jnp.where(lane < 2, first_point, jnp.where(lane < 4, first_point + WINDOW + 1, 1)).astype(F32)
    extra_ratio = BOUNDARY_RADIUS / (BOUNDARY_RADIUS + GRID_STEP * extra_point)
    ratio = BOUNDARY_RADIUS / radius

    def mix(states, scale):
        states = states.astype(jnp.bfloat16)
        mixed, power = 0.0, 1.0
        for level in range(NLAM):
            mixed = mixed + power * jnp.dot(mats(level), states, preferred_element_type=F32)
            power = power * scale
        return mixed.astype(jnp.bfloat16).astype(F32)

    symmetry, energy = extra[:, 6:7], extra[:, 7:8] + extra[:, 10:11]
    potential = symmetry * (symmetry + 1.0) / (2.0 * radius * radius) + energy
    mixed = mix(jnp.concatenate([cells, extra], axis=1), jnp.concatenate([ratio, extra_ratio], axis=1))
    main, beside = mixed[:, :LANES], mixed[:, LANES:]
    edge_ref[...] = beside
    start_ref[...] = edge_ref[pl.ds(pl.multiple_of(ch * padded, 8), padded), :]
    inner_end = (reg == 0) & (ch == 0)
    seams = ((0, WINDOW - 1), (WINDOW, 2 * WINDOW - 1))
    ends = [extra[:, 8 + part : 9 + part] + extra[:, 11 + part : 12 + part] for part in range(2)]
    lows = [jnp.where(inner_end, ends[part], extra[:, part : part + 1]) for part in range(2)]
    highs = [extra[:, 2 + part : 3 + part] for part in range(2)]
    first = FIRST * turn_lanes(stencil(cells, lows, highs, potential, seams) + main)
    later = mix(first, ratio)
    cross = FIRST * turn_lanes(main)
    mixed_lows = [jnp.where(inner_end, 0.0, beside[:, part : part + 1]) for part in range(2)]
    mixed_highs = [beside[:, 2 + part : 3 + part] for part in range(2)]
    lows = [FIRST * mixed_lows[1], -FIRST * mixed_lows[0]]
    highs = [FIRST * mixed_highs[1], -FIRST * mixed_highs[0]]
    cross = cross + SECOND * turn_lanes(stencil(cross, lows, highs, potential, seams) + later)
    cross_ref[...] = cross.reshape(groups, padded, LANES)
    copy.wait()


def plain_part(regs, reg, w_ref, side_ref, plain_ref):
    chan, count = plain_ref.shape[1], plain_ref.shape[2]
    side = side_ref[...][:chan]
    symmetry, energy = side[:, 2:3], side[:, 3:4]
    lane = lane_index((1, count))
    radius = BOUNDARY_RADIUS + GRID_STEP * (reg * count + lane + 1).astype(F32)
    potential = symmetry * (symmetry + 1.0) / (2.0 * radius * radius) + energy

    def potential_at(index):
        there = BOUNDARY_RADIUS + GRID_STEP * (reg * count + index + 1).astype(F32)
        return symmetry * (symmetry + 1.0) / (2.0 * there * there) + energy

    last = reg == regs - 1
    images, lows, highs = [], [], []
    values_of = [
        jnp.concatenate([cells_of(w_ref, part, piece, chan) for piece in range(count // LANES)], axis=1) for part in range(2)
    ]
    for part in range(2):
        values = values_of[part]
        at = 8 + 4 * part
        low2, low1, high1, high2 = (side[:, at + i : at + i + 1] for i in range(4))
        low = jnp.where(reg == 0, side[:, 6 + part : 7 + part], low1)
        images.append(stencil(values, [low], [high1], potential, ((0, count - 1),)))
        under = -2.0 * (values[:, 0:1] - 2.0 * low1 + low2) + potential_at(jnp.int32(-1)) * low1
        over = -2.0 * (high2 - 2.0 * high1 + values[:, count - 1 : count]) + potential_at(jnp.int32(count)) * high1
        lows.append(jnp.where(reg == 0, 0.0, under))
        highs.append(jnp.where(last, 0.0, over))
    turned = [FIRST * images[1], -FIRST * images[0]]
    lows = [FIRST * lows[1], -FIRST * lows[0]]
    highs = [FIRST * highs[1], -FIRST * highs[0]]
    again = [stencil(turned[p], [lows[p]], [highs[p]], potential, ((0, count - 1),)) for p in range(2)]
    plain_ref[0] = values_of[0] + turned[0] + SECOND * again[1]
    plain_ref[1] = values_of[1] + turned[1] - SECOND * again[0]


def second_kernel(
    ints_ref, near_ref, blocks_hbm, mine_ref, pair_ref, next_ref, own_ref, surf_ref, side_ref, start_ref, cross_ref,
    message_hbm, left_ref, right_ref, states_ref, sums_ref, held_ref, sems, total_ref, out_sems,
):
    sort_sides(ints_ref[0], pair_ref, next_ref, left_ref, right_ref)
    near = near_ref.shape[0]
    rest = fetched(blocks_hbm, near, held_ref, sems)
    outer_copy = pltpu.make_async_copy(cross_ref, message_hbm.at[:, total_ref.shape[0] :], out_sems.at[message_hbm.shape[0]])
    outer_copy.start()
    block = lambda i: near_ref[i] if i < near else rest(i)
    sum_blocks(ints_ref, near + held_ref.shape[0], block, mine_ref, left_ref, right_ref, states_ref, sums_ref)
    total_ref[...] = jnp.zeros(total_ref.shape, F32)
    reg = ints_ref[0]
    chan = surf_ref.shape[0]
    tiles = surf_ref.shape[1] // LANES
    ends = own_ref[HALO_ROWS:, :] + left_ref[HALO_ROWS:, :] + right_ref[HALO_ROWS:, :]
    boundary = square(ends)[:chan]
    mixed = start_ref[:chan, :]
    side = side_ref[:chan, :]
    image = [side[:, part : part + 1] + mixed[:, 4 + part : 5 + part] for part in range(2)]
    slope = [FIRST * image[1] - boundary[:, 0:1], -FIRST * image[0] - boundary[:, 1:2]]
    surface_rows(slope, surf_ref, wide(side[:, 2:3]), reg * tiles, tiles, total_ref)
    fold_sums(sums_ref, total_ref)
    lines = total_ref.shape[0]
    groups = message_hbm.shape[0]
    copies = [pltpu.make_async_copy(total_ref, message_hbm.at[group, :lines], out_sems.at[group]) for group in range(groups)]
    for copy in copies:
        copy.start()
    for copy in copies + [outer_copy]:
        copy.wait()


def finish_kernel(idx_ref, received_ref, u_ref, first_ref, energy_ref, plain_ref, ends_ref, inner_ref, outer_ref, total_ref):
    reg = idx_ref[0]
    lines = u_ref.shape[0]
    chan = plain_ref.shape[1]
    image = energy_ref[...] * first_ref[...]
    sources = received_ref.shape[0]
    for source in range(sources):
        image = image + received_ref[source, :lines, :]
    total = u_ref[...] + first_ref[...] + SECOND * turn_rows(image)
    total_ref[...] = total
    for tile in range(lines // 2):
        inner_ref[:, LANES * tile : LANES * (tile + 1)] = total_ref[2 * tile : 2 * tile + 2, :]
    columns = square(ends_ref[...])[:chan]
    lane = lane_index((chan, LANES))
    half = lane < WINDOW
    for piece in range(sources // 2):
        even = received_ref[2 * piece, lines : lines + chan, :]
        odd = received_ref[2 * piece + 1, lines : lines + chan, :]
        one = jnp.where(half, even, pltpu.roll(odd, WINDOW, 1))
        two = jnp.where(half, pltpu.roll(even, WINDOW, 1), odd)
        at = slice(LANES * piece, LANES * (piece + 1))
        one = plain_ref[0, :, at] + one
        two = plain_ref[1, :, at] + two
        if piece == 0:
            here = (lane == 0) & (reg == 0)
            one = one + jnp.where(here, -2.0 * SECOND * columns[:, 1:2], 0.0)
            two = two + jnp.where(here, 2.0 * SECOND * columns[:, 0:1], 0.0)
        for part, cells in enumerate((one, two)):
            outer_ref[pl.ds(2 * piece + part, chan, stride=sources), :] = cells


def aside_kernel(regs, idx_ref, table_ref, w_ref, side_ref, mats_ref, plain_ref):
    plain_part(regs, idx_ref[0], w_ref, side_ref, plain_ref)
    build_mats(table_ref, mats_ref)


def build_mats(table_ref, mats_ref):
    rows = mats_ref.shape[0] // NLAM
    span = table_ref.shape[1]
    entries = table_ref.shape[0] // 4
    for first in range(0, rows, LANES):
        count = min(LANES, rows - first)
        columns = square(table_ref[:, first : first + LANES])[:count]
        here = lane_index((count, span)).astype(F32)
        sums = [jnp.zeros((count, span), F32) for _ in range(NLAM)]
        for entry in range(entries):
            hit = columns[:, entry : entry + 1] == here
            order = columns[:, entries + entry : entries + entry + 1]
            weight = columns[:, 2 * entries + entry : 2 * entries + entry + 1]
            for level in range(NLAM):
                picked = jnp.where(order == level, weight, 0.0)
                sums[level] = sums[level] + jnp.where(hit, picked, 0.0)
        for level in range(NLAM):
            at = level * rows + first
            mats_ref[at : at + count, :] = sums[level][:, :rows].astype(jnp.bfloat16)


def coupling_table(source, order_list, weight, groups, chan, padded):
    place = (source // chan) * padded + source % chan
    rows = jnp.concatenate([place.T.astype(F32), order_list.T.astype(F32), weight.T, jnp.zeros_like(weight.T)], axis=0)
    rows = rows.reshape(rows.shape[0], groups, chan)
    rows = jnp.pad(rows, ((0, 0), (0, 0), (0, padded - chan))).reshape(rows.shape[0], groups * padded)
    return jnp.pad(rows, ((0, 0), (0, -rows.shape[1] % LANES)))


def shape_of(*shape):
    return jax.ShapeDtypeStruct(shape, F32)


def local(
    inner_state, energy, blocks, pattern, surface, channel_symmetry, outer_state, channel_energy,
    couple_source, couple_order, couple_weight, *, regs, groups,
):
    tile_len = inner_state.shape[1]
    lines = 2 * tile_len // LANES
    block_len = blocks.shape[1]
    block_rows = tile_len // block_len
    chan = outer_state.shape[1]
    count = outer_state.shape[2]
    padded = -(-chan // 8) * 8
    idx = jnp.stack([lax.axis_index("reg"), lax.axis_index("ch")]).astype(jnp.int32)
    smem = pl.BlockSpec(memory_space=pltpu.SMEM)
    vmem = pl.BlockSpec(memory_space=pltpu.VMEM)
    hbm = pl.BlockSpec(memory_space=pltpu.HBM)
    far = lambda array: pltpu.with_memory_space_constraint(array, pltpu.HBM)
    halo = HALO_ROWS + 8
    pieces = count // LANES
    cells = outer_state.reshape(2, chan, pieces, LANES).transpose(1, 2, 0, 3).reshape(2 * chan * pieces, LANES)
    near = blocks.shape[0] * 5 // 8

    both = [pltpu.VMEM((halo, LANES), F32)] * 2
    first_msg, pair, other, rows, cols, edges, energy_rows, ints = pl.pallas_call(
        start_kernel,
        out_shape=(
            shape_of(regs, 2, LANES), shape_of(halo, LANES), shape_of(halo, LANES), shape_of(lines, LANES),
            shape_of(padded, LANES), shape_of(4 * groups + 8, LANES), shape_of(lines, LANES),
            jax.ShapeDtypeStruct((2 + pattern.size,), jnp.int32),
        ),
        in_specs=[smem] + [hbm] * 7,
        out_specs=(vmem,) * 7 + (smem,),
        scratch_shapes=both
        + [
            pltpu.VMEM((2, count, LANES), F32), pltpu.VMEM((2, tile_len), F32), pltpu.VMEM((chan, tile_len), F32),
            pltpu.VMEM(cells.shape, F32), pltpu.VMEM((lines // 2, LANES), F32),
            pltpu.VMEM((1, chan), jnp.int32), pltpu.VMEM((1, chan), F32), pltpu.SMEM((2, blocks.shape[0]), jnp.int32),
            pltpu.SemaphoreType.DMA((7,)),
        ],
        compiler_params=params(8),
        name="start",
    )(idx, far(pattern.T), far(inner_state), far(surface), far(cells), far(energy.reshape(lines // 2, LANES)),
      far(channel_symmetry.reshape(1, chan)), far(channel_energy.reshape(1, chan)))

    firsts = lax.all_to_all(first_msg, "reg", 0, 0)
    on_chip = [(i, i ^ 1) for i in range(regs)]
    off_chip = [move for i in range(1, regs - 1, 2) for move in ((i, i + 1), (i + 1, i))]
    from_pair = lax.ppermute(pair, "reg", on_chip)
    from_other = lax.ppermute(other, "reg", off_chip)
    block_scratch = [
        pltpu.VMEM((2 * HALO_BLOCKS + block_rows, 8, LANES), F32),
        pltpu.VMEM((block_rows, 8, block_len), F32),
    ]
    held = lambda blocks: [pltpu.VMEM((blocks, block_len, block_len), F32), pltpu.SemaphoreType.DMA((blocks,))]
    dipole = pl.pallas_call(
        dipole_kernel,
        out_shape=shape_of(lines, LANES),
        in_specs=[smem, hbm] + [vmem] * 3,
        out_specs=vmem,
        scratch_shapes=both + block_scratch + held(blocks.shape[0]),
        compiler_params=params(16),
        name="dipole",
    )(ints, far(blocks), rows, from_pair, from_other)

    message, side = pl.pallas_call(
        pack_kernel,
        out_shape=(
            jax.ShapeDtypeStruct((groups, 2 * lines + WINDOW + 16, LANES), jnp.bfloat16), shape_of(padded, LANES),
        ),
        in_specs=[smem] + [vmem] * 8,
        out_specs=(hbm, vmem),
        scratch_shapes=both
        + [
            pltpu.VMEM((lines, LANES), F32), pltpu.VMEM((2 * lines, LANES), jnp.bfloat16),
            pltpu.VMEM((groups, WINDOW + 16, LANES), jnp.bfloat16),
            pltpu.SemaphoreType.DMA((groups + 1,)),
        ],
        compiler_params=params(8),
        name="pack",
    )(ints, dipole, surface, cols, edges, cells, firsts, from_pair, from_other)
    received = lax.all_to_all(message, "ch", 0, 0)

    table = coupling_table(couple_source, couple_order, couple_weight, groups, chan, padded)
    mats_shape = (NLAM * groups * padded, groups * padded)
    mats, plain = pl.pallas_call(
        functools.partial(aside_kernel, regs),
        out_shape=(jax.ShapeDtypeStruct(mats_shape, jnp.bfloat16), shape_of(2, chan, count)),
        in_specs=[smem] + [vmem] * 3,
        out_specs=(vmem,) * 2,
        compiler_params=params(8),
        name="aside",
    )(ints, table, cells, side)
    received, mats = lax.optimization_barrier((received, mats))

    first, pair, other = pl.pallas_call(
        update_kernel,
        out_shape=(shape_of(lines, LANES), shape_of(halo, LANES), shape_of(halo, LANES)),
        in_specs=[smem] + [vmem] * 5,
        out_specs=(vmem,) * 3,
        scratch_shapes=both,
        compiler_params=params(8),
        name="update",
    )(ints, received, rows, energy_rows, surface, cols)
    from_pair = lax.ppermute(pair, "reg", on_chip)
    from_other = lax.ppermute(other, "reg", off_chip)

    moves = [[(2, 0), (4, 6), (8, 10), (12, 14)], [(6, 0)], [(10, 0)], [(14, 0)]]
    ends = pair[HALO_ROWS:] + from_pair[HALO_ROWS:]
    ends = ends + lax.ppermute(ends, "reg", moves[0])
    cross, start, near_blocks = pl.pallas_call(
        functools.partial(outer_kernel, count),
        out_shape=(shape_of(groups, padded, LANES), shape_of(padded, LANES), shape_of(near, block_len, block_len)),
        in_specs=[smem, vmem, hbm, hbm],
        out_specs=(vmem,) * 3,
        scratch_shapes=[
            pltpu.VMEM((groups * padded, LANES), F32), pltpu.VMEM(mats_shape, jnp.bfloat16),
            pltpu.SemaphoreType.DMA((NLAM,)), pltpu.SemaphoreType.DMA,
        ],
        compiler_params=params(16),
        name="outer",
    )(ints, received, far(mats), far(blocks))
    cross, ends = lax.optimization_barrier((cross, ends))
    message = pl.pallas_call(
        second_kernel,
        out_shape=shape_of(groups, lines + padded, LANES),
        in_specs=[smem, vmem, hbm] + [vmem] * 8,
        out_specs=hbm,
        scratch_shapes=both
        + block_scratch
        + held(blocks.shape[0] - near)
        + [pltpu.VMEM((lines, LANES), F32), pltpu.SemaphoreType.DMA((groups + 1,))],
        compiler_params=params(16),
        name="second",
    )(ints, near_blocks, far(blocks), first, from_pair, from_other, pair, surface, side, start, cross)
    message, ends = lax.optimization_barrier((message, ends))
    received = lax.all_to_all(message, "ch", 0, 0)
    ends = ends + sum(lax.ppermute(ends, "reg", move) for move in moves[1:])

    inner, outer = pl.pallas_call(
        finish_kernel,
        out_shape=(shape_of(2, tile_len), shape_of(*cells.shape)),
        in_specs=[smem] + [vmem] * 6,
        out_specs=(vmem,) * 2,
        scratch_shapes=[pltpu.VMEM((lines, LANES), F32)],
        compiler_params=params(8),
        name="finish",
    )(ints, received, rows, first, energy_rows, plain, ends)
    return inner, outer.reshape(chan, pieces, 2, LANES).transpose(2, 0, 1, 3).reshape(2, chan, count)


def solution(mesh):
    return jax.shard_map(
        functools.partial(local, regs=mesh.shape["reg"], groups=mesh.shape["ch"]),
        mesh=mesh,
        in_specs=(
            P(None, "reg"),
            P("reg"),
            P(("reg", "ch"), None, None),
            P(("reg", "ch"), None),
            P("ch", "reg"),
            P("ch"),
            P(None, "ch", "reg"),
            P("ch"),
            P(),
            P(),
            P(),
        ),
        out_specs=(P(None, "reg"), P(None, "ch", "reg")),
        check_vma=False,
    )
```

```python
import functools

import jax
import jax.numpy as jnp
from jax import lax
from jax.experimental import pallas as pl
from jax.experimental.pallas import tpu as pltpu
from jax.sharding import PartitionSpec as P

BLOCKS_PER_SYMM = 4
NLAM = 3
TIME_STEP = 0.05
GRID_STEP = 0.5
BOUNDARY_RADIUS = 20.0
FIRST = TIME_STEP
SECOND = TIME_STEP / 2
LANES = 128
HALO_BLOCKS = 7
HALO_ROWS = 8 * HALO_BLOCKS
WINDOW = 64
SURFACE_PARTS = 4
F32 = jnp.float32
NT = (((1,), (1,)), ((), ()))


def params(megabytes):
    return pltpu.CompilerParams(vmem_limit_bytes=megabytes * 2**20)


def lane_index(shape):
    return lax.broadcasted_iota(jnp.int32, shape, len(shape) - 1)


def row_index(shape):
    return lax.broadcasted_iota(jnp.int32, shape, len(shape) - 2)


def square(rows):
    count = rows.shape[0]
    if count < LANES:
        rows = jnp.concatenate([rows, jnp.zeros((LANES - count, LANES), F32)], axis=0)
    return rows.T


def wide(column):
    return jnp.broadcast_to(column, (column.shape[0], LANES))


def cells_of(w_ref, part, piece, chan):
    pieces = w_ref.shape[0] // (2 * chan)
    return w_ref[pl.ds(2 * piece + part, chan, stride=2 * pieces), :]


def boundary_sum(vec_rows, surf_ref, sym, first_tile, tiles, waits=()):
    chan = surf_ref.shape[0]
    sums = [jnp.zeros((chan, LANES), F32) for _ in range(2)]
    for tile in range(tiles):
        if waits and tile % (tiles // len(waits)) == 0:
            waits[tile // (tiles // len(waits))].wait()
        here = ((first_tile + tile) // 16).astype(F32)
        values = jnp.where(sym == here, surf_ref[:, LANES * tile : LANES * (tile + 1)], 0.0)
        for part in range(2):
            sums[part] = sums[part] + values * vec_rows(tile, part)
    return [jnp.sum(total, axis=1, keepdims=True) for total in sums]


def surface_rows(slope, surf_ref, sym, first_tile, tiles, out_ref):
    columns = [wide(column) for column in slope]
    for tile in range(tiles):
        here = ((first_tile + tile) // 16).astype(F32)
        values = jnp.where(sym == here, surf_ref[:, LANES * tile : LANES * (tile + 1)], 0.0)
        rows = [jnp.sum(values * columns[part], axis=0, keepdims=True) for part in range(2)]
        at = slice(2 * tile, 2 * tile + 2)
        out_ref[at, :] = out_ref[at, :] + jnp.concatenate(rows, axis=0)


def turn_rows(rows):
    count = rows.shape[0]
    even = row_index(rows.shape) % 2 == 0
    return jnp.where(even, pltpu.roll(rows, count - 1, 0), -pltpu.roll(rows, 1, 0))


def turn_lanes(cells):
    other = pltpu.roll(cells, WINDOW, 1)
    return jnp.where(lane_index(cells.shape) < WINDOW, other, -other)


def halved(values):
    lead = values.astype(jnp.bfloat16).astype(F32)
    return lead, values - lead


def sort_sides(reg, pair_ref, next_ref, left_ref, right_ref):
    odd = reg % 2 == 1
    left_ref[...] = jnp.where(odd, pair_ref[...], next_ref[...])
    right_ref[...] = jnp.where(odd, next_ref[...], pair_ref[...])


def start_kernel(
    idx_ref, pattern_hbm, u_hbm, surf_hbm, w_hbm, energy_hbm, sym_hbm, level_hbm,
    first_ref, pair_ref, next_ref, rows_ref, cols_ref, edge_ref, doubled_ref, ints_ref,
    left_ref, right_ref, wt_ref, u_ref, surf_ref, w_ref, energy_ref, sym_ref, level_ref, pattern_ref, sems,
):
    width = surf_ref.shape[1] // SURFACE_PARTS
    spans = [pl.ds(part * width, width) for part in range(SURFACE_PARTS)]
    copies = [
        pltpu.make_async_copy(source, target, sems.at[i])
        for i, (source, target) in enumerate(
            [
                (sym_hbm, sym_ref), (level_hbm, level_ref), (w_hbm, w_ref), (energy_hbm, energy_ref), (u_hbm, u_ref),
                (pattern_hbm, pattern_ref),
                *((surf_hbm.at[:, span], surf_ref.at[:, span]) for span in spans),
            ]
        )
    ]
    for copy in copies:
        copy.start()
    reg = idx_ref[0]
    tiles = u_ref.shape[1] // LANES
    chan = surf_ref.shape[0]
    copies[0].wait()
    copies[1].wait()
    head = jnp.zeros((1, LANES - chan), F32)
    sym_row = jnp.concatenate([sym_ref[...].astype(F32), head], axis=1)
    energy_row = jnp.concatenate([level_ref[...], head], axis=1)
    base = square(jnp.concatenate([sym_row, energy_row], axis=0))
    sym = wide(base[:chan, 0:1])
    copies[2].wait()
    for part in range(2):
        for piece in range(wt_ref.shape[1] // LANES):
            cells = cells_of(w_ref, part, piece, chan)
            cells = jnp.concatenate([cells, jnp.zeros((LANES - chan, LANES), F32)], axis=0)
            wt_ref[part, LANES * piece : LANES * (piece + 1), :] = cells.T
    copies[3].wait()
    for tile in range(tiles):
        doubled_ref[2 * tile : 2 * tile + 2, :] = jnp.broadcast_to(energy_ref[tile : tile + 1, :], (2, LANES))
    copies[4].wait()
    for tile in range(tiles):
        rows_ref[2 * tile : 2 * tile + 2, :] = u_ref[:, LANES * tile : LANES * (tile + 1)]
    partial = boundary_sum(
        lambda tile, part: u_ref[part : part + 1, LANES * tile : LANES * (tile + 1)],
        surf_ref, sym, reg * tiles, tiles, copies[6:],
    )
    lane = lane_index((chan, LANES))
    cols = jnp.where(lane == 0, sym, 0.0)
    cols = jnp.where(lane == 1, wide(base[:chan, 1:2]), cols)
    for part in range(2):
        cols = jnp.where(lane == 2 + part, wide(partial[part]), cols)
    cols = jnp.concatenate([cols, jnp.zeros((cols_ref.shape[0] - chan, LANES), F32)], axis=0)
    cols_ref[...] = cols
    back = jnp.concatenate([cols, jnp.zeros((LANES - cols.shape[0], LANES), F32)], axis=0).T
    partial_rows = back[2:4, :]
    count = wt_ref.shape[1]
    spot = lambda part, point: wt_ref[part, point : point + 1, :]
    zeros = jnp.zeros((2, LANES), F32)
    left_ref[:HALO_ROWS, :] = rows_ref[:HALO_ROWS, :]
    left_ref[HALO_ROWS:, :] = jnp.concatenate([partial_rows, spot(0, 0), spot(0, 1), spot(1, 0), spot(1, 1), zeros], axis=0)
    right_ref[:HALO_ROWS, :] = rows_ref[2 * tiles - HALO_ROWS :, :]
    right_ref[HALO_ROWS:, :] = jnp.concatenate(
        [partial_rows, spot(0, count - 2), spot(0, count - 1), spot(1, count - 2), spot(1, count - 1), zeros], axis=0
    )
    sort_sides(reg, left_ref, right_ref, pair_ref, next_ref)
    cell0 = jnp.concatenate([spot(0, 0), spot(1, 0)], axis=0)
    cell1 = jnp.concatenate([spot(0, 1), spot(1, 1)], axis=0)
    shifted = pltpu.roll(jnp.concatenate([cell0] * 4, axis=0), WINDOW, 1)[0:2]
    first_ref[0] = partial_rows + shifted
    others = first_ref.shape[0] - 1
    first_ref[1:] = jnp.broadcast_to((cell1 + shifted)[None], (others, 2, LANES))
    windows = count // WINDOW
    zero = jnp.zeros((1, LANES), F32)
    for window in range(windows):
        low, high = WINDOW * window - 1, WINDOW * (window + 1)
        edge_ref[4 * window : 4 * window + 4, :] = jnp.concatenate(
            [
                spot(0, low) if window else zero,
                spot(1, low) if window else zero,
                spot(0, high) if window < windows - 1 else zero,
                spot(1, high) if window < windows - 1 else zero,
            ],
            axis=0,
        )
    edge_ref[4 * windows : 4 * windows + 8, :] = jnp.concatenate([cell1, cell0, sym_row, energy_row, zeros], axis=0)
    copies[5].wait()
    ints_ref[0], ints_ref[1] = idx_ref[0], idx_ref[1]
    held = pattern_ref.shape[1]
    for i in range(held):
        ints_ref[2 + i] = pattern_ref[0, i]
        ints_ref[2 + held + i] = pattern_ref[1, i]


def sum_blocks(ints_ref, count, blocks, mine_ref, left_ref, right_ref, states_ref, sums_ref):
    block_len = sums_ref.shape[2]
    rows = mine_ref.shape[0] // 8
    pieces = block_len // LANES
    for column in range(HALO_BLOCKS):
        states_ref[column] = left_ref[8 * column : 8 * column + 8, :]
        states_ref[HALO_BLOCKS + rows + column] = right_ref[8 * column : 8 * column + 8, :]
    for column in range(rows):
        states_ref[HALO_BLOCKS + column] = mine_ref[8 * column : 8 * column + 8, :]
    sums_ref[...] = jnp.zeros(sums_ref.shape, F32)
    for i in range(count):
        row = jnp.clip(ints_ref[2 + i], 0, rows - 1)
        column = jnp.clip(ints_ref[2 + count + i] - ints_ref[0] * rows + HALO_BLOCKS, 0, states_ref.shape[0] - 1)
        tile = states_ref[column]
        state = jnp.concatenate([tile[2 * piece : 2 * piece + 2, :] for piece in range(pieces)], axis=1)
        lead = state.astype(jnp.bfloat16).astype(F32)
        state = jnp.concatenate([lead, state - lead, jnp.zeros((12, block_len), F32)], axis=0).astype(jnp.bfloat16)
        block = blocks(i)
        lead = block.astype(jnp.bfloat16)
        rest = (block - lead.astype(F32)).astype(jnp.bfloat16)
        product = lax.dot_general(state, lead, NT, preferred_element_type=F32)
        product = product + lax.dot_general(state, rest, NT, preferred_element_type=F32)
        sums_ref[row] = sums_ref[row] + product[:8]


def fold_sums(sums_ref, out_ref):
    rows, pieces = sums_ref.shape[0], sums_ref.shape[2] // LANES
    shape = (8, LANES)
    for row in range(rows):
        total = sums_ref[row]
        total = total + pltpu.roll(total, 6, 0)
        picked = jnp.zeros(shape, F32)
        for piece in range(pieces):
            values = total[:, LANES * piece : LANES * (piece + 1)]
            values = pltpu.roll(values, 2 * piece, 0) if piece else values
            picked = jnp.where(row_index(shape) // 2 == piece, values, picked)
        out_ref[8 * row : 8 * row + 8, :] = out_ref[8 * row : 8 * row + 8, :] + picked


def fetched(blocks_hbm, first, held_ref, sems):
    copies = [pltpu.make_async_copy(blocks_hbm.at[first + i], held_ref.at[i], sems.at[i]) for i in range(held_ref.shape[0])]
    for copy in copies:
        copy.start()

    def block(i):
        copies[i - first].wait()
        return held_ref[i - first]

    return block


def dipole_kernel(
    ints_ref, blocks_hbm, mine_ref, pair_ref, next_ref, out_ref, left_ref, right_ref, states_ref, sums_ref, held_ref, sems
):
    sort_sides(ints_ref[0], pair_ref, next_ref, left_ref, right_ref)
    block = fetched(blocks_hbm, 0, held_ref, sems)
    sum_blocks(ints_ref, held_ref.shape[0], block, mine_ref, left_ref, right_ref, states_ref, sums_ref)
    out_ref[...] = jnp.zeros(out_ref.shape, F32)
    fold_sums(sums_ref, out_ref)


def pack_kernel(
    idx_ref, dipole_ref, surf_ref, cols_ref, edge_ref, w_ref, first_ref, pair_ref, next_ref,
    message_hbm, side_ref, left_ref, right_ref, total_ref, packed_ref, message_ref, sems,
):
    sort_sides(idx_ref[0], pair_ref, next_ref, left_ref, right_ref)
    reg = idx_ref[0]
    chan = surf_ref.shape[0]
    padded = cols_ref.shape[0]
    tiles = surf_ref.shape[1] // LANES
    windows = message_hbm.shape[0]
    regs = first_ref.shape[0]
    sym = wide(cols_ref[:chan, 0:1])
    received = first_ref[0]
    lane2 = lane_index((2, LANES))
    low = jnp.where(lane2 < WINDOW, received, 0.0)
    cell0 = jnp.where(lane2 < WINDOW, pltpu.roll(jnp.concatenate([received] * 4, axis=0), WINDOW, 1)[0:2], 0.0)
    cell1 = jnp.where(reg == 0, edge_ref[4 * windows : 4 * windows + 2, :], low)
    whole = jnp.zeros((2, LANES), F32)
    for source in range(regs):
        whole = whole + first_ref[source]
    whole = jnp.where((lane2 < WINDOW) & (reg == 0), whole, 0.0)
    beside = left_ref[HALO_ROWS : HALO_ROWS + 2, :] + right_ref[HALO_ROWS : HALO_ROWS + 2, :]
    side = square(
        jnp.concatenate(
            [
                cell0, cell1, beside, whole,
                left_ref[HALO_ROWS + 2 : HALO_ROWS + 4, :], right_ref[HALO_ROWS + 2 : HALO_ROWS + 4, :],
                left_ref[HALO_ROWS + 4 : HALO_ROWS + 6, :], right_ref[HALO_ROWS + 4 : HALO_ROWS + 6, :],
            ],
            axis=0,
        )
    )[:chan]
    symmetry, energy = cols_ref[:chan, 0:1], cols_ref[:chan, 1:2]
    radius = BOUNDARY_RADIUS + GRID_STEP
    potential = symmetry * (symmetry + 1.0) / (2.0 * radius * radius) + energy
    slope, start = [], []
    for part in range(2):
        here, beyond = side[:, part : part + 1], side[:, 2 + part : 3 + part]
        boundary = cols_ref[:chan, 2 + part : 3 + part] + side[:, 4 + part : 5 + part]
        slope.append(here - boundary)
        start.append(-2.0 * (beyond - 2.0 * here + boundary) + potential * here)
    lane = lane_index((chan, LANES))
    out = jnp.where((lane >= 6) & (lane < 16), side, 0.0)
    for part in range(2):
        out = jnp.where(lane == part, wide(start[part]), out)
    out = jnp.where(lane == 2, sym, out)
    out = jnp.where(lane == 3, wide(energy), out)
    side_ref[...] = jnp.concatenate([out, jnp.zeros((padded - chan, LANES), F32)], axis=0)
    level = halved(edge_ref[4 * windows + 5 : 4 * windows + 6, :])
    ends = halved(whole)
    tail = [cell0, edge_ref[4 * windows + 4 : 4 * windows + 5, :], level[0], ends[0], level[1], ends[1], jnp.zeros((3, LANES), F32)]
    gap = jnp.zeros((WINDOW - chan, LANES), F32)
    half = lane < WINDOW
    for window in range(windows):
        one, two = (cells_of(w_ref, part, window // 2, chan) for part in range(2))
        if window % 2 == 0:
            cells = jnp.where(half, one, pltpu.roll(two, WINDOW, 1))
        else:
            cells = jnp.where(half, pltpu.roll(one, WINDOW, 1), two)
        edges = edge_ref[4 * window : 4 * window + 4, :]
        if window == 0:
            edges = jnp.concatenate([left_ref[HALO_ROWS + 3 : HALO_ROWS + 4, :], left_ref[HALO_ROWS + 5 : HALO_ROWS + 6, :], edges[2:4]], axis=0)
        if window == windows - 1:
            edges = jnp.concatenate([edges[0:2], right_ref[HALO_ROWS + 2 : HALO_ROWS + 3, :], right_ref[HALO_ROWS + 4 : HALO_ROWS + 5, :]], axis=0)
        message_ref[window] = jnp.concatenate([cells, gap, edges] + tail, axis=0).astype(jnp.bfloat16)
    lines = packed_ref.shape[0]
    outer_copy = pltpu.make_async_copy(message_ref, message_hbm.at[:, lines:], sems.at[windows])
    outer_copy.start()
    total_ref[...] = dipole_ref[...]
    surface_rows(slope, surf_ref, sym, reg * tiles, tiles, total_ref)
    packed_ref[...] = jnp.concatenate(halved(total_ref[...]), axis=0).astype(jnp.bfloat16)
    copies = [pltpu.make_async_copy(packed_ref, message_hbm.at[window, :lines], sems.at[window]) for window in range(windows)]
    for copy in copies:
        copy.start()
    for copy in copies + [outer_copy]:
        copy.wait()


def update_kernel(
    idx_ref, received_ref, u_ref, energy_ref, surf_ref, cols_ref, out_ref, pair_ref, next_ref, left_ref, right_ref
):
    reg = idx_ref[0]
    lines = u_ref.shape[0]
    tiles = lines // 2
    chan = surf_ref.shape[0]
    image = energy_ref[...] * u_ref[...]
    for source in range(received_ref.shape[0]):
        values = received_ref[source, : 2 * lines, :].astype(F32)
        image = image + (values[:lines] + values[lines:])
    out_ref[...] = FIRST * turn_rows(image)
    sym = wide(cols_ref[:chan, 0:1])
    partial = boundary_sum(
        lambda tile, part: out_ref[2 * tile + part : 2 * tile + part + 1, :], surf_ref, sym, reg * tiles, tiles
    )
    lane = lane_index((chan, LANES))
    cols = jnp.where(lane == 0, wide(partial[0]), 0.0)
    cols = jnp.where(lane == 1, wide(partial[1]), cols)
    rows = jnp.concatenate([cols, jnp.zeros((LANES - chan, LANES), F32)], axis=0).T[0:8, :]
    left_ref[:HALO_ROWS, :] = out_ref[:HALO_ROWS, :]
    left_ref[HALO_ROWS:, :] = rows
    right_ref[:HALO_ROWS, :] = out_ref[lines - HALO_ROWS :, :]
    right_ref[HALO_ROWS:, :] = rows
    sort_sides(reg, left_ref, right_ref, pair_ref, next_ref)


def stencil(cells, lows, highs, potential, seams):
    count = cells.shape[1]
    lane = lane_index(cells.shape)
    below, above = pltpu.roll(cells, 1, 1), pltpu.roll(cells, count - 1, 1)
    for (first, last), low, high in zip(seams, lows, highs):
        below = jnp.where(lane == first, low, below)
        above = jnp.where(lane == last, high, above)
    return -2.0 * (above - 2.0 * cells + below) + potential * cells


def mats_of(mats_hbm, mats_ref, sems):
    rows = mats_ref.shape[0] // NLAM
    spans = [pl.ds(level * rows, rows) for level in range(NLAM)]
    copies = [pltpu.make_async_copy(mats_hbm.at[span], mats_ref.at[span], sems.at[i]) for i, span in enumerate(spans)]
    for copy in copies:
        copy.start()
    waiting = set(range(NLAM))

    def mats(level):
        if level in waiting:
            waiting.discard(level)
            copies[level].wait()
        return mats_ref[spans[level], :]

    return mats


def outer_kernel(count, idx_ref, received_ref, mats_hbm, blocks_hbm, cross_ref, start_ref, near_ref, edge_ref, mats_ref, sems, sem):
    copy = pltpu.make_async_copy(blocks_hbm.at[: near_ref.shape[0]], near_ref, sem)
    copy.start()
    mats = mats_of(mats_hbm, mats_ref, sems)
    reg, ch = idx_ref[0], idx_ref[1]
    groups, padded = cross_ref.shape[0], cross_ref.shape[1]
    lines = received_ref.shape[1] - WINDOW - 16
    rows = groups * padded
    cells = received_ref[:, lines : lines + WINDOW, :].astype(F32)[:, :padded].reshape(rows, LANES)
    flipped = received_ref[:, lines + WINDOW :, :].astype(F32).reshape(groups * 16, LANES).T
    extra = jnp.concatenate(
        [pltpu.roll(flipped[:padded], (LANES - 16 * group) % LANES, 1) for group in range(groups)], axis=0
    )
    first_point = reg * count + ch * WINDOW
    lane = lane_index((1, LANES))
    point = (first_point + lane % WINDOW + 1).astype(F32)
    radius = BOUNDARY_RADIUS + GRID_STEP * point
    extra_point = jnp.where(lane < 2, first_point, jnp.where(lane < 4, first_point + WINDOW + 1, 1)).astype(F32)
    extra_ratio = BOUNDARY_RADIUS / (BOUNDARY_RADIUS + GRID_STEP * extra_point)
    ratio = BOUNDARY_RADIUS / radius

    def mix(states, scale):
        states = states.astype(jnp.bfloat16)
        mixed, power = 0.0, 1.0
        for level in range(NLAM):
            mixed = mixed + power * jnp.dot(mats(level), states, preferred_element_type=F32)
            power = power * scale
        return mixed.astype(jnp.bfloat16).astype(F32)

    symmetry, energy = extra[:, 6:7], extra[:, 7:8] + extra[:, 10:11]
    potential = symmetry * (symmetry + 1.0) / (2.0 * radius * radius) + energy
    mixed = mix(jnp.concatenate([cells, extra], axis=1), jnp.concatenate([ratio, extra_ratio], axis=1))
    main, beside = mixed[:, :LANES], mixed[:, LANES:]
    edge_ref[...] = beside
    start_ref[...] = edge_ref[pl.ds(pl.multiple_of(ch * padded, 8), padded), :]
    inner_end = (reg == 0) & (ch == 0)
    seams = ((0, WINDOW - 1), (WINDOW, 2 * WINDOW - 1))
    ends = [extra[:, 8 + part : 9 + part] + extra[:, 11 + part : 12 + part] for part in range(2)]
    lows = [jnp.where(inner_end, ends[part], extra[:, part : part + 1]) for part in range(2)]
    highs = [extra[:, 2 + part : 3 + part] for part in range(2)]
    first = FIRST * turn_lanes(stencil(cells, lows, highs, potential, seams) + main)
    later = mix(first, ratio)
    cross = FIRST * turn_lanes(main)
    mixed_lows = [jnp.where(inner_end, 0.0, beside[:, part : part + 1]) for part in range(2)]
    mixed_highs = [beside[:, 2 + part : 3 + part] for part in range(2)]
    lows = [FIRST * mixed_lows[1], -FIRST * mixed_lows[0]]
    highs = [FIRST * mixed_highs[1], -FIRST * mixed_highs[0]]
    cross = cross + SECOND * turn_lanes(stencil(cross, lows, highs, potential, seams) + later)
    cross_ref[...] = cross.reshape(groups, padded, LANES)
    copy.wait()


def plain_part(regs, reg, w_ref, side_ref, plain_ref):
    chan, count = plain_ref.shape[1], plain_ref.shape[2]
    side = side_ref[...][:chan]
    symmetry, energy = side[:, 2:3], side[:, 3:4]
    lane = lane_index((1, count))
    radius = BOUNDARY_RADIUS + GRID_STEP * (reg * count + lane + 1).astype(F32)
    potential = symmetry * (symmetry + 1.0) / (2.0 * radius * radius) + energy

    def potential_at(index):
        there = BOUNDARY_RADIUS + GRID_STEP * (reg * count + index + 1).astype(F32)
        return symmetry * (symmetry + 1.0) / (2.0 * there * there) + energy

    last = reg == regs - 1
    images, lows, highs = [], [], []
    values_of = [
        jnp.concatenate([cells_of(w_ref, part, piece, chan) for piece in range(count // LANES)], axis=1) for part in range(2)
    ]
    for part in range(2):
        values = values_of[part]
        at = 8 + 4 * part
        low2, low1, high1, high2 = (side[:, at + i : at + i + 1] for i in range(4))
        low = jnp.where(reg == 0, side[:, 6 + part : 7 + part], low1)
        images.append(stencil(values, [low], [high1], potential, ((0, count - 1),)))
        under = -2.0 * (values[:, 0:1] - 2.0 * low1 + low2) + potential_at(jnp.int32(-1)) * low1
        over = -2.0 * (high2 - 2.0 * high1 + values[:, count - 1 : count]) + potential_at(jnp.int32(count)) * high1
        lows.append(jnp.where(reg == 0, 0.0, under))
        highs.append(jnp.where(last, 0.0, over))
    turned = [FIRST * images[1], -FIRST * images[0]]
    lows = [FIRST * lows[1], -FIRST * lows[0]]
    highs = [FIRST * highs[1], -FIRST * highs[0]]
    again = [stencil(turned[p], [lows[p]], [highs[p]], potential, ((0, count - 1),)) for p in range(2)]
    plain_ref[0] = values_of[0] + turned[0] + SECOND * again[1]
    plain_ref[1] = values_of[1] + turned[1] - SECOND * again[0]


def second_kernel(
    ints_ref, near_ref, blocks_hbm, mine_ref, pair_ref, next_ref, own_ref, surf_ref, side_ref, start_ref, cross_ref,
    message_hbm, left_ref, right_ref, states_ref, sums_ref, held_ref, sems, total_ref, out_sems,
):
    sort_sides(ints_ref[0], pair_ref, next_ref, left_ref, right_ref)
    near = near_ref.shape[0]
    rest = fetched(blocks_hbm, near, held_ref, sems)
    outer_copy = pltpu.make_async_copy(cross_ref, message_hbm.at[:, total_ref.shape[0] :], out_sems.at[message_hbm.shape[0]])
    outer_copy.start()
    block = lambda i: near_ref[i] if i < near else rest(i)
    sum_blocks(ints_ref, near + held_ref.shape[0], block, mine_ref, left_ref, right_ref, states_ref, sums_ref)
    total_ref[...] = jnp.zeros(total_ref.shape, F32)
    reg = ints_ref[0]
    chan = surf_ref.shape[0]
    tiles = surf_ref.shape[1] // LANES
    ends = own_ref[HALO_ROWS:, :] + left_ref[HALO_ROWS:, :] + right_ref[HALO_ROWS:, :]
    boundary = square(ends)[:chan]
    mixed = start_ref[:chan, :]
    side = side_ref[:chan, :]
    image = [side[:, part : part + 1] + mixed[:, 4 + part : 5 + part] for part in range(2)]
    slope = [FIRST * image[1] - boundary[:, 0:1], -FIRST * image[0] - boundary[:, 1:2]]
    surface_rows(slope, surf_ref, wide(side[:, 2:3]), reg * tiles, tiles, total_ref)
    fold_sums(sums_ref, total_ref)
    lines = total_ref.shape[0]
    groups = message_hbm.shape[0]
    copies = [pltpu.make_async_copy(total_ref, message_hbm.at[group, :lines], out_sems.at[group]) for group in range(groups)]
    for copy in copies:
        copy.start()
    for copy in copies + [outer_copy]:
        copy.wait()


def finish_kernel(idx_ref, received_ref, u_ref, first_ref, energy_ref, plain_ref, ends_ref, inner_ref, outer_ref, total_ref):
    reg = idx_ref[0]
    lines = u_ref.shape[0]
    chan = plain_ref.shape[1]
    image = energy_ref[...] * first_ref[...]
    sources = received_ref.shape[0]
    for source in range(sources):
        image = image + received_ref[source, :lines, :]
    total = u_ref[...] + first_ref[...] + SECOND * turn_rows(image)
    total_ref[...] = total
    for tile in range(lines // 2):
        inner_ref[:, LANES * tile : LANES * (tile + 1)] = total_ref[2 * tile : 2 * tile + 2, :]
    columns = square(ends_ref[...])[:chan]
    lane = lane_index((chan, LANES))
    half = lane < WINDOW
    for piece in range(sources // 2):
        even = received_ref[2 * piece, lines : lines + chan, :]
        odd = received_ref[2 * piece + 1, lines : lines + chan, :]
        one = jnp.where(half, even, pltpu.roll(odd, WINDOW, 1))
        two = jnp.where(half, pltpu.roll(even, WINDOW, 1), odd)
        at = slice(LANES * piece, LANES * (piece + 1))
        one = plain_ref[0, :, at] + one
        two = plain_ref[1, :, at] + two
        if piece == 0:
            here = (lane == 0) & (reg == 0)
            one = one + jnp.where(here, -2.0 * SECOND * columns[:, 1:2], 0.0)
            two = two + jnp.where(here, 2.0 * SECOND * columns[:, 0:1], 0.0)
        for part, cells in enumerate((one, two)):
            outer_ref[pl.ds(2 * piece + part, chan, stride=sources), :] = cells


def aside_kernel(regs, idx_ref, table_ref, w_ref, side_ref, mats_ref, plain_ref):
    plain_part(regs, idx_ref[0], w_ref, side_ref, plain_ref)
    build_mats(table_ref, mats_ref)


def build_mats(table_ref, mats_ref):
    rows = mats_ref.shape[0] // NLAM
    span = table_ref.shape[1]
    entries = table_ref.shape[0] // 4
    for first in range(0, rows, LANES):
        count = min(LANES, rows - first)
        columns = square(table_ref[:, first : first + LANES])[:count]
        here = lane_index((count, span)).astype(F32)
        sums = [jnp.zeros((count, span), F32) for _ in range(NLAM)]
        for entry in range(entries):
            hit = columns[:, entry : entry + 1] == here
            order = columns[:, entries + entry : entries + entry + 1]
            weight = columns[:, 2 * entries + entry : 2 * entries + entry + 1]
            for level in range(NLAM):
                picked = jnp.where(order == level, weight, 0.0)
                sums[level] = sums[level] + jnp.where(hit, picked, 0.0)
        for level in range(NLAM):
            at = level * rows + first
            mats_ref[at : at + count, :] = sums[level][:, :rows].astype(jnp.bfloat16)


def coupling_table(source, order_list, weight, groups, chan, padded):
    place = (source // chan) * padded + source % chan
    rows = jnp.concatenate([place.T.astype(F32), order_list.T.astype(F32), weight.T, jnp.zeros_like(weight.T)], axis=0)
    rows = rows.reshape(rows.shape[0], groups, chan)
    rows = jnp.pad(rows, ((0, 0), (0, 0), (0, padded - chan))).reshape(rows.shape[0], groups * padded)
    return jnp.pad(rows, ((0, 0), (0, -rows.shape[1] % LANES)))


def shape_of(*shape):
    return jax.ShapeDtypeStruct(shape, F32)


def local(
    inner_state, energy, blocks, pattern, surface, channel_symmetry, outer_state, channel_energy,
    couple_source, couple_order, couple_weight, *, regs, groups,
):
    tile_len = inner_state.shape[1]
    lines = 2 * tile_len // LANES
    block_len = blocks.shape[1]
    block_rows = tile_len // block_len
    chan = outer_state.shape[1]
    count = outer_state.shape[2]
    padded = -(-chan // 8) * 8
    idx = jnp.stack([lax.axis_index("reg"), lax.axis_index("ch")]).astype(jnp.int32)
    smem = pl.BlockSpec(memory_space=pltpu.SMEM)
    vmem = pl.BlockSpec(memory_space=pltpu.VMEM)
    hbm = pl.BlockSpec(memory_space=pltpu.HBM)
    far = lambda array: pltpu.with_memory_space_constraint(array, pltpu.HBM)
    halo = HALO_ROWS + 8
    pieces = count // LANES
    cells = outer_state.reshape(2, chan, pieces, LANES).transpose(1, 2, 0, 3).reshape(2 * chan * pieces, LANES)
    near = blocks.shape[0] * 5 // 8

    both = [pltpu.VMEM((halo, LANES), F32)] * 2
    first_msg, pair, other, rows, cols, edges, energy_rows, ints = pl.pallas_call(
        start_kernel,
        out_shape=(
            shape_of(regs, 2, LANES), shape_of(halo, LANES), shape_of(halo, LANES), shape_of(lines, LANES),
            shape_of(padded, LANES), shape_of(4 * groups + 8, LANES), shape_of(lines, LANES),
            jax.ShapeDtypeStruct((2 + pattern.size,), jnp.int32),
        ),
        in_specs=[smem] + [hbm] * 7,
        out_specs=(vmem,) * 7 + (smem,),
        scratch_shapes=both
        + [
            pltpu.VMEM((2, count, LANES), F32), pltpu.VMEM((2, tile_len), F32), pltpu.VMEM((chan, tile_len), F32),
            pltpu.VMEM(cells.shape, F32), pltpu.VMEM((lines // 2, LANES), F32),
            pltpu.VMEM((1, chan), jnp.int32), pltpu.VMEM((1, chan), F32), pltpu.SMEM((2, blocks.shape[0]), jnp.int32),
            pltpu.SemaphoreType.DMA((6 + SURFACE_PARTS,)),
        ],
        compiler_params=params(8),
        name="start",
    )(idx, far(pattern.T), far(inner_state), far(surface), far(cells), far(energy.reshape(lines // 2, LANES)),
      far(channel_symmetry.reshape(1, chan)), far(channel_energy.reshape(1, chan)))

    firsts = lax.all_to_all(first_msg, "reg", 0, 0)
    on_chip = [(i, i ^ 1) for i in range(regs)]
    off_chip = [move for i in range(1, regs - 1, 2) for move in ((i, i + 1), (i + 1, i))]
    from_pair = lax.ppermute(pair, "reg", on_chip)
    from_other = lax.ppermute(other, "reg", off_chip)
    block_scratch = [
        pltpu.VMEM((2 * HALO_BLOCKS + block_rows, 8, LANES), F32),
        pltpu.VMEM((block_rows, 8, block_len), F32),
    ]
    held = lambda blocks: [pltpu.VMEM((blocks, block_len, block_len), F32), pltpu.SemaphoreType.DMA((blocks,))]
    dipole = pl.pallas_call(
        dipole_kernel,
        out_shape=shape_of(lines, LANES),
        in_specs=[smem, hbm] + [vmem] * 3,
        out_specs=vmem,
        scratch_shapes=both + block_scratch + held(blocks.shape[0]),
        compiler_params=params(16),
        name="dipole",
    )(ints, far(blocks), rows, from_pair, from_other)

    message, side = pl.pallas_call(
        pack_kernel,
        out_shape=(
            jax.ShapeDtypeStruct((groups, 2 * lines + WINDOW + 16, LANES), jnp.bfloat16), shape_of(padded, LANES),
        ),
        in_specs=[smem] + [vmem] * 8,
        out_specs=(hbm, vmem),
        scratch_shapes=both
        + [
            pltpu.VMEM((lines, LANES), F32), pltpu.VMEM((2 * lines, LANES), jnp.bfloat16),
            pltpu.VMEM((groups, WINDOW + 16, LANES), jnp.bfloat16),
            pltpu.SemaphoreType.DMA((groups + 1,)),
        ],
        compiler_params=params(8),
        name="pack",
    )(ints, dipole, surface, cols, edges, cells, firsts, from_pair, from_other)
    received = lax.all_to_all(message, "ch", 0, 0)

    table = coupling_table(couple_source, couple_order, couple_weight, groups, chan, padded)
    mats_shape = (NLAM * groups * padded, groups * padded)
    mats, plain = pl.pallas_call(
        functools.partial(aside_kernel, regs),
        out_shape=(jax.ShapeDtypeStruct(mats_shape, jnp.bfloat16), shape_of(2, chan, count)),
        in_specs=[smem] + [vmem] * 3,
        out_specs=(vmem,) * 2,
        compiler_params=params(8),
        name="aside",
    )(ints, table, cells, side)
    received, mats = lax.optimization_barrier((received, mats))

    first, pair, other = pl.pallas_call(
        update_kernel,
        out_shape=(shape_of(lines, LANES), shape_of(halo, LANES), shape_of(halo, LANES)),
        in_specs=[smem] + [vmem] * 5,
        out_specs=(vmem,) * 3,
        scratch_shapes=both,
        compiler_params=params(8),
        name="update",
    )(ints, received, rows, energy_rows, surface, cols)
    from_pair = lax.ppermute(pair, "reg", on_chip)
    from_other = lax.ppermute(other, "reg", off_chip)

    moves = [[(2, 0), (4, 6), (8, 10), (12, 14)], [(6, 0)], [(10, 0)], [(14, 0)]]
    ends = pair[HALO_ROWS:] + from_pair[HALO_ROWS:]
    ends = ends + lax.ppermute(ends, "reg", moves[0])
    cross, start, near_blocks = pl.pallas_call(
        functools.partial(outer_kernel, count),
        out_shape=(shape_of(groups, padded, LANES), shape_of(padded, LANES), shape_of(near, block_len, block_len)),
        in_specs=[smem, vmem, hbm, hbm],
        out_specs=(vmem,) * 3,
        scratch_shapes=[
            pltpu.VMEM((groups * padded, LANES), F32), pltpu.VMEM(mats_shape, jnp.bfloat16),
            pltpu.SemaphoreType.DMA((NLAM,)), pltpu.SemaphoreType.DMA,
        ],
        compiler_params=params(16),
        name="outer",
    )(ints, received, far(mats), far(blocks))
    cross, ends = lax.optimization_barrier((cross, ends))
    message = pl.pallas_call(
        second_kernel,
        out_shape=shape_of(groups, lines + padded, LANES),
        in_specs=[smem, vmem, hbm] + [vmem] * 8,
        out_specs=hbm,
        scratch_shapes=both
        + block_scratch
        + held(blocks.shape[0] - near)
        + [pltpu.VMEM((lines, LANES), F32), pltpu.SemaphoreType.DMA((groups + 1,))],
        compiler_params=params(16),
        name="second",
    )(ints, near_blocks, far(blocks), first, from_pair, from_other, pair, surface, side, start, cross)
    message, ends = lax.optimization_barrier((message, ends))
    received = lax.all_to_all(message, "ch", 0, 0)
    ends = ends + sum(lax.ppermute(ends, "reg", move) for move in moves[1:])

    inner, outer = pl.pallas_call(
        finish_kernel,
        out_shape=(shape_of(2, tile_len), shape_of(*cells.shape)),
        in_specs=[smem] + [vmem] * 6,
        out_specs=(vmem,) * 2,
        scratch_shapes=[pltpu.VMEM((lines, LANES), F32)],
        compiler_params=params(8),
        name="finish",
    )(ints, received, rows, first, energy_rows, plain, ends)
    return inner, outer.reshape(chan, pieces, 2, LANES).transpose(2, 0, 1, 3).reshape(2, chan, count)


def solution(mesh):
    return jax.shard_map(
        functools.partial(local, regs=mesh.shape["reg"], groups=mesh.shape["ch"]),
        mesh=mesh,
        in_specs=(
            P(None, "reg"),
            P("reg"),
            P(("reg", "ch"), None, None),
            P(("reg", "ch"), None),
            P("ch", "reg"),
            P("ch"),
            P(None, "ch", "reg"),
            P("ch"),
            P(),
            P(),
            P(),
        ),
        out_specs=(P(None, "reg"), P(None, "ch", "reg")),
        check_vma=False,
    )
```

```python
import functools

import jax
import jax.numpy as jnp
from jax import lax
from jax.experimental import pallas as pl
from jax.experimental.pallas import tpu as pltpu
from jax.sharding import PartitionSpec as P

BLOCKS_PER_SYMM = 4
NLAM = 3
TIME_STEP = 0.05
GRID_STEP = 0.5
BOUNDARY_RADIUS = 20.0
FIRST = TIME_STEP
SECOND = TIME_STEP / 2
LANES = 128
HALO_BLOCKS = 7
HALO_ROWS = 8 * HALO_BLOCKS
WINDOW = 64
SURFACE_PARTS = 4
F32 = jnp.float32
NT = (((1,), (1,)), ((), ()))


def params(megabytes):
    return pltpu.CompilerParams(vmem_limit_bytes=megabytes * 2**20)


def lane_index(shape):
    return lax.broadcasted_iota(jnp.int32, shape, len(shape) - 1)


def row_index(shape):
    return lax.broadcasted_iota(jnp.int32, shape, len(shape) - 2)


def square(rows):
    count = rows.shape[0]
    if count < LANES:
        rows = jnp.concatenate([rows, jnp.zeros((LANES - count, LANES), F32)], axis=0)
    return rows.T


def wide(column):
    return jnp.broadcast_to(column, (column.shape[0], LANES))


def cells_of(w_ref, part, piece, chan):
    pieces = w_ref.shape[0] // (2 * chan)
    return w_ref[pl.ds(2 * piece + part, chan, stride=2 * pieces), :]


def boundary_sum(vec_rows, surf_ref, sym, first_tile, tiles, waits=()):
    chan = surf_ref.shape[0]
    sums = [jnp.zeros((chan, LANES), F32) for _ in range(2)]
    for tile in range(tiles):
        if waits and tile % (tiles // len(waits)) == 0:
            waits[tile // (tiles // len(waits))].wait()
        here = ((first_tile + tile) // 16).astype(F32)
        values = jnp.where(sym == here, surf_ref[:, LANES * tile : LANES * (tile + 1)], 0.0)
        for part in range(2):
            sums[part] = sums[part] + values * vec_rows(tile, part)
    return [jnp.sum(total, axis=1, keepdims=True) for total in sums]


def surface_rows(slope, surf_ref, sym, first_tile, tiles, out_ref):
    columns = [wide(column) for column in slope]
    for tile in range(tiles):
        here = ((first_tile + tile) // 16).astype(F32)
        values = jnp.where(sym == here, surf_ref[:, LANES * tile : LANES * (tile + 1)], 0.0)
        rows = [jnp.sum(values * columns[part], axis=0, keepdims=True) for part in range(2)]
        at = slice(2 * tile, 2 * tile + 2)
        out_ref[at, :] = out_ref[at, :] + jnp.concatenate(rows, axis=0)


def turn_rows(rows):
    count = rows.shape[0]
    even = row_index(rows.shape) % 2 == 0
    return jnp.where(even, pltpu.roll(rows, count - 1, 0), -pltpu.roll(rows, 1, 0))


def turn_lanes(cells):
    other = pltpu.roll(cells, WINDOW, 1)
    return jnp.where(lane_index(cells.shape) < WINDOW, other, -other)


def halved(values):
    lead = values.astype(jnp.bfloat16).astype(F32)
    return lead, values - lead


def sort_sides(reg, pair_ref, next_ref, left_ref, right_ref):
    odd = reg % 2 == 1
    left_ref[...] = jnp.where(odd, pair_ref[...], next_ref[...])
    right_ref[...] = jnp.where(odd, next_ref[...], pair_ref[...])


def start_kernel(
    idx_ref, pattern_hbm, u_hbm, surf_hbm, w_hbm, energy_hbm, sym_hbm, level_hbm,
    first_ref, pair_ref, next_ref, rows_ref, cols_ref, edge_ref, doubled_ref, ints_ref,
    left_ref, right_ref, wt_ref, u_ref, surf_ref, w_ref, energy_ref, sym_ref, level_ref, pattern_ref, sems,
):
    width = surf_ref.shape[1] // SURFACE_PARTS
    spans = [pl.ds(part * width, width) for part in range(SURFACE_PARTS)]
    copies = [
        pltpu.make_async_copy(source, target, sems.at[i])
        for i, (source, target) in enumerate(
            [
                (sym_hbm, sym_ref), (level_hbm, level_ref), (w_hbm, w_ref), (energy_hbm, energy_ref), (u_hbm, u_ref),
                (pattern_hbm, pattern_ref),
                *((surf_hbm.at[:, span], surf_ref.at[:, span]) for span in spans),
            ]
        )
    ]
    for copy in copies:
        copy.start()
    reg = idx_ref[0]
    tiles = u_ref.shape[1] // LANES
    chan = surf_ref.shape[0]
    copies[0].wait()
    copies[1].wait()
    head = jnp.zeros((1, LANES - chan), F32)
    sym_row = jnp.concatenate([sym_ref[...].astype(F32), head], axis=1)
    energy_row = jnp.concatenate([level_ref[...], head], axis=1)
    base = square(jnp.concatenate([sym_row, energy_row], axis=0))
    sym = wide(base[:chan, 0:1])
    copies[2].wait()
    for part in range(2):
        for piece in range(wt_ref.shape[1] // LANES):
            cells = cells_of(w_ref, part, piece, chan)
            cells = jnp.concatenate([cells, jnp.zeros((LANES - chan, LANES), F32)], axis=0)
            wt_ref[part, LANES * piece : LANES * (piece + 1), :] = cells.T
    copies[3].wait()
    for tile in range(tiles):
        doubled_ref[2 * tile : 2 * tile + 2, :] = jnp.broadcast_to(energy_ref[tile : tile + 1, :], (2, LANES))
    copies[4].wait()
    for tile in range(tiles):
        rows_ref[2 * tile : 2 * tile + 2, :] = u_ref[:, LANES * tile : LANES * (tile + 1)]
    partial = boundary_sum(
        lambda tile, part: u_ref[part : part + 1, LANES * tile : LANES * (tile + 1)],
        surf_ref, sym, reg * tiles, tiles, copies[6:],
    )
    lane = lane_index((chan, LANES))
    cols = jnp.where(lane == 0, sym, 0.0)
    cols = jnp.where(lane == 1, wide(base[:chan, 1:2]), cols)
    for part in range(2):
        cols = jnp.where(lane == 2 + part, wide(partial[part]), cols)
    cols = jnp.concatenate([cols, jnp.zeros((cols_ref.shape[0] - chan, LANES), F32)], axis=0)
    cols_ref[...] = cols
    back = jnp.concatenate([cols, jnp.zeros((LANES - cols.shape[0], LANES), F32)], axis=0).T
    partial_rows = back[2:4, :]
    count = wt_ref.shape[1]
    spot = lambda part, point: wt_ref[part, point : point + 1, :]
    zeros = jnp.zeros((2, LANES), F32)
    left_ref[:HALO_ROWS, :] = rows_ref[:HALO_ROWS, :]
    left_ref[HALO_ROWS:, :] = jnp.concatenate([partial_rows, spot(0, 0), spot(0, 1), spot(1, 0), spot(1, 1), zeros], axis=0)
    right_ref[:HALO_ROWS, :] = rows_ref[2 * tiles - HALO_ROWS :, :]
    right_ref[HALO_ROWS:, :] = jnp.concatenate(
        [partial_rows, spot(0, count - 2), spot(0, count - 1), spot(1, count - 2), spot(1, count - 1), zeros], axis=0
    )
    sort_sides(reg, left_ref, right_ref, pair_ref, next_ref)
    cell0 = jnp.concatenate([spot(0, 0), spot(1, 0)], axis=0)
    cell1 = jnp.concatenate([spot(0, 1), spot(1, 1)], axis=0)
    shifted = pltpu.roll(jnp.concatenate([cell0] * 4, axis=0), WINDOW, 1)[0:2]
    first_ref[0] = partial_rows + shifted
    others = first_ref.shape[0] - 1
    first_ref[1:] = jnp.broadcast_to((cell1 + shifted)[None], (others, 2, LANES))
    windows = count // WINDOW
    zero = jnp.zeros((1, LANES), F32)
    for window in range(windows):
        low, high = WINDOW * window - 1, WINDOW * (window + 1)
        edge_ref[4 * window : 4 * window + 4, :] = jnp.concatenate(
            [
                spot(0, low) if window else zero,
                spot(1, low) if window else zero,
                spot(0, high) if window < windows - 1 else zero,
                spot(1, high) if window < windows - 1 else zero,
            ],
            axis=0,
        )
    edge_ref[4 * windows : 4 * windows + 8, :] = jnp.concatenate([cell1, cell0, sym_row, energy_row, zeros], axis=0)
    copies[5].wait()
    ints_ref[0], ints_ref[1] = idx_ref[0], idx_ref[1]
    held = pattern_ref.shape[1]
    for i in range(held):
        ints_ref[2 + i] = pattern_ref[0, i]
        ints_ref[2 + held + i] = pattern_ref[1, i]


def sum_blocks(ints_ref, count, blocks, mine_ref, left_ref, right_ref, states_ref, sums_ref):
    block_len = sums_ref.shape[2]
    rows = mine_ref.shape[0] // 8
    pieces = block_len // LANES
    for column in range(HALO_BLOCKS):
        states_ref[column] = left_ref[8 * column : 8 * column + 8, :]
        states_ref[HALO_BLOCKS + rows + column] = right_ref[8 * column : 8 * column + 8, :]
    for column in range(rows):
        states_ref[HALO_BLOCKS + column] = mine_ref[8 * column : 8 * column + 8, :]
    sums_ref[...] = jnp.zeros(sums_ref.shape, F32)
    for i in range(count):
        row = jnp.clip(ints_ref[2 + i], 0, rows - 1)
        column = jnp.clip(ints_ref[2 + count + i] - ints_ref[0] * rows + HALO_BLOCKS, 0, states_ref.shape[0] - 1)
        tile = states_ref[column]
        state = jnp.concatenate([tile[2 * piece : 2 * piece + 2, :] for piece in range(pieces)], axis=1)
        lead = state.astype(jnp.bfloat16).astype(F32)
        state = jnp.concatenate([lead, state - lead, jnp.zeros((12, block_len), F32)], axis=0).astype(jnp.bfloat16)
        block = blocks(i)
        lead = block.astype(jnp.bfloat16)
        rest = (block - lead.astype(F32)).astype(jnp.bfloat16)
        product = lax.dot_general(state, lead, NT, preferred_element_type=F32)
        product = product + lax.dot_general(state, rest, NT, preferred_element_type=F32)
        sums_ref[row] = sums_ref[row] + product[:8]


def fold_sums(sums_ref, out_ref):
    rows, pieces = sums_ref.shape[0], sums_ref.shape[2] // LANES
    shape = (8, LANES)
    for row in range(rows):
        total = sums_ref[row]
        total = total + pltpu.roll(total, 6, 0)
        picked = jnp.zeros(shape, F32)
        for piece in range(pieces):
            values = total[:, LANES * piece : LANES * (piece + 1)]
            values = pltpu.roll(values, 2 * piece, 0) if piece else values
            picked = jnp.where(row_index(shape) // 2 == piece, values, picked)
        out_ref[8 * row : 8 * row + 8, :] = out_ref[8 * row : 8 * row + 8, :] + picked


def fetched(blocks_hbm, first, held_ref, sems):
    copies = [pltpu.make_async_copy(blocks_hbm.at[first + i], held_ref.at[i], sems.at[i]) for i in range(held_ref.shape[0])]
    for copy in copies:
        copy.start()

    def block(i):
        copies[i - first].wait()
        return held_ref[i - first]

    return block


def dipole_kernel(
    ints_ref, blocks_hbm, mine_ref, pair_ref, next_ref, out_ref, left_ref, right_ref, states_ref, sums_ref, held_ref, sems
):
    sort_sides(ints_ref[0], pair_ref, next_ref, left_ref, right_ref)
    block = fetched(blocks_hbm, 0, held_ref, sems)
    sum_blocks(ints_ref, held_ref.shape[0], block, mine_ref, left_ref, right_ref, states_ref, sums_ref)
    out_ref[...] = jnp.zeros(out_ref.shape, F32)
    fold_sums(sums_ref, out_ref)


def pack_kernel(
    idx_ref, dipole_ref, surf_ref, cols_ref, edge_ref, w_ref, first_ref, pair_ref, next_ref,
    message_hbm, side_ref, left_ref, right_ref, total_ref, packed_ref, message_ref, sems,
):
    sort_sides(idx_ref[0], pair_ref, next_ref, left_ref, right_ref)
    reg = idx_ref[0]
    chan = surf_ref.shape[0]
    padded = cols_ref.shape[0]
    tiles = surf_ref.shape[1] // LANES
    windows = message_hbm.shape[0]
    regs = first_ref.shape[0]
    sym = wide(cols_ref[:chan, 0:1])
    received = first_ref[0]
    lane2 = lane_index((2, LANES))
    low = jnp.where(lane2 < WINDOW, received, 0.0)
    cell0 = jnp.where(lane2 < WINDOW, pltpu.roll(jnp.concatenate([received] * 4, axis=0), WINDOW, 1)[0:2], 0.0)
    cell1 = jnp.where(reg == 0, edge_ref[4 * windows : 4 * windows + 2, :], low)
    whole = jnp.zeros((2, LANES), F32)
    for source in range(regs):
        whole = whole + first_ref[source]
    whole = jnp.where((lane2 < WINDOW) & (reg == 0), whole, 0.0)
    beside = left_ref[HALO_ROWS : HALO_ROWS + 2, :] + right_ref[HALO_ROWS : HALO_ROWS + 2, :]
    side = square(
        jnp.concatenate(
            [
                cell0, cell1, beside, whole,
                left_ref[HALO_ROWS + 2 : HALO_ROWS + 4, :], right_ref[HALO_ROWS + 2 : HALO_ROWS + 4, :],
                left_ref[HALO_ROWS + 4 : HALO_ROWS + 6, :], right_ref[HALO_ROWS + 4 : HALO_ROWS + 6, :],
            ],
            axis=0,
        )
    )[:chan]
    symmetry, energy = cols_ref[:chan, 0:1], cols_ref[:chan, 1:2]
    radius = BOUNDARY_RADIUS + GRID_STEP
    potential = symmetry * (symmetry + 1.0) / (2.0 * radius * radius) + energy
    slope, start = [], []
    for part in range(2):
        here, beyond = side[:, part : part + 1], side[:, 2 + part : 3 + part]
        boundary = cols_ref[:chan, 2 + part : 3 + part] + side[:, 4 + part : 5 + part]
        slope.append(here - boundary)
        start.append(-2.0 * (beyond - 2.0 * here + boundary) + potential * here)
    lane = lane_index((chan, LANES))
    out = jnp.where((lane >= 6) & (lane < 16), side, 0.0)
    for part in range(2):
        out = jnp.where(lane == part, wide(start[part]), out)
    out = jnp.where(lane == 2, sym, out)
    out = jnp.where(lane == 3, wide(energy), out)
    side_ref[...] = jnp.concatenate([out, jnp.zeros((padded - chan, LANES), F32)], axis=0)
    level = halved(edge_ref[4 * windows + 5 : 4 * windows + 6, :])
    ends = halved(whole)
    tail = [cell0, edge_ref[4 * windows + 4 : 4 * windows + 5, :], level[0], ends[0], level[1], ends[1], jnp.zeros((3, LANES), F32)]
    gap = jnp.zeros((WINDOW - chan, LANES), F32)
    half = lane < WINDOW
    for window in range(windows):
        one, two = (cells_of(w_ref, part, window // 2, chan) for part in range(2))
        if window % 2 == 0:
            cells = jnp.where(half, one, pltpu.roll(two, WINDOW, 1))
        else:
            cells = jnp.where(half, pltpu.roll(one, WINDOW, 1), two)
        edges = edge_ref[4 * window : 4 * window + 4, :]
        if window == 0:
            edges = jnp.concatenate([left_ref[HALO_ROWS + 3 : HALO_ROWS + 4, :], left_ref[HALO_ROWS + 5 : HALO_ROWS + 6, :], edges[2:4]], axis=0)
        if window == windows - 1:
            edges = jnp.concatenate([edges[0:2], right_ref[HALO_ROWS + 2 : HALO_ROWS + 3, :], right_ref[HALO_ROWS + 4 : HALO_ROWS + 5, :]], axis=0)
        message_ref[window] = jnp.concatenate([cells, gap, edges] + tail, axis=0).astype(jnp.bfloat16)
    lines = packed_ref.shape[0]
    outer_copy = pltpu.make_async_copy(message_ref, message_hbm.at[:, lines:], sems.at[windows])
    outer_copy.start()
    total_ref[...] = dipole_ref[...]
    surface_rows(slope, surf_ref, sym, reg * tiles, tiles, total_ref)
    packed_ref[...] = jnp.concatenate(halved(total_ref[...]), axis=0).astype(jnp.bfloat16)
    copies = [pltpu.make_async_copy(packed_ref, message_hbm.at[window, :lines], sems.at[window]) for window in range(windows)]
    for copy in copies:
        copy.start()
    for copy in copies + [outer_copy]:
        copy.wait()


def update_kernel(
    idx_ref, received_ref, u_ref, energy_ref, surf_ref, cols_ref, out_ref, pair_ref, next_ref, left_ref, right_ref
):
    reg = idx_ref[0]
    lines = u_ref.shape[0]
    tiles = lines // 2
    chan = surf_ref.shape[0]
    image = energy_ref[...] * u_ref[...]
    for source in range(received_ref.shape[0]):
        values = received_ref[source, : 2 * lines, :].astype(F32)
        image = image + (values[:lines] + values[lines:])
    out_ref[...] = FIRST * turn_rows(image)
    sym = wide(cols_ref[:chan, 0:1])
    partial = boundary_sum(
        lambda tile, part: out_ref[2 * tile + part : 2 * tile + part + 1, :], surf_ref, sym, reg * tiles, tiles
    )
    lane = lane_index((chan, LANES))
    cols = jnp.where(lane == 0, wide(partial[0]), 0.0)
    cols = jnp.where(lane == 1, wide(partial[1]), cols)
    rows = jnp.concatenate([cols, jnp.zeros((LANES - chan, LANES), F32)], axis=0).T[0:8, :]
    left_ref[:HALO_ROWS, :] = out_ref[:HALO_ROWS, :]
    left_ref[HALO_ROWS:, :] = rows
    right_ref[:HALO_ROWS, :] = out_ref[lines - HALO_ROWS :, :]
    right_ref[HALO_ROWS:, :] = rows
    sort_sides(reg, left_ref, right_ref, pair_ref, next_ref)


def stencil(cells, lows, highs, potential, seams):
    count = cells.shape[1]
    lane = lane_index(cells.shape)
    below, above = pltpu.roll(cells, 1, 1), pltpu.roll(cells, count - 1, 1)
    for (first, last), low, high in zip(seams, lows, highs):
        below = jnp.where(lane == first, low, below)
        above = jnp.where(lane == last, high, above)
    return -2.0 * (above - 2.0 * cells + below) + potential * cells


def mats_of(mats_hbm, mats_ref, sems):
    rows = mats_ref.shape[0] // NLAM
    spans = [pl.ds(level * rows, rows) for level in range(NLAM)]
    copies = [pltpu.make_async_copy(mats_hbm.at[span], mats_ref.at[span], sems.at[i]) for i, span in enumerate(spans)]
    for copy in copies:
        copy.start()
    waiting = set(range(NLAM))

    def mats(level):
        if level in waiting:
            waiting.discard(level)
            copies[level].wait()
        return mats_ref[spans[level], :]

    return mats


def outer_kernel(count, idx_ref, received_ref, mats_hbm, blocks_hbm, cross_ref, start_ref, near_ref, edge_ref, mats_ref, sems, sem):
    copy = pltpu.make_async_copy(blocks_hbm.at[: near_ref.shape[0]], near_ref, sem)
    copy.start()
    mats = mats_of(mats_hbm, mats_ref, sems)
    reg, ch = idx_ref[0], idx_ref[1]
    groups, padded = cross_ref.shape[0], cross_ref.shape[1]
    lines = received_ref.shape[1] - WINDOW - 16
    rows = groups * padded
    cells = received_ref[:, lines : lines + WINDOW, :].astype(F32)[:, :padded].reshape(rows, LANES)
    flipped = received_ref[:, lines + WINDOW :, :].astype(F32).reshape(groups * 16, LANES).T
    extra = jnp.concatenate(
        [pltpu.roll(flipped[:padded], (LANES - 16 * group) % LANES, 1) for group in range(groups)], axis=0
    )
    first_point = reg * count + ch * WINDOW
    lane = lane_index((1, LANES))
    point = (first_point + lane % WINDOW + 1).astype(F32)
    radius = BOUNDARY_RADIUS + GRID_STEP * point
    extra_point = jnp.where(lane < 2, first_point, jnp.where(lane < 4, first_point + WINDOW + 1, 1)).astype(F32)
    extra_ratio = BOUNDARY_RADIUS / (BOUNDARY_RADIUS + GRID_STEP * extra_point)
    ratio = BOUNDARY_RADIUS / radius

    def mix(states, scale):
        states = states.astype(jnp.bfloat16)
        mixed, power = 0.0, 1.0
        for level in range(NLAM):
            mixed = mixed + power * jnp.dot(mats(level), states, preferred_element_type=F32)
            power = power * scale
        return mixed.astype(jnp.bfloat16).astype(F32)

    symmetry, energy = extra[:, 6:7], extra[:, 7:8] + extra[:, 10:11]
    potential = symmetry * (symmetry + 1.0) / (2.0 * radius * radius) + energy
    mixed = mix(jnp.concatenate([cells, extra], axis=1), jnp.concatenate([ratio, extra_ratio], axis=1))
    main, beside = mixed[:, :LANES], mixed[:, LANES:]
    edge_ref[...] = beside
    start_ref[...] = edge_ref[pl.ds(pl.multiple_of(ch * padded, 8), padded), :]
    inner_end = (reg == 0) & (ch == 0)
    seams = ((0, WINDOW - 1), (WINDOW, 2 * WINDOW - 1))
    ends = [extra[:, 8 + part : 9 + part] + extra[:, 11 + part : 12 + part] for part in range(2)]
    lows = [jnp.where(inner_end, ends[part], extra[:, part : part + 1]) for part in range(2)]
    highs = [extra[:, 2 + part : 3 + part] for part in range(2)]
    first = FIRST * turn_lanes(stencil(cells, lows, highs, potential, seams) + main)
    later = mix(first, ratio)
    cross = FIRST * turn_lanes(main)
    mixed_lows = [jnp.where(inner_end, 0.0, beside[:, part : part + 1]) for part in range(2)]
    mixed_highs = [beside[:, 2 + part : 3 + part] for part in range(2)]
    lows = [FIRST * mixed_lows[1], -FIRST * mixed_lows[0]]
    highs = [FIRST * mixed_highs[1], -FIRST * mixed_highs[0]]
    cross = cross + SECOND * turn_lanes(stencil(cross, lows, highs, potential, seams) + later)
    cross_ref[...] = cross.reshape(groups, padded, LANES)
    copy.wait()


def plain_kernel(regs, idx_ref, w_ref, side_ref, plain_ref):
    reg = idx_ref[0]
    chan, count = plain_ref.shape[1], plain_ref.shape[2]
    side = side_ref[...][:chan]
    symmetry, energy = side[:, 2:3], side[:, 3:4]
    lane = lane_index((1, count))
    radius = BOUNDARY_RADIUS + GRID_STEP * (reg * count + lane + 1).astype(F32)
    potential = symmetry * (symmetry + 1.0) / (2.0 * radius * radius) + energy

    def potential_at(index):
        there = BOUNDARY_RADIUS + GRID_STEP * (reg * count + index + 1).astype(F32)
        return symmetry * (symmetry + 1.0) / (2.0 * there * there) + energy

    last = reg == regs - 1
    images, lows, highs = [], [], []
    values_of = [
        jnp.concatenate([cells_of(w_ref, part, piece, chan) for piece in range(count // LANES)], axis=1) for part in range(2)
    ]
    for part in range(2):
        values = values_of[part]
        at = 8 + 4 * part
        low2, low1, high1, high2 = (side[:, at + i : at + i + 1] for i in range(4))
        low = jnp.where(reg == 0, side[:, 6 + part : 7 + part], low1)
        images.append(stencil(values, [low], [high1], potential, ((0, count - 1),)))
        under = -2.0 * (values[:, 0:1] - 2.0 * low1 + low2) + potential_at(jnp.int32(-1)) * low1
        over = -2.0 * (high2 - 2.0 * high1 + values[:, count - 1 : count]) + potential_at(jnp.int32(count)) * high1
        lows.append(jnp.where(reg == 0, 0.0, under))
        highs.append(jnp.where(last, 0.0, over))
    turned = [FIRST * images[1], -FIRST * images[0]]
    lows = [FIRST * lows[1], -FIRST * lows[0]]
    highs = [FIRST * highs[1], -FIRST * highs[0]]
    again = [stencil(turned[p], [lows[p]], [highs[p]], potential, ((0, count - 1),)) for p in range(2)]
    plain_ref[0] = values_of[0] + turned[0] + SECOND * again[1]
    plain_ref[1] = values_of[1] + turned[1] - SECOND * again[0]


def second_kernel(
    ints_ref, near_ref, blocks_hbm, mine_ref, pair_ref, next_ref, own_ref, surf_ref, side_ref, start_ref, cross_ref,
    message_hbm, left_ref, right_ref, states_ref, sums_ref, held_ref, sems, total_ref, out_sems,
):
    sort_sides(ints_ref[0], pair_ref, next_ref, left_ref, right_ref)
    near = near_ref.shape[0]
    rest = fetched(blocks_hbm, near, held_ref, sems)
    outer_copy = pltpu.make_async_copy(cross_ref, message_hbm.at[:, total_ref.shape[0] :], out_sems.at[message_hbm.shape[0]])
    outer_copy.start()
    block = lambda i: near_ref[i] if i < near else rest(i)
    sum_blocks(ints_ref, near + held_ref.shape[0], block, mine_ref, left_ref, right_ref, states_ref, sums_ref)
    total_ref[...] = jnp.zeros(total_ref.shape, F32)
    reg = ints_ref[0]
    chan = surf_ref.shape[0]
    tiles = surf_ref.shape[1] // LANES
    ends = own_ref[HALO_ROWS:, :] + left_ref[HALO_ROWS:, :] + right_ref[HALO_ROWS:, :]
    boundary = square(ends)[:chan]
    mixed = start_ref[:chan, :]
    side = side_ref[:chan, :]
    image = [side[:, part : part + 1] + mixed[:, 4 + part : 5 + part] for part in range(2)]
    slope = [FIRST * image[1] - boundary[:, 0:1], -FIRST * image[0] - boundary[:, 1:2]]
    surface_rows(slope, surf_ref, wide(side[:, 2:3]), reg * tiles, tiles, total_ref)
    fold_sums(sums_ref, total_ref)
    lines = total_ref.shape[0]
    groups = message_hbm.shape[0]
    copies = [pltpu.make_async_copy(total_ref, message_hbm.at[group, :lines], out_sems.at[group]) for group in range(groups)]
    for copy in copies:
        copy.start()
    for copy in copies + [outer_copy]:
        copy.wait()


def finish_kernel(idx_ref, received_ref, u_ref, first_ref, energy_ref, plain_ref, ends_ref, inner_ref, outer_ref, total_ref):
    reg = idx_ref[0]
    lines = u_ref.shape[0]
    chan = plain_ref.shape[1]
    image = energy_ref[...] * first_ref[...]
    sources = received_ref.shape[0]
    for source in range(sources):
        image = image + received_ref[source, :lines, :]
    total = u_ref[...] + first_ref[...] + SECOND * turn_rows(image)
    total_ref[...] = total
    for tile in range(lines // 2):
        inner_ref[:, LANES * tile : LANES * (tile + 1)] = total_ref[2 * tile : 2 * tile + 2, :]
    columns = square(ends_ref[...])[:chan]
    lane = lane_index((chan, LANES))
    half = lane < WINDOW
    for piece in range(sources // 2):
        even = received_ref[2 * piece, lines : lines + chan, :]
        odd = received_ref[2 * piece + 1, lines : lines + chan, :]
        one = jnp.where(half, even, pltpu.roll(odd, WINDOW, 1))
        two = jnp.where(half, pltpu.roll(even, WINDOW, 1), odd)
        at = slice(LANES * piece, LANES * (piece + 1))
        one = plain_ref[0, :, at] + one
        two = plain_ref[1, :, at] + two
        if piece == 0:
            here = (lane == 0) & (reg == 0)
            one = one + jnp.where(here, -2.0 * SECOND * columns[:, 1:2], 0.0)
            two = two + jnp.where(here, 2.0 * SECOND * columns[:, 0:1], 0.0)
        for part, cells in enumerate((one, two)):
            outer_ref[pl.ds(2 * piece + part, chan, stride=sources), :] = cells


def mats_kernel(table_ref, after_ref, mats_hbm, mats_ref, sems):
    del after_ref
    rows = mats_ref.shape[0] // NLAM
    copies = []
    for first, last in build_mats(table_ref, mats_ref):
        for level in range(NLAM):
            span = pl.ds(level * rows + first, last - first)
            copies.append(pltpu.make_async_copy(mats_ref.at[span], mats_hbm.at[span], sems.at[len(copies)]))
            copies[-1].start()
    for copy in copies:
        copy.wait()


def build_mats(table_ref, mats_ref):
    rows = mats_ref.shape[0] // NLAM
    span = table_ref.shape[1]
    entries = table_ref.shape[0] // 4
    for first in range(0, rows, LANES):
        count = min(LANES, rows - first)
        columns = square(table_ref[:, first : first + LANES])[:count]
        here = lane_index((count, span)).astype(F32)
        sums = [jnp.zeros((count, span), F32) for _ in range(NLAM)]
        for entry in range(entries):
            hit = columns[:, entry : entry + 1] == here
            order = columns[:, entries + entry : entries + entry + 1]
            weight = columns[:, 2 * entries + entry : 2 * entries + entry + 1]
            for level in range(NLAM):
                picked = jnp.where(order == level, weight, 0.0)
                sums[level] = sums[level] + jnp.where(hit, picked, 0.0)
        for level in range(NLAM):
            at = level * rows + first
            mats_ref[at : at + count, :] = sums[level][:, :rows].astype(jnp.bfloat16)
        yield first, first + count


def coupling_table(source, order_list, weight, groups, chan, padded):
    place = (source // chan) * padded + source % chan
    rows = jnp.concatenate([place.T.astype(F32), order_list.T.astype(F32), weight.T, jnp.zeros_like(weight.T)], axis=0)
    rows = rows.reshape(rows.shape[0], groups, chan)
    rows = jnp.pad(rows, ((0, 0), (0, 0), (0, padded - chan))).reshape(rows.shape[0], groups * padded)
    return jnp.pad(rows, ((0, 0), (0, -rows.shape[1] % LANES)))


def shape_of(*shape):
    return jax.ShapeDtypeStruct(shape, F32)


def local(
    inner_state, energy, blocks, pattern, surface, channel_symmetry, outer_state, channel_energy,
    couple_source, couple_order, couple_weight, *, regs, groups,
):
    tile_len = inner_state.shape[1]
    lines = 2 * tile_len // LANES
    block_len = blocks.shape[1]
    block_rows = tile_len // block_len
    chan = outer_state.shape[1]
    count = outer_state.shape[2]
    padded = -(-chan // 8) * 8
    idx = jnp.stack([lax.axis_index("reg"), lax.axis_index("ch")]).astype(jnp.int32)
    smem = pl.BlockSpec(memory_space=pltpu.SMEM)
    vmem = pl.BlockSpec(memory_space=pltpu.VMEM)
    hbm = pl.BlockSpec(memory_space=pltpu.HBM)
    far = lambda array: pltpu.with_memory_space_constraint(array, pltpu.HBM)
    halo = HALO_ROWS + 8
    pieces = count // LANES
    cells = outer_state.reshape(2, chan, pieces, LANES).transpose(1, 2, 0, 3).reshape(2 * chan * pieces, LANES)
    near = blocks.shape[0] * 5 // 8

    both = [pltpu.VMEM((halo, LANES), F32)] * 2
    first_msg, pair, other, rows, cols, edges, energy_rows, ints = pl.pallas_call(
        start_kernel,
        out_shape=(
            shape_of(regs, 2, LANES), shape_of(halo, LANES), shape_of(halo, LANES), shape_of(lines, LANES),
            shape_of(padded, LANES), shape_of(4 * groups + 8, LANES), shape_of(lines, LANES),
            jax.ShapeDtypeStruct((2 + pattern.size,), jnp.int32),
        ),
        in_specs=[smem] + [hbm] * 7,
        out_specs=(vmem,) * 7 + (smem,),
        scratch_shapes=both
        + [
            pltpu.VMEM((2, count, LANES), F32), pltpu.VMEM((2, tile_len), F32), pltpu.VMEM((chan, tile_len), F32),
            pltpu.VMEM(cells.shape, F32), pltpu.VMEM((lines // 2, LANES), F32),
            pltpu.VMEM((1, chan), jnp.int32), pltpu.VMEM((1, chan), F32), pltpu.SMEM((2, blocks.shape[0]), jnp.int32),
            pltpu.SemaphoreType.DMA((6 + SURFACE_PARTS,)),
        ],
        compiler_params=params(8),
        name="start",
    )(idx, far(pattern.T), far(inner_state), far(surface), far(cells), far(energy.reshape(lines // 2, LANES)),
      far(channel_symmetry.reshape(1, chan)), far(channel_energy.reshape(1, chan)))

    firsts = lax.all_to_all(first_msg, "reg", 0, 0)
    on_chip = [(i, i ^ 1) for i in range(regs)]
    off_chip = [move for i in range(1, regs - 1, 2) for move in ((i, i + 1), (i + 1, i))]
    from_pair = lax.ppermute(pair, "reg", on_chip)
    from_other = lax.ppermute(other, "reg", off_chip)
    block_scratch = [
        pltpu.VMEM((2 * HALO_BLOCKS + block_rows, 8, LANES), F32),
        pltpu.VMEM((block_rows, 8, block_len), F32),
    ]
    held = lambda blocks: [pltpu.VMEM((blocks, block_len, block_len), F32), pltpu.SemaphoreType.DMA((blocks,))]
    dipole = pl.pallas_call(
        dipole_kernel,
        out_shape=shape_of(lines, LANES),
        in_specs=[smem, hbm] + [vmem] * 3,
        out_specs=vmem,
        scratch_shapes=both + block_scratch + held(blocks.shape[0]),
        compiler_params=params(16),
        name="dipole",
    )(ints, far(blocks), rows, from_pair, from_other)

    message, side = pl.pallas_call(
        pack_kernel,
        out_shape=(
            jax.ShapeDtypeStruct((groups, 2 * lines + WINDOW + 16, LANES), jnp.bfloat16), shape_of(padded, LANES),
        ),
        in_specs=[smem] + [vmem] * 8,
        out_specs=(hbm, vmem),
        scratch_shapes=both
        + [
            pltpu.VMEM((lines, LANES), F32), pltpu.VMEM((2 * lines, LANES), jnp.bfloat16),
            pltpu.VMEM((groups, WINDOW + 16, LANES), jnp.bfloat16),
            pltpu.SemaphoreType.DMA((groups + 1,)),
        ],
        compiler_params=params(8),
        name="pack",
    )(ints, dipole, surface, cols, edges, cells, firsts, from_pair, from_other)
    received = lax.all_to_all(message, "ch", 0, 0)

    table = coupling_table(couple_source, couple_order, couple_weight, groups, chan, padded)
    mats_shape = (NLAM * groups * padded, groups * padded)
    copies = NLAM * -(-mats_shape[1] // LANES)
    mats = pl.pallas_call(
        mats_kernel,
        out_shape=pltpu.HBM(mats_shape, jnp.bfloat16),
        in_specs=[vmem, hbm],
        out_specs=hbm,
        scratch_shapes=[pltpu.VMEM(mats_shape, jnp.bfloat16), pltpu.SemaphoreType.DMA((copies,))],
        compiler_params=params(8),
        name="mats",
    )(table, side)
    received, mats = lax.optimization_barrier((received, mats))

    first, pair, other = pl.pallas_call(
        update_kernel,
        out_shape=(shape_of(lines, LANES), shape_of(halo, LANES), shape_of(halo, LANES)),
        in_specs=[smem] + [vmem] * 5,
        out_specs=(vmem,) * 3,
        scratch_shapes=both,
        compiler_params=params(8),
        name="update",
    )(ints, received, rows, energy_rows, surface, cols)
    from_pair = lax.ppermute(pair, "reg", on_chip)
    from_other = lax.ppermute(other, "reg", off_chip)

    moves = [[(2, 0), (4, 6), (8, 10), (12, 14)], [(6, 0)], [(10, 0)], [(14, 0)]]
    ends = pair[HALO_ROWS:] + from_pair[HALO_ROWS:]
    ends = ends + lax.ppermute(ends, "reg", moves[0])
    cross, start, near_blocks = pl.pallas_call(
        functools.partial(outer_kernel, count),
        out_shape=(shape_of(groups, padded, LANES), shape_of(padded, LANES), shape_of(near, block_len, block_len)),
        in_specs=[smem, vmem, hbm, hbm],
        out_specs=(vmem,) * 3,
        scratch_shapes=[
            pltpu.VMEM((groups * padded, LANES), F32), pltpu.VMEM(mats_shape, jnp.bfloat16),
            pltpu.SemaphoreType.DMA((NLAM,)), pltpu.SemaphoreType.DMA,
        ],
        compiler_params=params(16),
        name="outer",
    )(ints, received, far(mats), far(blocks))
    cross, ends = lax.optimization_barrier((cross, ends))
    message = pl.pallas_call(
        second_kernel,
        out_shape=shape_of(groups, lines + padded, LANES),
        in_specs=[smem, vmem, hbm] + [vmem] * 8,
        out_specs=hbm,
        scratch_shapes=both
        + block_scratch
        + held(blocks.shape[0] - near)
        + [pltpu.VMEM((lines, LANES), F32), pltpu.SemaphoreType.DMA((groups + 1,))],
        compiler_params=params(16),
        name="second",
    )(ints, near_blocks, far(blocks), first, from_pair, from_other, pair, surface, side, start, cross)
    message, ends, side = lax.optimization_barrier((message, ends, side))
    received = lax.all_to_all(message, "ch", 0, 0)
    plain = pl.pallas_call(
        functools.partial(plain_kernel, regs),
        out_shape=shape_of(2, chan, count),
        in_specs=[smem] + [vmem] * 2,
        out_specs=vmem,
        compiler_params=params(8),
        name="plain",
    )(ints, cells, side)
    ends = ends + sum(lax.ppermute(ends, "reg", move) for move in moves[1:])

    inner, outer = pl.pallas_call(
        finish_kernel,
        out_shape=(shape_of(2, tile_len), shape_of(*cells.shape)),
        in_specs=[smem] + [vmem] * 6,
        out_specs=(vmem,) * 2,
        scratch_shapes=[pltpu.VMEM((lines, LANES), F32)],
        compiler_params=params(8),
        name="finish",
    )(ints, received, rows, first, energy_rows, plain, ends)
    return inner, outer.reshape(chan, pieces, 2, LANES).transpose(2, 0, 1, 3).reshape(2, chan, count)


def solution(mesh):
    return jax.shard_map(
        functools.partial(local, regs=mesh.shape["reg"], groups=mesh.shape["ch"]),
        mesh=mesh,
        in_specs=(
            P(None, "reg"),
            P("reg"),
            P(("reg", "ch"), None, None),
            P(("reg", "ch"), None),
            P("ch", "reg"),
            P("ch"),
            P(None, "ch", "reg"),
            P("ch"),
            P(),
            P(),
            P(),
        ),
        out_specs=(P(None, "reg"), P(None, "ch", "reg")),
        check_vma=False,
    )
```
